32 devices in a mesh: group: 2 (over y), gx: 4 (over z), gy: 4 (over x, core).
Axes of the slice: x: 2, y: 2, z: 4, core: 2. Of those that a mesh axis runs over, the one named last changes fastest.
Arguments:
- tokens: bfloat16 [512, 8192], P(('group', 'gx'), 'gy'), parts along dimension 0, may hold values from -6 to 6
- gate_weight: bfloat16 [8192, 26624], P('gy', 'gx'), may hold values from -0.0625 to 0.0625
- up_weight: bfloat16 [8192, 26624], P('gy', 'gx'), may hold values from -0.0625 to 0.0625
- down_weight: bfloat16 [26624, 8192], P('gx', 'gy'), may hold values from -0.0390625 to 0.0390625
- lengths: int32 [8], P('group'), parts along dimension 0, may hold values from 1 to 64, 192 in all
Outputs:
- scored: bfloat16 [512, 8192], P(('group', 'gx'), 'gy'), parts along dimension 0
The draws below stay inside these ranges and needn't reach their ends.
There are 2 independent parts, one for each index of `group`. The reference program is written for one: setup_inputs(seed, part) draws one part's arguments, and reference() takes and returns one part's arrays. A program takes and returns all parts, laid end to end along the dimension named above; an argument that names none is the same for every part. Nothing has to cross between parts.
Inputs may be any that keep to these rules, and one draw needn't show every extreme that they name: The live tokens of row group g are its first lengths[g] slots; the lengths of one part sum to exactly 192, and the longest is exactly 64.
All inputs are finite; a program needn't handle non-finite values.
Results may differ from the reference program's by a relative error of at most 0.019.
Values may be sent and summed in bfloat16 or wider, within the bound.
No kernel may reach another device: no remote copies, remote signals or barrier semaphores. Data moves between devices by JAX's collectives and lax.ppermute only.
A program may use at most 192 MiB of HBM per device.

```python
import math
import jax
import jax.numpy as jnp
import numpy as np
from jax import lax

D = 8192
FF = 26624
TOK_DEV = 64
TOKENS = 256
LIVE = 192
N_GX = 4
N_GY = 4


def block_scale(rng, dims, pieces, smallest, high):
    def one(dim, shards_of):
        heights = jax.random.uniform(jax.random.fold_in(jax.random.fold_in(rng, 6), dim), (shards_of,), jnp.float32, smallest / len(pieces), high / len(pieces))
        return jnp.repeat(jnp.exp(heights), dims[dim] // shards_of).reshape((-1,) + (1,) * (len(dims) - dim - 1))

    loudness = one(*pieces[0])
    for cut in pieces[1:]:
        loudness = loudness * one(*cut)
    return loudness


def profile(number_of, total, bound, lean):
    weights = [(1 << 20) // math.isqrt(rank ** lean) + 1 for rank in range(2, number_of + 1)]
    rest, given = total - bound - (number_of - 1), [1] * (number_of - 1)
    while rest > 0:
        free = [i for i in range(number_of - 1) if given[i] < bound]
        pool, budget = sum([weights[i] for i in free]), rest
        for i in free:
            more = min(bound - given[i], max(1, budget * weights[i] // pool), rest)
            given[i] = given[i] + more
            rest = rest - more
    return np.array([bound] + given)


def uneven_parts(key, count, total, reach, skew):
    if count == 2:
        one = jax.random.randint(key, (), max(1, total - reach), min(reach, total - 1) + 1)
        return jnp.stack([one, total - one])
    sizes = jnp.asarray(profile(count, total, reach, skew), jnp.int32)
    twos = (count - 1) // 2
    donor, receiver = sizes[1:1 + 2 * twos:2], sizes[2:2 + 2 * twos:2]
    margin = jnp.minimum(donor - 1, reach - receiver)
    shifted = jax.random.randint(jax.random.fold_in(key, 1), (twos,), 0, 1 << 20) % (margin + 1)
    sizes = sizes.at[1:1 + 2 * twos:2].set(donor - shifted).at[2:2 + 2 * twos:2].set(receiver + shifted)
    return sizes[jax.random.permutation(jax.random.fold_in(key, 2), count)]


def scatter_about(own_key, extent, deviation, reach, pieces=(), held_as=jnp.bfloat16):
    gain = block_scale(own_key, extent, pieces, -0.22, 0.18) if pieces else 1.0
    array = jax.random.normal(own_key, extent, jnp.float32) * deviation * gain
    return jnp.minimum(jnp.maximum(array, -reach), reach).astype(held_as)


def setup_inputs(seed: int = 0, part: int = 0) -> dict:
    splits = jax.random.split(jax.random.key(seed), 6)
    part_splits = jax.random.split(jax.random.fold_in(splits[5], part), 6)
    tokens = scatter_about(part_splits[0], (TOKENS, D), 1.0, 6.0, ((0, 4), (1, 4)))
    gate_weight = scatter_about(splits[1], (D, FF), D ** -0.5, 0.0625, ((0, 4), (1, 4)))
    up_weight = scatter_about(splits[2], (D, FF), D ** -0.5, 0.0625, ((0, 4), (1, 4)))
    down_weight = scatter_about(splits[3], (FF, D), FF ** -0.5, 0.0390625, ((0, 4), (1, 4)))
    lengths = uneven_parts(part_splits[4], N_GX, LIVE, TOK_DEV, 2).astype(jnp.int32)
    return {"tokens": tokens, "gate_weight": gate_weight, "up_weight": up_weight, "down_weight": down_weight, "lengths": lengths}


def rounded(values):
    low_values = values.astype(jnp.bfloat16)
    low_values = lax.optimization_barrier(low_values)
    return low_values.astype(jnp.float32)


def reference(tokens, gate_weight, up_weight, down_weight, lengths):
    block_width = D // N_GY

    def block_sum(totals, block_index):
        first_row = block_index * block_width
        features = lax.dynamic_slice_in_dim(tokens, first_row, block_width, 1)
        gate_rows = lax.dynamic_slice_in_dim(gate_weight, first_row, block_width, 0)
        up_rows = lax.dynamic_slice_in_dim(up_weight, first_row, block_width, 0)
        gate_part = rounded(jnp.dot(features, gate_rows, preferred_element_type=jnp.float32))
        up_part = rounded(jnp.dot(features, up_rows, preferred_element_type=jnp.float32))
        return (totals[0] + gate_part, totals[1] + up_part), None

    empty = jnp.zeros((TOKENS, FF), jnp.float32)
    sums, unused = lax.scan(block_sum, (empty, empty), jnp.arange(N_GY, dtype=jnp.int32))
    hidden = (jax.nn.silu(sums[0]) * sums[1]).astype(jnp.bfloat16)
    mixed_out = jnp.dot(hidden, down_weight, preferred_element_type=jnp.float32)
    live_mask = (jnp.arange(TOK_DEV, dtype=jnp.int32)[None, :] < lengths[:, None]).reshape(TOKENS)
    return jnp.where(live_mask[:, None], mixed_out, 0.0).astype(jnp.bfloat16)
```

```python
import functools

import jax
import jax.numpy as jnp
from jax import lax
from jax.experimental import pallas as pl
from jax.experimental.pallas import tpu as pltpu
from jax.sharding import PartitionSpec as P

MIB = 1 << 20
BF16, F32 = jnp.bfloat16, jnp.float32


def row_sources(lengths_ref, rows, n_gx, tok_dev):
    start = jnp.int32(0)
    slot = rows
    for g in range(n_gx):
        slot = jnp.where(rows >= start, rows - start + g * tok_dev, slot)
        start = start + lengths_ref[g]
    return slot


def local_rows(shape, dim, quarter, nx):
    gy = lax.axis_index("gy")
    x, core = gy // 2, gy % 2
    j = lax.broadcasted_iota(jnp.int32, shape, dim)
    rows = jnp.zeros(shape, jnp.int32)
    for kc in range(2):
        for kx in range(nx):
            first = (kc * nx + kx) * quarter
            owner = lax.rem(x + kx, nx) * 2 + (1 - core if kc else core)
            rows = jnp.where(j >= first, owner * quarter + j - first, rows)
    return rows


def compact_kernel(n_gx, nx, lengths_ref, *refs):
    blocks, out_ref = refs[:-1], refs[-1]
    live, tok_dev = out_ref.shape[0], blocks[0].shape[0]
    z = lax.axis_index("gx")
    slot = row_sources(lengths_ref, local_rows((live, tok_dev), 0, live // (2 * nx), nx), n_gx, tok_dev)
    column = lax.broadcasted_iota(jnp.int32, (live, tok_dev), 1)
    total = jnp.zeros(out_ref.shape, F32)
    for k in range(n_gx):
        pick = (slot == column + (z ^ k) * tok_dev).astype(F32).astype(BF16)
        total += jnp.dot(pick, blocks[k][...], preferred_element_type=F32)
    out_ref[...] = total.astype(BF16)


def compact(lengths, blocks, live, nx):
    n_gx = len(blocks)
    rows, width = blocks[0].shape
    tile = min(width, 512)
    return pl.pallas_call(
        functools.partial(compact_kernel, n_gx, nx),
        out_shape=jax.ShapeDtypeStruct((live, width), BF16),
        grid_spec=pltpu.PrefetchScalarGridSpec(
            num_scalar_prefetch=1,
            grid=(width // tile,),
            in_specs=[pl.BlockSpec((rows, tile), lambda j, s: (0, j))] * n_gx,
            out_specs=pl.BlockSpec((live, tile), lambda j, s: (0, j)),
        ),
        name="compact",
    )(lengths, *blocks)


def gate_up_kernel(tok_ref, gate_ref, up_ref, send_ref, keep_ref):
    half = keep_ref.shape[1]
    rows = tok_ref[...]
    for i, w_ref in enumerate((gate_ref, up_ref)):
        part = jnp.dot(rows, w_ref[...], preferred_element_type=F32)
        keep_ref[i] = part[:half]
        send_ref[i] = part[half:].astype(BF16)


def gate_up(tok, gate_weight, up_weight, start, width, tile):
    live, depth = tok.shape
    half = live // 2
    weight = pl.BlockSpec((depth, tile), lambda j: (0, start // tile + j))
    out = pl.BlockSpec((2, half, tile), lambda j: (0, 0, j))
    return pl.pallas_call(
        gate_up_kernel,
        out_shape=[jax.ShapeDtypeStruct((2, half, width), BF16), jax.ShapeDtypeStruct((2, half, width), F32)],
        grid=(width // tile,),
        in_specs=[pl.BlockSpec((live, depth), lambda j: (0, 0)), weight, weight],
        out_specs=[out, out],
        compiler_params=pltpu.CompilerParams(vmem_limit_bytes=32 * MIB),
        cost_estimate=pl.CostEstimate(
            flops=4 * live * depth * width, bytes_accessed=4 * depth * width, transcendentals=0
        ),
        name="gate_up",
    )(tok, gate_weight, up_weight)


def down_kernel(n_h, n_gx, nx, first, last, lengths_ref, *refs):
    h_refs, w_ref, refs = refs[:n_h], refs[n_h], refs[n_h + 1:]
    h = jnp.concatenate([r[...] for r in h_refs], axis=0)
    total = jnp.dot(h, w_ref[...], preferred_element_type=F32)
    if not first:
        total += refs[0][...]
        refs = refs[1:]
    if not last:
        refs[0][...] = total
        return
    live, tok_dev = total.shape[0], refs[0].shape[0]
    z = lax.axis_index("gx")
    slot = row_sources(lengths_ref, local_rows((tok_dev, live), 1, live // (2 * nx), nx), n_gx, tok_dev)
    row = lax.broadcasted_iota(jnp.int32, (tok_dev, live), 0)
    total = total.astype(BF16)
    for k in range(n_gx):
        pick = (slot == row + (z ^ k) * tok_dev).astype(F32).astype(BF16)
        refs[k][...] = jnp.dot(pick, total, preferred_element_type=F32).astype(BF16)


def down(lengths, hidden, down_weight, total, start, width, n_gx, nx, tok_dev, last):
    live = sum(h.shape[0] for h in hidden)
    out_width = down_weight.shape[1]
    tile = min(out_width, 512)
    rows = pl.BlockSpec((live, tile), lambda j, s: (0, j))
    operands = [*hidden, down_weight]
    in_specs = [pl.BlockSpec(h.shape, lambda j, s: (0, 0)) for h in hidden]
    in_specs.append(pl.BlockSpec((pl.Element(width), pl.Element(tile)), lambda j, s: (start, j * tile)))
    if total is not None:
        operands.append(total)
        in_specs.append(rows)
    if last:
        out_shape = [jax.ShapeDtypeStruct((tok_dev, out_width), BF16)] * n_gx
        out_specs = [pl.BlockSpec((tok_dev, tile), lambda j, s: (0, j))] * n_gx
    else:
        out_shape, out_specs = jax.ShapeDtypeStruct((live, out_width), F32), rows
    return pl.pallas_call(
        functools.partial(down_kernel, len(hidden), n_gx, nx, total is None, last),
        out_shape=out_shape,
        grid_spec=pltpu.PrefetchScalarGridSpec(
            num_scalar_prefetch=1, grid=(out_width // tile,), in_specs=in_specs, out_specs=out_specs
        ),
        compiler_params=pltpu.CompilerParams(vmem_limit_bytes=32 * MIB),
        cost_estimate=pl.CostEstimate(
            flops=2 * live * width * out_width, bytes_accessed=2 * width * out_width, transcendentals=0
        ),
        name="down",
    )(lengths, *operands)


def column_chunks(cols, tile):
    tiles = cols // tile
    shares = (5, 7, 8, 6)
    edges = [round(tiles * sum(shares[:i]) / sum(shares)) for i in range(len(shares) + 1)]
    return [(a * tile, (b - a) * tile) for a, b in zip(edges, edges[1:]) if b > a]


def local(n_gx, n_gy, tokens, gate_weight, up_weight, down_weight, lengths):
    nx = n_gy // 2
    tok_dev = tokens.shape[0]
    live = 3 * tok_dev * n_gx // 4
    quarter = live // n_gy
    cols = gate_weight.shape[1]
    tile = 256 if cols % 256 == 0 else 128
    chunks = column_chunks(cols, tile)

    def over_z(block, k):
        return lax.ppermute(block, "gx", [(z, z ^ k) for z in range(n_gx)])

    def over_core(block):
        return lax.ppermute(block, "gy", [(i, i ^ 1) for i in range(n_gy)])

    def over_x(block, k):
        return lax.ppermute(block, "gy", [(i, (i + 2 * k) % n_gy) for i in range(n_gy)])

    blocks = [tokens] + [over_z(tokens, k) for k in range(1, n_gx)]
    tok = compact(lengths, blocks, live, nx)

    total = None
    for i, (start, width) in enumerate(chunks):
        send, keep = gate_up(tok, gate_weight, up_weight, start, width, tile)
        sums = keep + over_core(send).astype(F32)
        mine = sums[:, :quarter]
        for k in range(1, nx):
            block = sums[:, k * quarter:(k + 1) * quarter].astype(BF16)
            mine = mine + over_x(block, k).astype(F32)
        own = (jax.nn.silu(mine[0]) * mine[1]).astype(BF16)
        hidden = [own] + [over_x(own, -k) for k in range(1, nx)]
        hidden += [over_core(h) for h in hidden]
        last = i == len(chunks) - 1
        total = down(lengths, hidden, down_weight, total, start, width, n_gx, nx, tok_dev, last)

    out = total[0].astype(F32)
    for k in range(1, n_gx):
        out = out + over_z(total[k], k).astype(F32)
    return out.astype(BF16)


def solution(mesh):
    placed = (P(("group", "gx"), "gy"), P("gy", "gx"), P("gy", "gx"), P("gx", "gy"), P("group"))
    return jax.shard_map(
        functools.partial(local, mesh.shape["gx"], mesh.shape["gy"]),
        mesh=mesh, in_specs=placed, out_specs=P(("group", "gx"), "gy"), check_vma=False,
    )
```

```python
import functools

import jax
import jax.numpy as jnp
from jax import lax
from jax.experimental import pallas as pl
from jax.experimental.pallas import tpu as pltpu
from jax.sharding import PartitionSpec as P

MIB = 1 << 20
BF16, F32 = jnp.bfloat16, jnp.float32


def row_sources(lengths_ref, rows, n_gx, tok_dev):
    start = jnp.int32(0)
    slot = rows
    for g in range(n_gx):
        slot = jnp.where(rows >= start, rows - start + g * tok_dev, slot)
        start = start + lengths_ref[g]
    return slot


def local_rows(shape, dim, quarter, nx):
    gy = lax.axis_index("gy")
    x, core = gy // 2, gy % 2
    j = lax.broadcasted_iota(jnp.int32, shape, dim)
    rows = jnp.zeros(shape, jnp.int32)
    for kc in range(2):
        for kx in range(nx):
            first = (kc * nx + kx) * quarter
            owner = lax.rem(x + kx, nx) * 2 + (1 - core if kc else core)
            rows = jnp.where(j >= first, owner * quarter + j - first, rows)
    return rows


def picks_kernel(n_gx, nx, tok_dev, lengths_ref, in_ref, out_ref):
    z = lax.axis_index("gx")
    live, slots = in_ref.shape
    quarter = live // (2 * nx)

    def slot_of(column):
        return (z ^ (column // tok_dev)) * tok_dev + column % tok_dev

    shape = (live, slots)
    source = row_sources(lengths_ref, local_rows(shape, 0, quarter, nx), n_gx, tok_dev)
    in_ref[...] = (source == slot_of(lax.broadcasted_iota(jnp.int32, shape, 1))).astype(F32).astype(BF16)
    shape = (slots, live)
    source = row_sources(lengths_ref, local_rows(shape, 1, quarter, nx), n_gx, tok_dev)
    out_ref[...] = (source == slot_of(lax.broadcasted_iota(jnp.int32, shape, 0))).astype(F32).astype(BF16)


def picks(lengths, n_gx, nx, tok_dev, live):
    slots = n_gx * tok_dev
    return pl.pallas_call(
        functools.partial(picks_kernel, n_gx, nx, tok_dev),
        out_shape=[jax.ShapeDtypeStruct((live, slots), BF16), jax.ShapeDtypeStruct((slots, live), BF16)],
        in_specs=[pl.BlockSpec(memory_space=pltpu.SMEM)],
        cost_estimate=pl.CostEstimate(flops=0, bytes_accessed=4 * live * slots, transcendentals=0),
        name="picks",
    )(lengths)


def compact_kernel(groups, pick_ref, *refs):
    refs, out_ref = list(refs[:-1]), refs[-1]
    blocks = []
    for n in groups:
        block = refs.pop(0)[...]
        for _ in range(n - 1):
            block = block + refs.pop(0)[...]
        blocks.append(block)
    rows = jnp.concatenate(blocks, axis=0)
    out_ref[...] = jnp.dot(pick_ref[...], rows, preferred_element_type=F32).astype(BF16)


def compact(pick, blocks):
    flat = [b for group in blocks for b in group]
    return pl.pallas_call(
        functools.partial(compact_kernel, [len(group) for group in blocks]),
        out_shape=jax.ShapeDtypeStruct((pick.shape[0], flat[0].shape[1]), BF16),
        cost_estimate=pl.CostEstimate(
            flops=2 * pick.size * flat[0].shape[1], bytes_accessed=2 * pick.size, transcendentals=0
        ),
        name="compact",
    )(pick, *flat)


def gate_up_kernel(tok_ref, gate_ref, up_ref, *refs):
    send_ref, keep_ref = refs[-2:]
    half = keep_ref.shape[1]
    rows = tok_ref[...]
    for i, w_ref in enumerate((gate_ref, up_ref)):
        part = jnp.dot(rows, w_ref[...], preferred_element_type=F32)
        keep_ref[i] = part[:half]
        send_ref[i] = part[half:].astype(BF16)


def gate_up(tok, gate_weight, up_weight, after, start, width, tile):
    live, depth = tok.shape
    half = live // 2
    weight = pl.BlockSpec((depth, tile), lambda j: (0, start // tile + j))
    out = pl.BlockSpec((2, half, tile), lambda j: (0, 0, j))
    return pl.pallas_call(
        gate_up_kernel,
        out_shape=[jax.ShapeDtypeStruct((2, half, width), BF16), jax.ShapeDtypeStruct((2, half, width), F32)],
        grid=(width // tile,),
        in_specs=[pl.BlockSpec((live, depth), lambda j: (0, 0)), weight, weight]
        + [pl.BlockSpec(memory_space=pl.ANY)] * len(after),
        out_specs=[out, out],
        compiler_params=pltpu.CompilerParams(vmem_limit_bytes=32 * MIB),
        cost_estimate=pl.CostEstimate(
            flops=0, bytes_accessed=0, transcendentals=0
        ),
        name="gate_up",
    )(tok, gate_weight, up_weight, *after)


def down_kernel(n_h, first, last, *refs):
    h_refs, w_ref, refs = refs[:n_h], refs[n_h], refs[n_h + 1:]
    h = jnp.concatenate([r[...] for r in h_refs], axis=0)
    total = jnp.dot(h, w_ref[...], preferred_element_type=F32)
    if not first:
        total += refs[0][...]
        refs = refs[1:]
    if not last:
        refs[0][...] = total
        return
    pick_ref, outs = refs[0], refs[1:]
    spread = jnp.dot(pick_ref[...], total.astype(BF16), preferred_element_type=F32).astype(BF16)
    rows = spread.shape[0] // len(outs)
    for k, out_ref in enumerate(outs):
        out_ref[...] = spread[k * rows:(k + 1) * rows]


def down(hidden, down_weight, total, pick, start, width, n_gx):
    live = sum(h.shape[0] for h in hidden)
    out_width = down_weight.shape[1]
    tile = min(out_width, 512)
    last = pick is not None
    rows = pl.BlockSpec((live, tile), lambda j: (0, j))
    operands = [*hidden, down_weight]
    in_specs = [pl.BlockSpec(h.shape, lambda j: (0, 0)) for h in hidden]
    in_specs.append(pl.BlockSpec((pl.Element(width), pl.Element(tile)), lambda j: (start, j * tile)))
    if total is not None:
        operands.append(total)
        in_specs.append(rows)
    if last:
        tok_dev = pick.shape[0] // n_gx
        operands.append(pick)
        in_specs.append(pl.BlockSpec(pick.shape, lambda j: (0, 0)))
        out_shape = [jax.ShapeDtypeStruct((tok_dev, out_width), BF16)] * n_gx
        out_specs = [pl.BlockSpec((tok_dev, tile), lambda j: (0, j))] * n_gx
    else:
        out_shape, out_specs = jax.ShapeDtypeStruct((live, out_width), F32), rows
    return pl.pallas_call(
        functools.partial(down_kernel, len(hidden), total is None, last),
        out_shape=out_shape,
        grid=(out_width // tile,),
        in_specs=in_specs,
        out_specs=out_specs,
        compiler_params=pltpu.CompilerParams(vmem_limit_bytes=32 * MIB),
        cost_estimate=pl.CostEstimate(
            flops=0, bytes_accessed=0, transcendentals=0
        ),
        name="down",
    )(*operands)


def column_chunks(cols, tile):
    tiles = cols // tile
    shares = (3, 5, 5)
    edges = [round(tiles * sum(shares[:i]) / sum(shares)) for i in range(len(shares) + 1)]
    return [(a * tile, (b - a) * tile) for a, b in zip(edges, edges[1:]) if b > a]


def local(n_gx, n_gy, tokens, gate_weight, up_weight, down_weight, lengths):
    nx = n_gy // 2
    tok_dev = tokens.shape[0]
    live = 3 * tok_dev * n_gx // 4
    quarter = live // n_gy
    cols = gate_weight.shape[1]
    tile = 512 if cols % 512 == 0 else 128
    chunks = column_chunks(cols, tile)

    def over_z(block, k, among=range(n_gx)):
        return lax.ppermute(block, "gx", [(z, z ^ k) for z in among])

    def over_core(block):
        return lax.ppermute(block, "gy", [(i, i ^ 1) for i in range(n_gy)])

    def over_x(block, k):
        return lax.ppermute(block, "gy", [(i, (i + 2 * k) % n_gy) for i in range(n_gy)])

    pick_in, pick_out = picks(lengths, n_gx, nx, tok_dev, live)
    if n_gx == 4:
        two = over_z(tokens, 2)
        one = over_z(tokens, 1)
        middle = over_z(tokens, 3, (1, 2))
        ends = over_z(two, 1, (1, 2))
        blocks = [[tokens], [one], [two], [middle, ends]]
    else:
        blocks = [[tokens]] + [[over_z(tokens, k)] for k in range(1, n_gx)]
    tok = compact(pick_in, blocks)

    total, after = None, []
    for i, (start, width) in enumerate(chunks):
        send, keep = gate_up(tok, gate_weight, up_weight, after, start, width, tile)
        sums = keep + over_core(send).astype(F32)
        mine = sums[:, :quarter]
        after = []
        for k in range(1, nx):
            block = sums[:, k * quarter:(k + 1) * quarter].astype(BF16)
            after.append(block)
            mine = mine + over_x(block, k).astype(F32)
        own = (jax.nn.silu(mine[0]) * mine[1]).astype(BF16)
        hidden = [own] + [over_x(own, -k) for k in range(1, nx)]
        hidden += [over_core(h) for h in hidden]
        last = i == len(chunks) - 1
        total = down(hidden, down_weight, total, pick_out if last else None, start, width, n_gx)

    if n_gx == 4:
        ends = over_z(total[3], 1, (0, 3))
        one = over_z(total[1], 1)
        middle = over_z(total[3], 3, (1, 2))
        two = over_z((total[2].astype(F32) + ends.astype(F32)).astype(BF16), 2)
        parts = [total[0], one, middle, two]
    else:
        parts = [total[0]] + [over_z(total[k], k) for k in range(1, n_gx)]
    return sum(p.astype(F32) for p in parts).astype(BF16)


def solution(mesh):
    placed = (P(("group", "gx"), "gy"), P("gy", "gx"), P("gy", "gx"), P("gx", "gy"), P("group"))
    return jax.shard_map(
        functools.partial(local, mesh.shape["gx"], mesh.shape["gy"]),
        mesh=mesh, in_specs=placed, out_specs=P(("group", "gx"), "gy"), check_vma=False,
    )
```

```python
import functools

import jax
import jax.numpy as jnp
from jax import lax
from jax.experimental import pallas as pl
from jax.experimental.pallas import tpu as pltpu
from jax.sharding import PartitionSpec as P

MIB = 1 << 20
BF16, F32 = jnp.bfloat16, jnp.float32


def row_sources(lengths_ref, rows, n_gx, tok_dev):
    start = jnp.int32(0)
    slot = rows
    for g in range(n_gx):
        slot = jnp.where(rows >= start, rows - start + g * tok_dev, slot)
        start = start + lengths_ref[g]
    return slot


def local_rows(shape, dim, quarter, nx):
    gy = lax.axis_index("gy")
    x, core = gy // 2, gy % 2
    j = lax.broadcasted_iota(jnp.int32, shape, dim)
    rows = jnp.zeros(shape, jnp.int32)
    for kc in range(2):
        for kx in range(nx):
            first = (kc * nx + kx) * quarter
            owner = lax.rem(x + kx, nx) * 2 + (1 - core if kc else core)
            rows = jnp.where(j >= first, owner * quarter + j - first, rows)
    return rows


def picks_kernel(n_gx, nx, tok_dev, lengths_ref, in_ref, out_ref):
    z = lax.axis_index("gx")
    live, slots = in_ref.shape
    quarter = live // (2 * nx)

    def slot_of(column):
        return (z ^ (column // tok_dev)) * tok_dev + column % tok_dev

    shape = (live, slots)
    source = row_sources(lengths_ref, local_rows(shape, 0, quarter, nx), n_gx, tok_dev)
    in_ref[...] = (source == slot_of(lax.broadcasted_iota(jnp.int32, shape, 1))).astype(F32).astype(BF16)
    shape = (slots, live)
    source = row_sources(lengths_ref, local_rows(shape, 1, quarter, nx), n_gx, tok_dev)
    out_ref[...] = (source == slot_of(lax.broadcasted_iota(jnp.int32, shape, 0))).astype(F32).astype(BF16)


def picks(lengths, n_gx, nx, tok_dev, live):
    slots = n_gx * tok_dev
    return pl.pallas_call(
        functools.partial(picks_kernel, n_gx, nx, tok_dev),
        out_shape=[jax.ShapeDtypeStruct((live, slots), BF16), jax.ShapeDtypeStruct((slots, live), BF16)],
        in_specs=[pl.BlockSpec(memory_space=pltpu.SMEM)],
        cost_estimate=pl.CostEstimate(flops=0, bytes_accessed=4 * live * slots, transcendentals=0),
        name="picks",
    )(lengths)


def compact_kernel(groups, pick_ref, *refs):
    refs, out_ref = list(refs[:-1]), refs[-1]
    blocks = []
    for n in groups:
        block = refs.pop(0)[...]
        for _ in range(n - 1):
            block = block + refs.pop(0)[...]
        blocks.append(block)
    rows = jnp.concatenate(blocks, axis=0)
    out_ref[...] = jnp.dot(pick_ref[...], rows, preferred_element_type=F32).astype(BF16)


def compact(pick, blocks):
    flat = [b for group in blocks for b in group]
    return pl.pallas_call(
        functools.partial(compact_kernel, [len(group) for group in blocks]),
        out_shape=jax.ShapeDtypeStruct((pick.shape[0], flat[0].shape[1]), BF16),
        cost_estimate=pl.CostEstimate(
            flops=2 * pick.size * flat[0].shape[1], bytes_accessed=2 * pick.size, transcendentals=0
        ),
        name="compact",
    )(pick, *flat)


def gate_up_kernel(tok_ref, gate_ref, up_ref, *refs):
    send_ref, keep_ref = refs[-2:]
    half = keep_ref.shape[1]
    rows = tok_ref[...]
    for i, w_ref in enumerate((gate_ref, up_ref)):
        part = jnp.dot(rows, w_ref[...], preferred_element_type=F32)
        keep_ref[i] = part[:half]
        send_ref[i] = part[half:].astype(BF16)


def gate_up(tok, gate_weight, up_weight, after, start, width, tile):
    live, depth = tok.shape
    half = live // 2
    weight = pl.BlockSpec((depth, tile), lambda j: (0, start // tile + j))
    out = pl.BlockSpec((2, half, tile), lambda j: (0, 0, j))
    return pl.pallas_call(
        gate_up_kernel,
        out_shape=[jax.ShapeDtypeStruct((2, half, width), BF16), jax.ShapeDtypeStruct((2, half, width), F32)],
        grid=(width // tile,),
        in_specs=[pl.BlockSpec((live, depth), lambda j: (0, 0)), weight, weight]
        + [pl.BlockSpec(memory_space=pl.ANY)] * len(after),
        out_specs=[out, out],
        compiler_params=pltpu.CompilerParams(vmem_limit_bytes=32 * MIB),
        cost_estimate=pl.CostEstimate(
            flops=0, bytes_accessed=0, transcendentals=0
        ),
        name="gate_up",
    )(tok, gate_weight, up_weight, *after)


def join_kernel(keep_ref, got_ref, *out_refs):
    quarter = out_refs[0].shape[1]
    for k, out_ref in enumerate(out_refs):
        rows = pl.ds(k * quarter, quarter)
        out_ref[...] = (keep_ref[:, rows] + got_ref[:, rows].astype(F32)).astype(out_ref.dtype)


def join(keep, got, nx):
    two, half, width = keep.shape
    shape = (two, half // nx, width)
    return pl.pallas_call(
        join_kernel,
        out_shape=[jax.ShapeDtypeStruct(shape, BF16 if k else F32) for k in range(nx)],
        cost_estimate=pl.CostEstimate(flops=0, bytes_accessed=0, transcendentals=0),
        name="join",
    )(keep, got)


def activate_kernel(n_got, mine_ref, *refs):
    own_ref = refs[n_got]
    both = mine_ref[...]
    for got_ref in refs[:n_got]:
        both = both + got_ref[...].astype(F32)
    gate, up = both[0], both[1]
    own_ref[...] = (gate / (1.0 + jnp.exp(-gate)) * up).astype(BF16)


def activate(mine, got, handed, after):
    def body(*refs):
        n_in = 1 + len(got) + len(handed) + len(after)
        activate_kernel(len(got), *refs[:1 + len(got)], refs[n_in])

    held = [pl.BlockSpec(memory_space=pltpu.VMEM)] * (1 + len(got))
    anywhere = pl.BlockSpec(memory_space=pl.ANY)
    out = pl.pallas_call(
        body,
        out_shape=[jax.ShapeDtypeStruct(mine.shape[1:], BF16)]
        + [jax.ShapeDtypeStruct(a.shape, a.dtype) for a in handed],
        in_specs=held + [anywhere] * (len(handed) + len(after)),
        out_specs=[pl.BlockSpec(memory_space=pltpu.VMEM)] + [anywhere] * len(handed),
        input_output_aliases={1 + len(got) + i: 1 + i for i in range(len(handed))},
        cost_estimate=pl.CostEstimate(flops=0, bytes_accessed=0, transcendentals=0),
        name="activate",
    )(mine, *got, *handed, *after)
    return out[0], out[1:]


def down_kernel(n_h, first, last, *refs):
    h_refs, w_ref, refs = refs[:n_h], refs[n_h], refs[n_h + 1:]
    h = jnp.concatenate([r[...] for r in h_refs], axis=0)
    total = jnp.dot(h, w_ref[...], preferred_element_type=F32)
    if not first:
        total += refs[0][...]
        refs = refs[1:]
    if not last:
        refs[0][...] = total
        return
    pick_ref, outs = refs[0], refs[1:]
    spread = jnp.dot(pick_ref[...], total.astype(BF16), preferred_element_type=F32).astype(BF16)
    rows = spread.shape[0] // len(outs)
    for k, out_ref in enumerate(outs):
        out_ref[...] = spread[k * rows:(k + 1) * rows]


def down(hidden, down_weight, total, pick, start, width, n_gx):
    live = sum(h.shape[0] for h in hidden)
    out_width = down_weight.shape[1]
    tile = min(out_width, 256)
    last = pick is not None
    rows = pl.BlockSpec((live, tile), lambda j: (0, j))
    operands = [*hidden, down_weight]
    in_specs = [pl.BlockSpec(h.shape, lambda j: (0, 0)) for h in hidden]
    in_specs.append(
        pl.BlockSpec(
            (pl.Element(width), pl.Element(tile)), lambda j: (start, j * tile)
        )
    )
    if total is not None:
        operands.append(total)
        in_specs.append(rows)
    if last:
        tok_dev = pick.shape[0] // n_gx
        operands.append(pick)
        in_specs.append(pl.BlockSpec(pick.shape, lambda j: (0, 0)))
        out_shape = [jax.ShapeDtypeStruct((tok_dev, out_width), BF16)] * n_gx
        out_specs = [pl.BlockSpec((tok_dev, tile), lambda j: (0, j))] * n_gx
    else:
        out_shape, out_specs = jax.ShapeDtypeStruct((live, out_width), F32), rows
    return pl.pallas_call(
        functools.partial(down_kernel, len(hidden), total is None, last),
        out_shape=out_shape,
        grid=(out_width // tile,),
        in_specs=in_specs,
        out_specs=out_specs,
        compiler_params=pltpu.CompilerParams(vmem_limit_bytes=32 * MIB),
        cost_estimate=pl.CostEstimate(
            flops=0, bytes_accessed=0, transcendentals=0
        ),
        name="down",
    )(*operands)


def column_chunks(cols, tile):
    tiles = cols // tile
    shares = (2, 4, 4, 3)
    edges = [round(tiles * sum(shares[:i]) / sum(shares)) for i in range(len(shares) + 1)]
    return [(a * tile, (b - a) * tile) for a, b in zip(edges, edges[1:]) if b > a]


def local(n_gx, n_gy, tokens, gate_weight, up_weight, down_weight, lengths):
    nx = n_gy // 2
    tok_dev = tokens.shape[0]
    live = 3 * tok_dev * n_gx // 4
    quarter = live // n_gy
    cols = gate_weight.shape[1]
    tile = 512 if cols % 512 == 0 else 128
    chunks = column_chunks(cols, tile)

    def over_z(block, k, among=range(n_gx)):
        return lax.ppermute(block, "gx", [(z, z ^ k) for z in among])

    def over_core(block):
        return lax.ppermute(block, "gy", [(i, i ^ 1) for i in range(n_gy)])

    def over_x(block, k):
        return lax.ppermute(block, "gy", [(i, (i + 2 * k) % n_gy) for i in range(n_gy)])

    pick_in, pick_out = picks(lengths, n_gx, nx, tok_dev, live)
    if n_gx == 4:
        two = over_z(tokens, 2)
        one = over_z(tokens, 1)
        middle = over_z(tokens, 3, (1, 2))
        ends = over_z(two, 1, (1, 2))
        blocks = [[tokens], [one], [two], [middle, ends]]
    else:
        blocks = [[tokens]] + [[over_z(tokens, k)] for k in range(1, n_gx)]
    tok = compact(pick_in, blocks)

    n = len(chunks)
    send, keep = gate_up(tok, gate_weight, up_weight, [], *chunks[0], tile)
    keeps, fars, hiddens, totals = [keep], [], [], []
    for i in range(n):
        mine, *blocks = join(keeps[i], over_core(send), nx)
        got = [over_x(b, k + 1) for k, b in enumerate(blocks)]
        handed = []
        if i + 1 < n:
            send, keep = gate_up(tok, gate_weight, up_weight, blocks, *chunks[i + 1], tile)
            keeps.append(keep)
            handed = [send]
        after = (fars[i - 1] if i >= 1 else []) + (totals[i - 2:i - 1] if i >= 2 else [])
        own, handed = activate(mine, got, handed, after)
        if handed:
            send = handed[0]
        fars.append([over_x(own, -k) for k in range(1, nx)])
        hiddens.append([own] + fars[i])
        if i >= 1:
            h = hiddens[i - 1]
            h = h + [over_core(a) for a in h]
            total = totals[-1] if totals else None
            totals.append(down(h, down_weight, total, None, *chunks[i - 1], n_gx))
    h = hiddens[-1]
    h = h + [over_core(a) for a in h]
    total = down(h, down_weight, totals[-1] if totals else None, pick_out, *chunks[-1], n_gx)

    if n_gx == 4:
        ends = over_z(total[3], 1, (0, 3))
        one = over_z(total[1], 1)
        middle = over_z(total[3], 3, (1, 2))
        two = over_z((total[2].astype(F32) + ends.astype(F32)).astype(BF16), 2)
        parts = [total[0], one, middle, two]
    else:
        parts = [total[0]] + [over_z(total[k], k) for k in range(1, n_gx)]
    return sum(p.astype(F32) for p in parts).astype(BF16)


def solution(mesh):
    placed = (P(("group", "gx"), "gy"), P("gy", "gx"), P("gy", "gx"), P("gx", "gy"), P("group"))
    return jax.shard_map(
        functools.partial(local, mesh.shape["gx"], mesh.shape["gy"]),
        mesh=mesh, in_specs=placed, out_specs=P(("group", "gx"), "gy"), check_vma=False,
    )
```

```python
import functools

import jax
import jax.numpy as jnp
from jax import lax
from jax.experimental import pallas as pl
from jax.experimental.pallas import tpu as pltpu
from jax.sharding import PartitionSpec as P

MIB = 1 << 20
BF16, F32 = jnp.bfloat16, jnp.float32


def row_sources(lengths_ref, rows, n_gx, tok_dev):
    start = jnp.int32(0)
    slot = rows
    for g in range(n_gx):
        slot = jnp.where(rows >= start, rows - start + g * tok_dev, slot)
        start = start + lengths_ref[g]
    return slot


def local_rows(shape, dim, quarter, nx):
    gy = lax.axis_index("gy")
    x, core = gy // 2, gy % 2
    j = lax.broadcasted_iota(jnp.int32, shape, dim)
    rows = jnp.zeros(shape, jnp.int32)
    for kc in range(2):
        for kx in range(nx):
            first = (kc * nx + kx) * quarter
            owner = lax.rem(x + kx, nx) * 2 + (1 - core if kc else core)
            rows = jnp.where(j >= first, owner * quarter + j - first, rows)
    return rows


def picks_kernel(n_gx, nx, tok_dev, lengths_ref, in_ref, out_ref):
    z = lax.axis_index("gx")
    live, slots = in_ref.shape
    quarter = live // (2 * nx)

    def slot_of(column):
        return (z ^ (column // tok_dev)) * tok_dev + column % tok_dev

    shape = (live, slots)
    source = row_sources(lengths_ref, local_rows(shape, 0, quarter, nx), n_gx, tok_dev)
    in_ref[...] = (source == slot_of(lax.broadcasted_iota(jnp.int32, shape, 1))).astype(F32).astype(BF16)
    shape = (slots, live)
    source = row_sources(lengths_ref, local_rows(shape, 1, quarter, nx), n_gx, tok_dev)
    out_ref[...] = (source == slot_of(lax.broadcasted_iota(jnp.int32, shape, 0))).astype(F32).astype(BF16)


def picks(lengths, n_gx, nx, tok_dev, live):
    slots = n_gx * tok_dev
    return pl.pallas_call(
        functools.partial(picks_kernel, n_gx, nx, tok_dev),
        out_shape=[jax.ShapeDtypeStruct((live, slots), BF16), jax.ShapeDtypeStruct((slots, live), BF16)],
        in_specs=[pl.BlockSpec(memory_space=pltpu.SMEM)],
        cost_estimate=pl.CostEstimate(flops=0, bytes_accessed=4 * live * slots, transcendentals=0),
        compiler_params=pltpu.CompilerParams(vmem_limit_bytes=8 * MIB),
        name="picks",
    )(lengths)


def compact_kernel(groups, pick_ref, *refs):
    refs, out_ref = list(refs[:-1]), refs[-1]
    blocks = []
    for n in groups:
        block = refs.pop(0)[...]
        for _ in range(n - 1):
            block = block + refs.pop(0)[...]
        blocks.append(block)
    rows = jnp.concatenate(blocks, axis=0)
    out_ref[...] = jnp.dot(pick_ref[...], rows, preferred_element_type=F32).astype(BF16)


def compact(pick, blocks):
    flat = [b for group in blocks for b in group]
    return pl.pallas_call(
        functools.partial(compact_kernel, [len(group) for group in blocks]),
        out_shape=jax.ShapeDtypeStruct((pick.shape[0], flat[0].shape[1]), BF16),
        cost_estimate=pl.CostEstimate(
            flops=2 * pick.size * flat[0].shape[1], bytes_accessed=2 * pick.size, transcendentals=0
        ),
        compiler_params=pltpu.CompilerParams(vmem_limit_bytes=8 * MIB),
        name="compact",
    )(pick, *flat)


def gate_up_kernel(tok_ref, gate_ref, up_ref, *refs):
    send_ref, keep_ref = refs[-2:]
    half = keep_ref.shape[1]
    rows = tok_ref[...]
    for i, w_ref in enumerate((gate_ref, up_ref)):
        part = jnp.dot(rows, w_ref[...], preferred_element_type=F32)
        keep_ref[i] = part[:half]
        send_ref[i] = part[half:].astype(BF16)


def gate_up(tok, gate_weight, up_weight, after, start, width, tile):
    live, depth = tok.shape
    half = live // 2
    weight = pl.BlockSpec((depth, tile), lambda j: (0, start // tile + j))
    out = pl.BlockSpec((2, half, tile), lambda j: (0, 0, j))
    return pl.pallas_call(
        gate_up_kernel,
        out_shape=[jax.ShapeDtypeStruct((2, half, width), BF16), jax.ShapeDtypeStruct((2, half, width), F32)],
        grid=(width // tile,),
        in_specs=[pl.BlockSpec((live, depth), lambda j: (0, 0)), weight, weight]
        + [pl.BlockSpec(memory_space=pl.ANY)] * len(after),
        out_specs=[out, out],
        compiler_params=pltpu.CompilerParams(vmem_limit_bytes=20 * MIB),
        cost_estimate=pl.CostEstimate(
            flops=0, bytes_accessed=0, transcendentals=0
        ),
        name="gate_up",
    )(tok, gate_weight, up_weight, *after)


def join_kernel(keep_ref, got_ref, *out_refs):
    quarter = out_refs[0].shape[1]
    for k, out_ref in enumerate(out_refs):
        rows = pl.ds(k * quarter, quarter)
        out_ref[...] = (keep_ref[:, rows] + got_ref[:, rows].astype(F32)).astype(out_ref.dtype)


def join(keep, got, nx):
    two, half, width = keep.shape
    shape = (two, half // nx, width)
    return pl.pallas_call(
        join_kernel,
        out_shape=[jax.ShapeDtypeStruct(shape, BF16 if k else F32) for k in range(nx)],
        cost_estimate=pl.CostEstimate(flops=0, bytes_accessed=0, transcendentals=0),
        compiler_params=pltpu.CompilerParams(vmem_limit_bytes=8 * MIB),
        name="join",
    )(keep, got)


def activate_kernel(n_got, mine_ref, *refs):
    own_ref = refs[n_got]
    both = mine_ref[...]
    for got_ref in refs[:n_got]:
        both = both + got_ref[...].astype(F32)
    gate, up = both[0], both[1]
    own_ref[...] = (gate / (1.0 + jnp.exp(-gate)) * up).astype(BF16)


def activate(mine, got, handed, after):
    def body(*refs):
        n_in = 1 + len(got) + len(handed) + len(after)
        activate_kernel(len(got), *refs[:1 + len(got)], refs[n_in])

    held = [pl.BlockSpec(memory_space=pltpu.VMEM)] * (1 + len(got))
    anywhere = pl.BlockSpec(memory_space=pl.ANY)
    out = pl.pallas_call(
        body,
        out_shape=[jax.ShapeDtypeStruct(mine.shape[1:], BF16)]
        + [jax.ShapeDtypeStruct(a.shape, a.dtype) for a in handed],
        in_specs=held + [anywhere] * (len(handed) + len(after)),
        out_specs=[pl.BlockSpec(memory_space=pltpu.VMEM)] + [anywhere] * len(handed),
        input_output_aliases={1 + len(got) + i: 1 + i for i in range(len(handed))},
        cost_estimate=pl.CostEstimate(flops=0, bytes_accessed=0, transcendentals=0),
        compiler_params=pltpu.CompilerParams(vmem_limit_bytes=8 * MIB),
        name="activate",
    )(mine, *got, *handed, *after)
    return out[0], out[1:]


def down_kernel(n_h, first, last, *refs):
    h_refs, w_ref, refs = refs[:n_h], refs[n_h], refs[n_h + 1:]
    h = jnp.concatenate([r[...] for r in h_refs], axis=0)
    total = jnp.dot(h, w_ref[...], preferred_element_type=F32)
    if not first:
        total += refs[0][...]
        refs = refs[1:]
    if not last:
        refs[0][...] = total
        return
    pick_ref, outs = refs[0], refs[1:]
    spread = jnp.dot(pick_ref[...], total.astype(BF16), preferred_element_type=F32).astype(BF16)
    rows = spread.shape[0] // len(outs)
    for k, out_ref in enumerate(outs):
        out_ref[...] = spread[k * rows:(k + 1) * rows]


def down(hidden, down_weight, total, pick, start, width, n_gx):
    live = sum(h.shape[0] for h in hidden)
    out_width = down_weight.shape[1]
    tile = min(out_width, 256)
    last = pick is not None
    rows = pl.BlockSpec((live, tile), lambda j: (0, j))
    operands = [*hidden, down_weight]
    in_specs = [pl.BlockSpec(h.shape, lambda j: (0, 0)) for h in hidden]
    in_specs.append(
        pl.BlockSpec(
            (pl.Element(width), pl.Element(tile)), lambda j: (start, j * tile)
        )
    )
    if total is not None:
        operands.append(total)
        in_specs.append(rows)
    if last:
        tok_dev = pick.shape[0] // n_gx
        operands.append(pick)
        in_specs.append(pl.BlockSpec(pick.shape, lambda j: (0, 0)))
        out_shape = [jax.ShapeDtypeStruct((tok_dev, out_width), BF16)] * n_gx
        out_specs = [pl.BlockSpec((tok_dev, tile), lambda j: (0, j))] * n_gx
    else:
        out_shape, out_specs = jax.ShapeDtypeStruct((live, out_width), F32), rows
    return pl.pallas_call(
        functools.partial(down_kernel, len(hidden), total is None, last),
        out_shape=out_shape,
        grid=(out_width // tile,),
        in_specs=in_specs,
        out_specs=out_specs,
        compiler_params=pltpu.CompilerParams(vmem_limit_bytes=20 * MIB),
        cost_estimate=pl.CostEstimate(
            flops=0, bytes_accessed=0, transcendentals=0
        ),
        name="down",
    )(*operands)


def column_chunks(cols, tile):
    tiles = cols // tile
    shares = (2, 4, 4, 3)
    edges = [round(tiles * sum(shares[:i]) / sum(shares)) for i in range(len(shares) + 1)]
    return [(a * tile, (b - a) * tile) for a, b in zip(edges, edges[1:]) if b > a]


def local(n_gx, n_gy, tokens, gate_weight, up_weight, down_weight, lengths):
    nx = n_gy // 2
    tok_dev = tokens.shape[0]
    live = 3 * tok_dev * n_gx // 4
    quarter = live // n_gy
    cols = gate_weight.shape[1]
    tile = 512 if cols % 512 == 0 else 128
    chunks = column_chunks(cols, tile)

    def over_z(block, k, among=range(n_gx)):
        return lax.ppermute(block, "gx", [(z, z ^ k) for z in among])

    def over_core(block):
        return lax.ppermute(block, "gy", [(i, i ^ 1) for i in range(n_gy)])

    def over_x(block, k):
        return lax.ppermute(block, "gy", [(i, (i + 2 * k) % n_gy) for i in range(n_gy)])

    pick_in, pick_out = picks(lengths, n_gx, nx, tok_dev, live)
    if n_gx == 4:
        two = over_z(tokens, 2)
        one = over_z(tokens, 1)
        middle = over_z(tokens, 3, (1, 2))
        ends = over_z(two, 1, (1, 2))
        blocks = [[tokens], [one], [two], [middle, ends]]
    else:
        blocks = [[tokens]] + [[over_z(tokens, k)] for k in range(1, n_gx)]
    tok = compact(pick_in, blocks)

    n = len(chunks)
    send, keep = gate_up(tok, gate_weight, up_weight, [], *chunks[0], tile)
    keeps, fars, hiddens, totals = [keep], [], [], []
    for i in range(n):
        mine, *blocks = join(keeps[i], over_core(send), nx)
        got = [over_x(b, k + 1) for k, b in enumerate(blocks)]
        handed = []
        if i + 1 < n:
            send, keep = gate_up(tok, gate_weight, up_weight, blocks, *chunks[i + 1], tile)
            keeps.append(keep)
            handed = [send]
        after = (fars[i - 1] if i >= 1 else []) + (totals[i - 2:i - 1] if i >= 2 else [])
        own, handed = activate(mine, got, handed, after)
        if handed:
            send = handed[0]
        fars.append([over_x(own, -k) for k in range(1, nx)])
        hiddens.append([own] + fars[i])
        if i >= 1:
            h = hiddens[i - 1]
            h = h + [over_core(a) for a in h]
            total = totals[-1] if totals else None
            totals.append(down(h, down_weight, total, None, *chunks[i - 1], n_gx))
    h = hiddens[-1]
    h = h + [over_core(a) for a in h]
    total = down(h, down_weight, totals[-1] if totals else None, pick_out, *chunks[-1], n_gx)

    if n_gx == 4:
        ends = over_z(total[3], 1, (0, 3))
        one = over_z(total[1], 1)
        middle = over_z(total[3], 3, (1, 2))
        two = over_z((total[2].astype(F32) + ends.astype(F32)).astype(BF16), 2)
        parts = [total[0], one, middle, two]
    else:
        parts = [total[0]] + [over_z(total[k], k) for k in range(1, n_gx)]
    return sum(p.astype(F32) for p in parts).astype(BF16)


def solution(mesh):
    placed = (P(("group", "gx"), "gy"), P("gy", "gx"), P("gy", "gx"), P("gx", "gy"), P("group"))
    return jax.shard_map(
        functools.partial(local, mesh.shape["gx"], mesh.shape["gy"]),
        mesh=mesh, in_specs=placed, out_specs=P(("group", "gx"), "gy"), check_vma=False,
    )
```

```python
import functools

import jax
import jax.numpy as jnp
from jax import lax
from jax.experimental import pallas as pl
from jax.experimental.pallas import tpu as pltpu
from jax.sharding import PartitionSpec as P

MIB = 1 << 20
BF16, F32 = jnp.bfloat16, jnp.float32


def row_sources(lengths_ref, rows, n_gx, tok_dev):
    start = jnp.int32(0)
    slot = rows
    for g in range(n_gx):
        slot = jnp.where(rows >= start, rows - start + g * tok_dev, slot)
        start = start + lengths_ref[g]
    return slot


def local_rows(shape, dim, quarter, nx):
    gy = lax.axis_index("gy")
    x, core = gy // 2, gy % 2
    j = lax.broadcasted_iota(jnp.int32, shape, dim)
    rows = jnp.zeros(shape, jnp.int32)
    for kc in range(2):
        for kx in range(nx):
            first = (kc * nx + kx) * quarter
            owner = lax.rem(x + kx, nx) * 2 + (1 - core if kc else core)
            rows = jnp.where(j >= first, owner * quarter + j - first, rows)
    return rows


def picks_kernel(n_gx, nx, tok_dev, lengths_ref, in_ref, out_ref):
    z = lax.axis_index("gx")
    live, slots = in_ref.shape
    quarter = live // (2 * nx)

    def slot_of(column):
        return (z ^ (column // tok_dev)) * tok_dev + column % tok_dev

    shape = (live, slots)
    source = row_sources(lengths_ref, local_rows(shape, 0, quarter, nx), n_gx, tok_dev)
    in_ref[...] = (source == slot_of(lax.broadcasted_iota(jnp.int32, shape, 1))).astype(F32).astype(BF16)
    shape = (slots, live)
    source = row_sources(lengths_ref, local_rows(shape, 1, quarter, nx), n_gx, tok_dev)
    out_ref[...] = (source == slot_of(lax.broadcasted_iota(jnp.int32, shape, 0))).astype(F32).astype(BF16)


def picks(lengths, n_gx, nx, tok_dev, live):
    slots = n_gx * tok_dev
    return pl.pallas_call(
        functools.partial(picks_kernel, n_gx, nx, tok_dev),
        out_shape=[jax.ShapeDtypeStruct((live, slots), BF16), jax.ShapeDtypeStruct((slots, live), BF16)],
        in_specs=[pl.BlockSpec(memory_space=pltpu.SMEM)],
        cost_estimate=pl.CostEstimate(flops=0, bytes_accessed=4 * live * slots, transcendentals=0),
        compiler_params=pltpu.CompilerParams(vmem_limit_bytes=8 * MIB),
        name="picks",
    )(lengths)


def compact_kernel(groups, pick_ref, *refs):
    refs, out_ref = list(refs[:-1]), refs[-1]
    blocks = []
    for n in groups:
        block = refs.pop(0)[...]
        for _ in range(n - 1):
            block = block + refs.pop(0)[...]
        blocks.append(block)
    rows = jnp.concatenate(blocks, axis=0)
    out_ref[...] = jnp.dot(pick_ref[...], rows, preferred_element_type=F32).astype(BF16)


def compact(pick, blocks):
    flat = [b for group in blocks for b in group]
    return pl.pallas_call(
        functools.partial(compact_kernel, [len(group) for group in blocks]),
        out_shape=jax.ShapeDtypeStruct((pick.shape[0], flat[0].shape[1]), BF16),
        cost_estimate=pl.CostEstimate(
            flops=2 * pick.size * flat[0].shape[1], bytes_accessed=2 * pick.size, transcendentals=0
        ),
        compiler_params=pltpu.CompilerParams(vmem_limit_bytes=8 * MIB),
        name="compact",
    )(pick, *flat)


def gate_up_kernel(tok_ref, gate_ref, up_ref, *refs):
    send_ref, keep_ref = refs[-2:]
    half = keep_ref.shape[1]
    rows = tok_ref[...]
    for i, w_ref in enumerate((gate_ref, up_ref)):
        part = jnp.dot(rows, w_ref[...], preferred_element_type=F32)
        keep_ref[i] = part[:half]
        send_ref[i] = part[half:].astype(BF16)


def gate_up(tok, gate_weight, up_weight, after, start, width, tile):
    live, depth = tok.shape
    half = live // 2
    weight = pl.BlockSpec((depth, tile), lambda j: (0, start // tile + j))
    out = pl.BlockSpec((2, half, tile), lambda j: (0, 0, j))
    return pl.pallas_call(
        gate_up_kernel,
        out_shape=[jax.ShapeDtypeStruct((2, half, width), BF16), jax.ShapeDtypeStruct((2, half, width), F32)],
        grid=(width // tile,),
        in_specs=[pl.BlockSpec((live, depth), lambda j: (0, 0)), weight, weight]
        + [pl.BlockSpec(memory_space=pl.ANY)] * len(after),
        out_specs=[out, out],
        compiler_params=pltpu.CompilerParams(vmem_limit_bytes=40 * MIB),
        cost_estimate=pl.CostEstimate(
            flops=0, bytes_accessed=0, transcendentals=0
        ),
        name="gate_up",
    )(tok, gate_weight, up_weight, *after)


def join_kernel(n_handed, n_after, nx, keep_ref, got_ref, *refs):
    out_refs = refs[n_handed + n_after:][:nx]
    quarter = out_refs[0].shape[1]
    for k, out_ref in enumerate(out_refs):
        rows = pl.ds(k * quarter, quarter)
        out_ref[...] = (keep_ref[:, rows] + got_ref[:, rows].astype(F32)).astype(out_ref.dtype)


def join(keep, got, handed, after, nx):
    two, half, width = keep.shape
    shape = (two, half // nx, width)
    held, anywhere = pl.BlockSpec(memory_space=pltpu.VMEM), pl.BlockSpec(memory_space=pl.ANY)
    out = pl.pallas_call(
        functools.partial(join_kernel, len(handed), len(after), nx),
        out_shape=[jax.ShapeDtypeStruct(shape, BF16 if k else F32) for k in range(nx)]
        + [jax.ShapeDtypeStruct(a.shape, a.dtype) for a in handed],
        in_specs=[held, held] + [anywhere] * (len(handed) + len(after)),
        out_specs=[held] * nx + [anywhere] * len(handed),
        input_output_aliases={2 + i: nx + i for i in range(len(handed))},
        compiler_params=pltpu.CompilerParams(vmem_limit_bytes=8 * MIB),
        cost_estimate=pl.CostEstimate(flops=0, bytes_accessed=0, transcendentals=0),
        name="join",
    )(keep, got, *handed, *after)
    return out[0], out[1:nx], out[nx:]


def activate_kernel(n_got, mine_ref, *refs):
    both = mine_ref[...]
    for got_ref in refs[:n_got]:
        both = both + got_ref[...].astype(F32)
    gate, up = both[0], both[1]
    refs[-1][...] = (gate / (1.0 + jnp.exp(-gate)) * up).astype(BF16)


def activate(mine, got, after):
    held, anywhere = pl.BlockSpec(memory_space=pltpu.VMEM), pl.BlockSpec(memory_space=pl.ANY)
    return pl.pallas_call(
        functools.partial(activate_kernel, len(got)),
        out_shape=jax.ShapeDtypeStruct(mine.shape[1:], BF16),
        in_specs=[held] * (1 + len(got)) + [anywhere] * len(after),
        out_specs=held,
        compiler_params=pltpu.CompilerParams(vmem_limit_bytes=8 * MIB),
        cost_estimate=pl.CostEstimate(flops=0, bytes_accessed=0, transcendentals=0),
        name="activate",
    )(mine, *got, *after)


def down_kernel(n_h, n_after, first, last, *refs):
    h_refs, w_ref, refs = refs[:n_h], refs[n_h], refs[n_h + 1 + n_after:]
    h = jnp.concatenate([r[...] for r in h_refs], axis=0)
    total = jnp.dot(h, w_ref[...], preferred_element_type=F32)
    if not first:
        total += refs[0][...]
        refs = refs[1:]
    if not last:
        refs[0][...] = total
        return
    pick_ref, outs = refs[0], refs[1:]
    spread = jnp.dot(pick_ref[...], total.astype(BF16), preferred_element_type=F32).astype(BF16)
    rows = spread.shape[0] // len(outs)
    for k, out_ref in enumerate(outs):
        out_ref[...] = spread[k * rows:(k + 1) * rows]


def down(hidden, down_weight, total, pick, after, start, width, n_gx):
    live = sum(h.shape[0] for h in hidden)
    out_width = down_weight.shape[1]
    tile = min(out_width, 512)
    last = pick is not None
    rows = pl.BlockSpec((live, tile), lambda j: (0, j))
    operands = [*hidden, down_weight]
    in_specs = [pl.BlockSpec(h.shape, lambda j: (0, 0)) for h in hidden]
    in_specs.append(
        pl.BlockSpec(
            (pl.Element(width), pl.Element(tile)), lambda j: (start, j * tile)
        )
    )
    operands += after
    in_specs += [pl.BlockSpec(memory_space=pl.ANY)] * len(after)
    if total is not None:
        operands.append(total)
        in_specs.append(rows)
    if last:
        tok_dev = pick.shape[0] // n_gx
        operands.append(pick)
        in_specs.append(pl.BlockSpec(pick.shape, lambda j: (0, 0)))
        out_shape = [jax.ShapeDtypeStruct((tok_dev, out_width), BF16)] * n_gx
        out_specs = [pl.BlockSpec((tok_dev, tile), lambda j: (0, j))] * n_gx
    else:
        out_shape, out_specs = jax.ShapeDtypeStruct((live, out_width), F32), rows
    return pl.pallas_call(
        functools.partial(down_kernel, len(hidden), len(after), total is None, last),
        out_shape=out_shape,
        grid=(out_width // tile,),
        in_specs=in_specs,
        out_specs=out_specs,
        compiler_params=pltpu.CompilerParams(vmem_limit_bytes=40 * MIB),
        cost_estimate=pl.CostEstimate(
            flops=0, bytes_accessed=0, transcendentals=0
        ),
        name="down",
    )(*operands)


def column_chunks(cols, tile):
    tiles = cols // tile
    shares = (2, 4, 4, 3)
    edges = [round(tiles * sum(shares[:i]) / sum(shares)) for i in range(len(shares) + 1)]
    return [(a * tile, (b - a) * tile) for a, b in zip(edges, edges[1:]) if b > a]


def local(n_gx, n_gy, tokens, gate_weight, up_weight, down_weight, lengths):
    nx = n_gy // 2
    tok_dev = tokens.shape[0]
    live = 3 * tok_dev * n_gx // 4
    quarter = live // n_gy
    cols = gate_weight.shape[1]
    tile = 512 if cols % 512 == 0 else 128
    chunks = column_chunks(cols, tile)

    def over_z(block, k, among=range(n_gx)):
        return lax.ppermute(block, "gx", [(z, z ^ k) for z in among])

    def over_core(block):
        return lax.ppermute(block, "gy", [(i, i ^ 1) for i in range(n_gy)])

    def over_x(block, k):
        return lax.ppermute(block, "gy", [(i, (i + 2 * k) % n_gy) for i in range(n_gy)])

    pick_in, pick_out = picks(lengths, n_gx, nx, tok_dev, live)
    if n_gx == 4:
        two = over_z(tokens, 2)
        one = over_z(tokens, 1)
        middle = over_z(tokens, 3, (1, 2))
        ends = over_z(two, 1, (1, 2))
        blocks = [[tokens], [one], [two], [middle, ends]]
    else:
        blocks = [[tokens]] + [[over_z(tokens, k)] for k in range(1, n_gx)]
    tok = compact(pick_in, blocks)

    n = len(chunks)
    first = [gate_up(tok, gate_weight, up_weight, [], *chunk, tile) for chunk in chunks[:2]]
    sends, keeps = [list(a) for a in zip(*first)]
    owns, fars, totals = [], [], []

    def add_down(after):
        i = len(totals)
        h = [owns[i]] + fars[i]
        h = h + [over_core(a) for a in h]
        pick = pick_out if i == n - 1 else None
        totals.append(down(h, down_weight, totals[-1] if totals else None, pick, after, *chunks[i], n_gx))

    for j in range(n):
        after = owns[j - 1:] + (fars[j - 2] if j >= 2 else []) + totals[-1:]
        mine, blocks, handed = join(keeps[j], over_core(sends[j]), sends[j + 1:j + 2], after, nx)
        sends[j + 1:j + 2] = handed
        got = [over_x(b, k + 1) for k, b in enumerate(blocks)]
        if j + 2 < n:
            send, keep = gate_up(tok, gate_weight, up_weight, blocks, *chunks[j + 2], tile)
            sends.append(send)
            keeps.append(keep)
        elif j >= n - 2 and len(totals) < n - 1:
            add_down(list(blocks))
        own = activate(mine, got, totals[-1:])
        owns.append(own)
        fars.append([over_x(own, -k) for k in range(1, nx)])
    while len(totals) < n:
        add_down([])
    total = totals[-1]

    if n_gx == 4:
        ends = over_z(total[3], 1, (0, 3))
        one = over_z(total[1], 1)
        middle = over_z(total[3], 3, (1, 2))
        two = over_z((total[2].astype(F32) + ends.astype(F32)).astype(BF16), 2)
        parts = [total[0], one, middle, two]
    else:
        parts = [total[0]] + [over_z(total[k], k) for k in range(1, n_gx)]
    return sum(p.astype(F32) for p in parts).astype(BF16)


def solution(mesh):
    placed = (P(("group", "gx"), "gy"), P("gy", "gx"), P("gy", "gx"), P("gx", "gy"), P("group"))
    return jax.shard_map(
        functools.partial(local, mesh.shape["gx"], mesh.shape["gy"]),
        mesh=mesh, in_specs=placed, out_specs=P(("group", "gx"), "gy"), check_vma=False,
    )
```

```python
import functools

import jax
import jax.numpy as jnp
from jax import lax
from jax.experimental import pallas as pl
from jax.experimental.pallas import tpu as pltpu
from jax.sharding import PartitionSpec as P

MIB = 1 << 20
BF16, F32 = jnp.bfloat16, jnp.float32


def row_sources(lengths_ref, rows, n_gx, tok_dev):
    start = jnp.int32(0)
    slot = rows
    for g in range(n_gx):
        slot = jnp.where(rows >= start, rows - start + g * tok_dev, slot)
        start = start + lengths_ref[g]
    return slot


def local_rows(shape, dim, quarter, nx):
    gy = lax.axis_index("gy")
    x, core = gy // 2, gy % 2
    j = lax.broadcasted_iota(jnp.int32, shape, dim)
    rows = jnp.zeros(shape, jnp.int32)
    for kc in range(2):
        for kx in range(nx):
            first = (kc * nx + kx) * quarter
            owner = lax.rem(x + kx, nx) * 2 + (1 - core if kc else core)
            rows = jnp.where(j >= first, owner * quarter + j - first, rows)
    return rows


def picks_kernel(n_gx, nx, tok_dev, lengths_ref, tok_ref, in_ref, out_ref, held_ref):
    z = lax.axis_index("gx")
    live, slots = in_ref.shape
    held_ref[...] = tok_ref[...]
    quarter = live // (2 * nx)

    def slot_of(column):
        return (z ^ (column // tok_dev)) * tok_dev + column % tok_dev

    shape = (live, slots)
    source = row_sources(lengths_ref, local_rows(shape, 0, quarter, nx), n_gx, tok_dev)
    in_ref[...] = (source == slot_of(lax.broadcasted_iota(jnp.int32, shape, 1))).astype(F32).astype(BF16)
    shape = (slots, live)
    source = row_sources(lengths_ref, local_rows(shape, 1, quarter, nx), n_gx, tok_dev)
    out_ref[...] = (source == slot_of(lax.broadcasted_iota(jnp.int32, shape, 0))).astype(F32).astype(BF16)


def picks(lengths, tokens, n_gx, nx, live):
    tok_dev = tokens.shape[0]
    slots = n_gx * tok_dev
    held = pl.BlockSpec(memory_space=pltpu.VMEM)
    return pl.pallas_call(
        functools.partial(picks_kernel, n_gx, nx, tok_dev),
        out_shape=[
            jax.ShapeDtypeStruct((live, slots), BF16),
            jax.ShapeDtypeStruct((slots, live), BF16),
            jax.ShapeDtypeStruct(tokens.shape, tokens.dtype),
        ],
        in_specs=[pl.BlockSpec(memory_space=pltpu.SMEM), held],
        out_specs=[held] * 3,
        cost_estimate=pl.CostEstimate(flops=0, bytes_accessed=4 * live * slots, transcendentals=0),
        compiler_params=pltpu.CompilerParams(vmem_limit_bytes=8 * MIB),
        name="picks",
    )(lengths, tokens)


def compact_kernel(groups, pick_ref, *refs):
    refs = list(refs)
    out_ref = refs.pop()

    def rows_of(n):
        return jnp.concatenate([refs.pop(0)[...] for _ in range(n)], axis=0)

    blocks = []
    for group in groups:
        block = rows_of(group[0])
        for n in group[1:]:
            block = block + rows_of(n)
        blocks.append(block)
    rows = jnp.concatenate(blocks, axis=0)
    out_ref[...] = jnp.dot(pick_ref[...], rows, preferred_element_type=F32).astype(BF16)


def compact(pick, blocks):
    flat = [piece for group in blocks for pieces in group for piece in pieces]
    return pl.pallas_call(
        functools.partial(compact_kernel, [[len(pieces) for pieces in group] for group in blocks]),
        out_shape=jax.ShapeDtypeStruct((pick.shape[0], flat[0].shape[1]), BF16),
        compiler_params=pltpu.CompilerParams(vmem_limit_bytes=8 * MIB),
        cost_estimate=pl.CostEstimate(
            flops=2 * pick.size * flat[0].shape[1], bytes_accessed=2 * pick.size, transcendentals=0
        ),
        name="compact",
    )(pick, *flat)


def gate_up_kernel(tok_ref, gate_ref, up_ref, *refs):
    send_ref, keep_ref = refs[-2:]
    half = keep_ref.shape[1]
    rows = tok_ref[...]
    for i, w_ref in enumerate((gate_ref, up_ref)):
        part = jnp.dot(rows, w_ref[...], preferred_element_type=F32)
        keep_ref[i] = part[:half]
        send_ref[i] = part[half:].astype(BF16)


def gate_up(tok, gate_weight, up_weight, after, start, width, tile):
    live, depth = tok.shape
    half = live // 2
    weight = pl.BlockSpec((depth, tile), lambda j: (0, start // tile + j))
    out = pl.BlockSpec((2, half, tile), lambda j: (0, 0, j))
    return pl.pallas_call(
        gate_up_kernel,
        out_shape=[jax.ShapeDtypeStruct((2, half, width), BF16), jax.ShapeDtypeStruct((2, half, width), F32)],
        grid=(width // tile,),
        in_specs=[pl.BlockSpec((live, depth), lambda j: (0, 0)), weight, weight]
        + [pl.BlockSpec(memory_space=pl.ANY)] * len(after),
        out_specs=[out, out],
        compiler_params=pltpu.CompilerParams(vmem_limit_bytes=40 * MIB),
        cost_estimate=pl.CostEstimate(
            flops=0, bytes_accessed=0, transcendentals=0
        ),
        name="gate_up",
    )(tok, gate_weight, up_weight, *after)


def join_kernel(n_handed, n_after, nx, keep_ref, got_ref, *refs):
    out_refs = refs[n_handed + n_after:][:nx]
    quarter = out_refs[0].shape[1]
    for k, out_ref in enumerate(out_refs):
        rows = pl.ds(k * quarter, quarter)
        out_ref[...] = (keep_ref[:, rows] + got_ref[:, rows].astype(F32)).astype(out_ref.dtype)


def join(keep, got, handed, after, nx):
    two, half, width = keep.shape
    shape = (two, half // nx, width)
    held, anywhere = pl.BlockSpec(memory_space=pltpu.VMEM), pl.BlockSpec(memory_space=pl.ANY)
    out = pl.pallas_call(
        functools.partial(join_kernel, len(handed), len(after), nx),
        out_shape=[jax.ShapeDtypeStruct(shape, BF16 if k else F32) for k in range(nx)]
        + [jax.ShapeDtypeStruct(a.shape, a.dtype) for a in handed],
        in_specs=[held, held] + [anywhere] * (len(handed) + len(after)),
        out_specs=[held] * nx + [anywhere] * len(handed),
        input_output_aliases={2 + i: nx + i for i in range(len(handed))},
        compiler_params=pltpu.CompilerParams(vmem_limit_bytes=8 * MIB),
        cost_estimate=pl.CostEstimate(flops=0, bytes_accessed=0, transcendentals=0),
        name="join",
    )(keep, got, *handed, *after)
    return out[0], out[1:nx], out[nx:]


def activate_kernel(n_got, n_unread, mine_ref, *refs):
    both = mine_ref[...]
    for got_ref in refs[:n_got]:
        both = both + got_ref[...].astype(F32)
    gate, up = both[0], both[1]
    refs[n_got + n_unread][...] = (gate / (1.0 + jnp.exp(-gate)) * up).astype(BF16)


def activate(mine, got, handed, after):
    held, anywhere = pl.BlockSpec(memory_space=pltpu.VMEM), pl.BlockSpec(memory_space=pl.ANY)
    out = pl.pallas_call(
        functools.partial(activate_kernel, len(got), len(handed) + len(after)),
        out_shape=[jax.ShapeDtypeStruct(mine.shape[1:], BF16)]
        + [jax.ShapeDtypeStruct(a.shape, a.dtype) for a in handed],
        in_specs=[held] * (1 + len(got)) + [anywhere] * (len(handed) + len(after)),
        out_specs=[held] + [anywhere] * len(handed),
        input_output_aliases={1 + len(got) + i: 1 + i for i in range(len(handed))},
        compiler_params=pltpu.CompilerParams(vmem_limit_bytes=8 * MIB),
        cost_estimate=pl.CostEstimate(flops=0, bytes_accessed=0, transcendentals=0),
        name="activate",
    )(mine, *got, *handed, *after)
    return out[0], out[1:]


def relay_kernel(own_ref, got_ref, *refs):
    out_ref = refs[len(refs) // 2]
    out_ref[...] = (own_ref[...].astype(F32) + got_ref[...].astype(F32)).astype(BF16)


def relay(own, got, handed, after):
    held, anywhere = pl.BlockSpec(memory_space=pltpu.VMEM), pl.BlockSpec(memory_space=pl.ANY)
    out = pl.pallas_call(
        relay_kernel,
        out_shape=[jax.ShapeDtypeStruct(a.shape, a.dtype) for a in (own, *handed)],
        in_specs=[held, held] + [anywhere] * (1 + len(handed)),
        out_specs=[held] + [anywhere] * len(handed),
        input_output_aliases={2 + i: 1 + i for i in range(len(handed))},
        compiler_params=pltpu.CompilerParams(vmem_limit_bytes=8 * MIB),
        cost_estimate=pl.CostEstimate(flops=0, bytes_accessed=0, transcendentals=0),
        name="relay",
    )(own, got, *handed, after)
    return out[0], out[1:]


def down_kernel(pieces, n_after, first, last, *refs):
    refs, hidden = list(refs[:-1]), refs[-1]
    h_refs = [[refs.pop(0) for _ in range(n)] for n in pieces]
    w_ref, refs = refs[0], refs[1 + n_after:]

    @pl.when(pl.program_id(0) == 0)
    def _():
        column = 0
        for chunk in h_refs:
            row = 0
            for r in chunk:
                n, width = r.shape
                hidden[row:row + n, column:column + width] = r[...]
                row += n
            column += width

    total = jnp.dot(hidden[...], w_ref[...], preferred_element_type=F32)
    if not first:
        total += refs[0][...]
        refs = refs[1:]
    if not last:
        refs[0][...] = total
        return
    pick_ref, outs = refs[0], refs[1:]
    spread = jnp.dot(pick_ref[...], total.astype(BF16), preferred_element_type=F32).astype(BF16)
    row = 0
    for out_ref in outs:
        n = out_ref.shape[0]
        out_ref[...] = spread[row:row + n]
        row += n


def down(hidden, down_weight, total, pick, out_rows, after, start):
    live = sum(h.shape[0] for h in hidden[0])
    width = sum(chunk[0].shape[1] for chunk in hidden)
    out_width = down_weight.shape[1]
    tile = min(out_width, 512 if width <= 2560 else 256)
    last = pick is not None
    rows = pl.BlockSpec((live, tile), lambda j: (0, j))
    flat = [h for chunk in hidden for h in chunk]
    operands = [*flat, down_weight, *after]
    in_specs = [pl.BlockSpec(h.shape, lambda j: (0, 0)) for h in flat]
    in_specs.append(pl.BlockSpec((pl.Element(width), pl.Element(tile)), lambda j: (start, j * tile)))
    in_specs += [pl.BlockSpec(memory_space=pl.ANY)] * len(after)
    if total is not None:
        operands.append(total)
        in_specs.append(rows)
    if last:
        operands.append(pick)
        in_specs.append(pl.BlockSpec(pick.shape, lambda j: (0, 0)))
        out_shape = [jax.ShapeDtypeStruct((n, out_width), BF16) for n in out_rows]
        out_specs = [pl.BlockSpec((n, tile), lambda j: (0, j)) for n in out_rows]
    else:
        out_shape, out_specs = jax.ShapeDtypeStruct((live, out_width), F32), rows
    return pl.pallas_call(
        functools.partial(down_kernel, [len(c) for c in hidden], len(after), total is None, last),
        out_shape=out_shape,
        grid=(out_width // tile,),
        in_specs=in_specs,
        out_specs=out_specs,
        scratch_shapes=[pltpu.VMEM((live, width), BF16)],
        compiler_params=pltpu.CompilerParams(vmem_limit_bytes=40 * MIB),
        cost_estimate=pl.CostEstimate(flops=0, bytes_accessed=0, transcendentals=0),
        name="down",
    )(*operands)


def column_chunks(cols, tile):
    tiles = cols // tile
    shares = (4, 5, 4)
    edges = [round(tiles * sum(shares[:i]) / sum(shares)) for i in range(len(shares) + 1)]
    return [(a * tile, (b - a) * tile) for a, b in zip(edges, edges[1:]) if b > a]


def local(n_gx, n_gy, tokens, gate_weight, up_weight, down_weight, lengths):
    nx = n_gy // 2
    tok_dev = tokens.shape[0]
    live = 3 * tok_dev * n_gx // 4
    cols = gate_weight.shape[1]
    tile = 512 if cols % 512 == 0 else 128
    chunks = column_chunks(cols, tile)
    n = len(chunks)
    line = n_gx == 4
    part = tok_dev // 2

    def over_z(block, k, among=range(n_gx)):
        return lax.ppermute(block, "gx", [(z, z ^ k) for z in among])

    def over_core(block):
        return lax.ppermute(block, "gy", [(i, i ^ 1) for i in range(n_gy)])

    def over_x(block, k):
        return lax.ppermute(block, "gy", [(i, (i + 2 * k) % n_gy) for i in range(n_gy)])

    pick_in, pick_out, held = picks(lengths, tokens, n_gx, nx, live)
    if line:
        two = [over_z(tokens[:part], 2), over_z(tokens[part:], 2)]
        one = over_z(tokens, 1)
        middle = over_z(tokens, 3, (1, 2))
        ends = [over_z(piece, 1, (1, 2)) for piece in two]
        blocks = [[[held]], [[one]], [two], [[middle], ends]]
    else:
        blocks = [[[held]]] + [[[over_z(tokens, k)]] for k in range(1, n_gx)]
    tok = compact(pick_in, blocks)

    send, keep = gate_up(tok, gate_weight, up_weight, [], *chunks[0], tile)
    hidden, fars, total = [], [], None

    def pieces(own, far):
        h = [own] + far
        return h + [over_core(a) for a in h]

    for j in range(n):
        mine, blocks, _ = join(keep, over_core(send), [], [], nx)
        got = [over_x(b, k + 1) for k, b in enumerate(blocks)]
        handed, after = [], fars[-1] if fars else []
        if j + 1 < n:
            send, keep = gate_up(tok, gate_weight, up_weight, blocks, *chunks[j + 1], tile)
            handed = [send]
        elif n > 1:
            total = down(hidden, down_weight, None, None, None, list(blocks), chunks[0][0])
            after = [total]
        own, handed = activate(mine, got, handed, after)
        if handed:
            send = handed[0]
        far = [over_x(own, -k) for k in range(1, nx)]
        fars.append(far)
        hidden.append(pieces(own, far))
    out_rows = [tok_dev, part, part, tok_dev, tok_dev] if line else [tok_dev] * n_gx
    spread = down(hidden[-1:], down_weight, total, pick_out, out_rows, [], chunks[-1][0])

    if line:
        own, low, high, two, three = spread
        ends = over_z(three, 1, (0, 3))
        middle = over_z(three, 3, (1, 2))
        two, near = relay(two, ends, [low, high], middle)
        far = over_z(two, 2)
        near = [over_z(a, 1) for a in near]
        parts = [own, jnp.concatenate(near, axis=0), far, middle]
    else:
        parts = [spread[0]] + [over_z(spread[k], k) for k in range(1, n_gx)]
    return sum(p.astype(F32) for p in parts).astype(BF16)


def solution(mesh):
    placed = (P(("group", "gx"), "gy"), P("gy", "gx"), P("gy", "gx"), P("gx", "gy"), P("group"))
    return jax.shard_map(
        functools.partial(local, mesh.shape["gx"], mesh.shape["gy"]),
        mesh=mesh, in_specs=placed, out_specs=P(("group", "gx"), "gy"), check_vma=False,
    )
```

```python
import functools

import jax
import jax.numpy as jnp
from jax import lax
from jax.experimental import pallas as pl
from jax.experimental.pallas import tpu as pltpu
from jax.sharding import PartitionSpec as P

MIB = 1 << 20
BF16, F32 = jnp.bfloat16, jnp.float32


def row_sources(lengths_ref, rows, n_gx, tok_dev):
    start = jnp.int32(0)
    slot = rows
    for g in range(n_gx):
        slot = jnp.where(rows >= start, rows - start + g * tok_dev, slot)
        start = start + lengths_ref[g]
    return slot


def local_rows(shape, dim, quarter, nx):
    gy = lax.axis_index("gy")
    x, core = gy // 2, gy % 2
    j = lax.broadcasted_iota(jnp.int32, shape, dim)
    rows = jnp.zeros(shape, jnp.int32)
    for kc in range(2):
        for kx in range(nx):
            first = (kc * nx + kx) * quarter
            owner = lax.rem(x + kx, nx) * 2 + (1 - core if kc else core)
            rows = jnp.where(j >= first, owner * quarter + j - first, rows)
    return rows


def prepare_kernel(n_gx, nx, lengths_ref, tok_ref, gate_ref, up_ref, in_ref, out_ref, held_ref, gate_out, up_out, sems):
    fetched = pl.ds(0, gate_out.shape[1])
    copies = [
        pltpu.make_async_copy(src.at[:, fetched], dst, sems.at[i])
        for i, (src, dst) in enumerate(((gate_ref, gate_out), (up_ref, up_out)))
    ]
    for copy in copies:
        copy.start()
    tok_dev = tok_ref.shape[0]
    z = lax.axis_index("gx")
    live, slots = in_ref.shape
    quarter = live // (2 * nx)
    held_ref[...] = tok_ref[...]

    def slot_of(column):
        return (z ^ (column // tok_dev)) * tok_dev + column % tok_dev

    shape = (live, slots)
    source = row_sources(lengths_ref, local_rows(shape, 0, quarter, nx), n_gx, tok_dev)
    in_ref[...] = (source == slot_of(lax.broadcasted_iota(jnp.int32, shape, 1))).astype(F32).astype(BF16)
    shape = (slots, live)
    source = row_sources(lengths_ref, local_rows(shape, 1, quarter, nx), n_gx, tok_dev)
    out_ref[...] = (source == slot_of(lax.broadcasted_iota(jnp.int32, shape, 0))).astype(F32).astype(BF16)
    for copy in copies:
        copy.wait()


def prepare(lengths, tokens, gate_weight, up_weight, fetched, n_gx, nx, live):
    slots = n_gx * tokens.shape[0]
    held, anywhere = pl.BlockSpec(memory_space=pltpu.VMEM), pl.BlockSpec(memory_space=pl.ANY)
    weight = jax.ShapeDtypeStruct((gate_weight.shape[0], fetched), BF16)
    return pl.pallas_call(
        functools.partial(prepare_kernel, n_gx, nx),
        out_shape=[
            jax.ShapeDtypeStruct((live, slots), BF16),
            jax.ShapeDtypeStruct((slots, live), BF16),
            jax.ShapeDtypeStruct(tokens.shape, tokens.dtype),
            weight,
            weight,
        ],
        in_specs=[pl.BlockSpec(memory_space=pltpu.SMEM), held, anywhere, anywhere],
        out_specs=[held] * 5,
        scratch_shapes=[pltpu.SemaphoreType.DMA((2,))],
        cost_estimate=pl.CostEstimate(flops=0, bytes_accessed=0, transcendentals=0),
        compiler_params=pltpu.CompilerParams(vmem_limit_bytes=8 * MIB),
        name="prepare",
    )(lengths, tokens, gate_weight, up_weight)


def follow(handed, after):
    anywhere = pl.BlockSpec(memory_space=pl.ANY)
    return pl.pallas_call(
        lambda *refs: None,
        out_shape=jax.ShapeDtypeStruct(handed.shape, handed.dtype),
        in_specs=[anywhere] * (1 + len(after)),
        out_specs=anywhere,
        input_output_aliases={0: 0},
        compiler_params=pltpu.CompilerParams(vmem_limit_bytes=8 * MIB),
        cost_estimate=pl.CostEstimate(flops=0, bytes_accessed=0, transcendentals=0),
        name="follow",
    )(handed, *after)


def compact_kernel(groups, pick_ref, *refs):
    refs = list(refs)
    out_ref = refs.pop()

    def rows_of(n):
        return jnp.concatenate([refs.pop(0)[...] for _ in range(n)], axis=0)

    blocks = []
    for group in groups:
        block = rows_of(group[0])
        for n in group[1:]:
            block = block + rows_of(n)
        blocks.append(block)
    rows = jnp.concatenate(blocks, axis=0)
    out_ref[...] = jnp.dot(pick_ref[...], rows, preferred_element_type=F32).astype(BF16)


def compact(pick, blocks):
    flat = [piece for group in blocks for pieces in group for piece in pieces]
    return pl.pallas_call(
        functools.partial(compact_kernel, [[len(pieces) for pieces in group] for group in blocks]),
        out_shape=jax.ShapeDtypeStruct((pick.shape[0], flat[0].shape[1]), BF16),
        compiler_params=pltpu.CompilerParams(vmem_limit_bytes=8 * MIB),
        cost_estimate=pl.CostEstimate(
            flops=2 * pick.size * flat[0].shape[1], bytes_accessed=2 * pick.size, transcendentals=0
        ),
        name="compact",
    )(pick, *flat)


def gate_up_kernel(tok_ref, gate_ref, up_ref, *refs):
    send_ref, keep_ref = refs[-2:]
    half = keep_ref.shape[1]
    rows = tok_ref[...]
    for i, w_ref in enumerate((gate_ref, up_ref)):
        part = jnp.dot(rows, w_ref[...], preferred_element_type=F32)
        keep_ref[i] = part[:half]
        send_ref[i] = part[half:].astype(BF16)


def gate_up(tok, gate_weight, up_weight, after, start, width, tile):
    live, depth = tok.shape
    half = live // 2
    weight = pl.BlockSpec((depth, tile), lambda j: (0, start // tile + j))
    out = pl.BlockSpec((2, half, tile), lambda j: (0, 0, j))
    return pl.pallas_call(
        gate_up_kernel,
        out_shape=[jax.ShapeDtypeStruct((2, half, width), BF16), jax.ShapeDtypeStruct((2, half, width), F32)],
        grid=(width // tile,),
        in_specs=[pl.BlockSpec((live, depth), lambda j: (0, 0)), weight, weight]
        + [pl.BlockSpec(memory_space=pl.ANY)] * len(after),
        out_specs=[out, out],
        compiler_params=pltpu.CompilerParams(vmem_limit_bytes=40 * MIB),
        cost_estimate=pl.CostEstimate(
            flops=0, bytes_accessed=0, transcendentals=0
        ),
        name="gate_up",
    )(tok, gate_weight, up_weight, *after)


def gate_up_held_kernel(start, width, tile, tok_ref, gate_ref, up_ref, send_ref, keep_ref):
    half = keep_ref.shape[1]
    rows = tok_ref[...]
    for j in range(0, width, tile):
        for i, w_ref in enumerate((gate_ref, up_ref)):
            part = jnp.dot(rows, w_ref[:, start + j:start + j + tile], preferred_element_type=F32)
            keep_ref[i, :, j:j + tile] = part[:half]
            send_ref[i, :, j:j + tile] = part[half:].astype(BF16)


def gate_up_held(tok, gate_held, up_held, start, width, tile):
    half = tok.shape[0] // 2
    held = pl.BlockSpec(memory_space=pltpu.VMEM)
    return pl.pallas_call(
        functools.partial(gate_up_held_kernel, start, width, tile),
        out_shape=[jax.ShapeDtypeStruct((2, half, width), BF16), jax.ShapeDtypeStruct((2, half, width), F32)],
        in_specs=[held] * 3,
        out_specs=[held] * 2,
        compiler_params=pltpu.CompilerParams(vmem_limit_bytes=12 * MIB),
        cost_estimate=pl.CostEstimate(flops=0, bytes_accessed=0, transcendentals=0),
        name="gate_up_held",
    )(tok, gate_held, up_held)


def join_kernel(n_handed, n_after, nx, keep_ref, got_ref, *refs):
    out_refs = refs[n_handed + n_after:][:nx]
    quarter = out_refs[0].shape[1]
    for k, out_ref in enumerate(out_refs):
        rows = pl.ds(k * quarter, quarter)
        out_ref[...] = (keep_ref[:, rows] + got_ref[:, rows].astype(F32)).astype(out_ref.dtype)


def join(keep, got, handed, after, nx):
    two, half, width = keep.shape
    shape = (two, half // nx, width)
    held, anywhere = pl.BlockSpec(memory_space=pltpu.VMEM), pl.BlockSpec(memory_space=pl.ANY)
    out = pl.pallas_call(
        functools.partial(join_kernel, len(handed), len(after), nx),
        out_shape=[jax.ShapeDtypeStruct(shape, BF16 if k else F32) for k in range(nx)]
        + [jax.ShapeDtypeStruct(a.shape, a.dtype) for a in handed],
        in_specs=[held, held] + [anywhere] * (len(handed) + len(after)),
        out_specs=[held] * nx + [anywhere] * len(handed),
        input_output_aliases={2 + i: nx + i for i in range(len(handed))},
        compiler_params=pltpu.CompilerParams(vmem_limit_bytes=8 * MIB),
        cost_estimate=pl.CostEstimate(flops=0, bytes_accessed=0, transcendentals=0),
        name="join",
    )(keep, got, *handed, *after)
    return out[0], out[1:nx], out[nx:]


def activate_kernel(n_got, n_unread, mine_ref, *refs):
    both = mine_ref[...]
    for got_ref in refs[:n_got]:
        both = both + got_ref[...].astype(F32)
    gate, up = both[0], both[1]
    refs[n_got + n_unread][...] = (gate / (1.0 + jnp.exp(-gate)) * up).astype(BF16)


def activate(mine, got, handed, after):
    held, anywhere = pl.BlockSpec(memory_space=pltpu.VMEM), pl.BlockSpec(memory_space=pl.ANY)
    out = pl.pallas_call(
        functools.partial(activate_kernel, len(got), len(handed) + len(after)),
        out_shape=[jax.ShapeDtypeStruct(mine.shape[1:], BF16)]
        + [jax.ShapeDtypeStruct(a.shape, a.dtype) for a in handed],
        in_specs=[held] * (1 + len(got)) + [anywhere] * (len(handed) + len(after)),
        out_specs=[held] + [anywhere] * len(handed),
        input_output_aliases={1 + len(got) + i: 1 + i for i in range(len(handed))},
        compiler_params=pltpu.CompilerParams(vmem_limit_bytes=8 * MIB),
        cost_estimate=pl.CostEstimate(flops=0, bytes_accessed=0, transcendentals=0),
        name="activate",
    )(mine, *got, *handed, *after)
    return out[0], out[1:]


def relay_kernel(own_ref, got_ref, *refs):
    out_ref = refs[len(refs) // 2]
    out_ref[...] = (own_ref[...].astype(F32) + got_ref[...].astype(F32)).astype(BF16)


def relay(own, got, handed, after):
    held, anywhere = pl.BlockSpec(memory_space=pltpu.VMEM), pl.BlockSpec(memory_space=pl.ANY)
    out = pl.pallas_call(
        relay_kernel,
        out_shape=[jax.ShapeDtypeStruct(a.shape, a.dtype) for a in (own, *handed)],
        in_specs=[held, held] + [anywhere] * (1 + len(handed)),
        out_specs=[held] + [anywhere] * len(handed),
        input_output_aliases={2 + i: 1 + i for i in range(len(handed))},
        compiler_params=pltpu.CompilerParams(vmem_limit_bytes=8 * MIB),
        cost_estimate=pl.CostEstimate(flops=0, bytes_accessed=0, transcendentals=0),
        name="relay",
    )(own, got, *handed, after)
    return out[0], out[1:]


def down_kernel(pieces, n_after, first, last, *refs):
    refs, hidden = list(refs[:-1]), refs[-1]
    h_refs = [[refs.pop(0) for _ in range(n)] for n in pieces]
    w_ref, refs = refs[0], refs[1 + n_after:]

    @pl.when(pl.program_id(0) == 0)
    def _():
        column = 0
        for chunk in h_refs:
            row = 0
            for r in chunk:
                n, width = r.shape
                hidden[row:row + n, column:column + width] = r[...]
                row += n
            column += width

    total = jnp.dot(hidden[...], w_ref[...], preferred_element_type=F32)
    if not first:
        total += refs[0][...]
        refs = refs[1:]
    if not last:
        refs[0][...] = total
        return
    pick_ref, outs = refs[0], refs[1:]
    spread = jnp.dot(pick_ref[...], total.astype(BF16), preferred_element_type=F32).astype(BF16)
    row = 0
    for out_ref in outs:
        n = out_ref.shape[0]
        out_ref[...] = spread[row:row + n]
        row += n


def down(hidden, down_weight, total, pick, out_rows, after, start):
    live = sum(h.shape[0] for h in hidden[0])
    width = sum(chunk[0].shape[1] for chunk in hidden)
    out_width = down_weight.shape[1]
    tile = min(out_width, 512 if width <= 2560 else 256)
    last = pick is not None
    rows = pl.BlockSpec((live, tile), lambda j: (0, j))
    flat = [h for chunk in hidden for h in chunk]
    operands = [*flat, down_weight, *after]
    in_specs = [pl.BlockSpec(h.shape, lambda j: (0, 0)) for h in flat]
    in_specs.append(pl.BlockSpec((pl.Element(width), pl.Element(tile)), lambda j: (start, j * tile)))
    in_specs += [pl.BlockSpec(memory_space=pl.ANY)] * len(after)
    if total is not None:
        operands.append(total)
        in_specs.append(rows)
    if last:
        operands.append(pick)
        in_specs.append(pl.BlockSpec(pick.shape, lambda j: (0, 0)))
        out_shape = [jax.ShapeDtypeStruct((n, out_width), BF16) for n in out_rows]
        out_specs = [pl.BlockSpec((n, tile), lambda j: (0, j)) for n in out_rows]
    else:
        out_shape, out_specs = jax.ShapeDtypeStruct((live, out_width), F32), rows
    return pl.pallas_call(
        functools.partial(down_kernel, [len(c) for c in hidden], len(after), total is None, last),
        out_shape=out_shape,
        grid=(out_width // tile,),
        in_specs=in_specs,
        out_specs=out_specs,
        scratch_shapes=[pltpu.VMEM((live, width), BF16)],
        compiler_params=pltpu.CompilerParams(vmem_limit_bytes=40 * MIB),
        cost_estimate=pl.CostEstimate(flops=0, bytes_accessed=0, transcendentals=0),
        name="down",
    )(*operands)


def column_chunks(cols, tile):
    tiles = cols // tile
    shares = (3, 3, 4, 3)
    edges = [round(tiles * sum(shares[:i]) / sum(shares)) for i in range(len(shares) + 1)]
    return [(a * tile, (b - a) * tile) for a, b in zip(edges, edges[1:]) if b > a]


def local(n_gx, n_gy, tokens, gate_weight, up_weight, down_weight, lengths):
    nx = n_gy // 2
    tok_dev = tokens.shape[0]
    live = 3 * tok_dev * n_gx // 4
    cols = gate_weight.shape[1]
    tile = 512 if cols % 512 == 0 else 128
    chunks = column_chunks(cols, tile)
    n = len(chunks)
    line = n_gx == 4
    part = tok_dev // 2

    def over_z(block, k, among=range(n_gx)):
        return lax.ppermute(block, "gx", [(z, z ^ k) for z in among])

    def over_core(block):
        return lax.ppermute(block, "gy", [(i, i ^ 1) for i in range(n_gy)])

    def over_x(block, k):
        return lax.ppermute(block, "gy", [(i, (i + 2 * k) % n_gy) for i in range(n_gy)])

    first = sum(width for _, width in chunks[:2])
    pick_in, pick_out, held, gate_held, up_held = prepare(
        lengths, tokens, gate_weight, up_weight, first, n_gx, nx, live
    )
    if line:
        two = [over_z(tokens[:part], 2), over_z(tokens[part:], 2)]
        one = over_z(tokens, 1)
        middle = over_z(tokens, 3, (1, 2))
        two = [follow(piece, [pick_in]) for piece in two]
        ends = [over_z(piece, 1, (1, 2)) for piece in two]
        blocks = [[[held]], [[one]], [two], [[middle], ends]]
    else:
        blocks = [[[held]]] + [[[over_z(tokens, k)]] for k in range(1, n_gx)]
    tok = compact(pick_in, blocks)

    made = [gate_up_held(tok, gate_held, up_held, *chunk, tile) for chunk in chunks[:2]]
    sends, keeps = [list(a) for a in zip(*made)]
    mines, gots, owns, fars, hidden, total = [], [], [], [], [], None

    def exchange(j, handed):
        mine, blocks, handed = join(keeps[j], over_core(sends[j]), handed, [], nx)
        mines.append(mine)
        gots.append([over_x(b, k + 1) for k, b in enumerate(blocks)])
        return list(blocks), handed

    def finish(j, handed, after):
        own, handed = activate(mines[j], gots[j], handed, after)
        far = [over_x(own, -k) for k in range(1, nx)]
        owns.append(own)
        fars.append(far)
        h = [own] + far
        hidden.append(h + [over_core(a) for a in h])
        return handed

    ready, sends[1:2] = exchange(0, sends[1:2])
    ready += exchange(1, [])[0]
    for j in range(2, n):
        send, keep = gate_up(tok, gate_weight, up_weight, ready, *chunks[j], tile)
        keeps.append(keep)
        sends += finish(j - 2, [send], [])
        ready = exchange(j, [])[0]
    finish(n - 2, [], ready)
    total = down(hidden[:n - 2], down_weight, None, None, None, [owns[n - 2]], chunks[0][0])
    finish(n - 1, [], [total])
    total = down(hidden[n - 2:n - 1], down_weight, total, None, None, [], chunks[n - 2][0])
    out_rows = [tok_dev, part, part, tok_dev, tok_dev] if line else [tok_dev] * n_gx
    spread = down(hidden[-1:], down_weight, total, pick_out, out_rows, [], chunks[-1][0])

    if line:
        own, low, high, two, three = spread
        ends = over_z(three, 1, (0, 3))
        middle = over_z(three, 3, (1, 2))
        two, near = relay(two, ends, [low, high], middle)
        far = over_z(two, 2)
        near = [over_z(a, 1) for a in near]
        parts = [own, jnp.concatenate(near, axis=0), far, middle]
    else:
        parts = [spread[0]] + [over_z(spread[k], k) for k in range(1, n_gx)]
    return sum(p.astype(F32) for p in parts).astype(BF16)


def solution(mesh):
    placed = (P(("group", "gx"), "gy"), P("gy", "gx"), P("gy", "gx"), P("gx", "gy"), P("group"))
    return jax.shard_map(
        functools.partial(local, mesh.shape["gx"], mesh.shape["gy"]),
        mesh=mesh, in_specs=placed, out_specs=P(("group", "gx"), "gy"), check_vma=False,
    )
```

```python
import functools

import jax
import jax.numpy as jnp
from jax import lax
from jax.experimental import pallas as pl
from jax.experimental.pallas import tpu as pltpu
from jax.sharding import PartitionSpec as P

MIB = 1 << 20
BF16, F32 = jnp.bfloat16, jnp.float32


def row_sources(lengths_ref, rows, n_gx, tok_dev):
    start = jnp.int32(0)
    slot = rows
    for g in range(n_gx):
        slot = jnp.where(rows >= start, rows - start + g * tok_dev, slot)
        start = start + lengths_ref[g]
    return slot


def local_rows(shape, dim, quarter, nx):
    gy = lax.axis_index("gy")
    x, core = gy // 2, gy % 2
    j = lax.broadcasted_iota(jnp.int32, shape, dim)
    rows = jnp.zeros(shape, jnp.int32)
    for kc in range(2):
        for kx in range(nx):
            first = (kc * nx + kx) * quarter
            owner = lax.rem(x + kx, nx) * 2 + (1 - core if kc else core)
            rows = jnp.where(j >= first, owner * quarter + j - first, rows)
    return rows


def prepare_kernel(n_gx, nx, lengths_ref, tok_ref, gate_ref, up_ref, in_ref, out_ref, held_ref, gate_out, up_out, sems):
    fetched = pl.ds(0, gate_out.shape[1])
    copies = [
        pltpu.make_async_copy(src.at[:, fetched], dst, sems.at[i])
        for i, (src, dst) in enumerate(((gate_ref, gate_out), (up_ref, up_out)))
    ]
    for copy in copies:
        copy.start()
    tok_dev = tok_ref.shape[0]
    z = lax.axis_index("gx")
    live, slots = in_ref.shape
    quarter = live // (2 * nx)
    held_ref[...] = tok_ref[...]

    def slot_of(column):
        return (z ^ (column // tok_dev)) * tok_dev + column % tok_dev

    shape = (live, slots)
    source = row_sources(lengths_ref, local_rows(shape, 0, quarter, nx), n_gx, tok_dev)
    in_ref[...] = (source == slot_of(lax.broadcasted_iota(jnp.int32, shape, 1))).astype(F32).astype(BF16)
    shape = (slots, live)
    source = row_sources(lengths_ref, local_rows(shape, 1, quarter, nx), n_gx, tok_dev)
    out_ref[...] = (source == slot_of(lax.broadcasted_iota(jnp.int32, shape, 0))).astype(F32).astype(BF16)
    for copy in copies:
        copy.wait()


def prepare(lengths, tokens, gate_weight, up_weight, fetched, n_gx, nx, live):
    slots = n_gx * tokens.shape[0]
    held, anywhere = pl.BlockSpec(memory_space=pltpu.VMEM), pl.BlockSpec(memory_space=pl.ANY)
    weight = jax.ShapeDtypeStruct((gate_weight.shape[0], fetched), BF16)
    return pl.pallas_call(
        functools.partial(prepare_kernel, n_gx, nx),
        out_shape=[
            jax.ShapeDtypeStruct((live, slots), BF16),
            jax.ShapeDtypeStruct((slots, live), BF16),
            jax.ShapeDtypeStruct(tokens.shape, tokens.dtype),
            weight,
            weight,
        ],
        in_specs=[pl.BlockSpec(memory_space=pltpu.SMEM), held, anywhere, anywhere],
        out_specs=[held] * 5,
        scratch_shapes=[pltpu.SemaphoreType.DMA((2,))],
        cost_estimate=pl.CostEstimate(flops=0, bytes_accessed=0, transcendentals=0),
        compiler_params=pltpu.CompilerParams(vmem_limit_bytes=8 * MIB),
        name="prepare",
    )(lengths, tokens, gate_weight, up_weight)


def compact_kernel(groups, pick_ref, *refs):
    refs = list(refs)
    out_ref = refs.pop()

    def rows_of(n):
        return jnp.concatenate([refs.pop(0)[...] for _ in range(n)], axis=0)

    blocks = []
    for group in groups:
        block = rows_of(group[0])
        for n in group[1:]:
            block = block + rows_of(n)
        blocks.append(block)
    rows = jnp.concatenate(blocks, axis=0)
    out_ref[...] = jnp.dot(pick_ref[...], rows, preferred_element_type=F32).astype(BF16)


def compact(pick, blocks):
    flat = [piece for group in blocks for pieces in group for piece in pieces]
    return pl.pallas_call(
        functools.partial(compact_kernel, [[len(pieces) for pieces in group] for group in blocks]),
        out_shape=jax.ShapeDtypeStruct((pick.shape[0], flat[0].shape[1]), BF16),
        compiler_params=pltpu.CompilerParams(vmem_limit_bytes=8 * MIB),
        cost_estimate=pl.CostEstimate(
            flops=2 * pick.size * flat[0].shape[1], bytes_accessed=2 * pick.size, transcendentals=0
        ),
        name="compact",
    )(pick, *flat)


def gate_up_kernel(tok_ref, gate_ref, up_ref, *refs):
    send_ref, keep_ref = refs[-2:]
    half = keep_ref.shape[1]
    rows = tok_ref[...]
    for i, w_ref in enumerate((gate_ref, up_ref)):
        part = jnp.dot(rows, w_ref[...], preferred_element_type=F32)
        keep_ref[i] = part[:half]
        send_ref[i] = part[half:].astype(BF16)


def gate_up(tok, gate_weight, up_weight, after, start, width, tile):
    live, depth = tok.shape
    half = live // 2
    weight = pl.BlockSpec((depth, tile), lambda j: (0, start // tile + j))
    out = pl.BlockSpec((2, half, tile), lambda j: (0, 0, j))
    return pl.pallas_call(
        gate_up_kernel,
        out_shape=[jax.ShapeDtypeStruct((2, half, width), BF16), jax.ShapeDtypeStruct((2, half, width), F32)],
        grid=(width // tile,),
        in_specs=[pl.BlockSpec((live, depth), lambda j: (0, 0)), weight, weight]
        + [pl.BlockSpec(memory_space=pl.ANY)] * len(after),
        out_specs=[out, out],
        compiler_params=pltpu.CompilerParams(vmem_limit_bytes=40 * MIB),
        cost_estimate=pl.CostEstimate(
            flops=0, bytes_accessed=0, transcendentals=0
        ),
        name="gate_up",
    )(tok, gate_weight, up_weight, *after)


def gate_up_held_kernel(start, width, tile, tok_ref, gate_ref, up_ref, send_ref, keep_ref):
    half = keep_ref.shape[1]
    rows = tok_ref[...]
    for j in range(0, width, tile):
        for i, w_ref in enumerate((gate_ref, up_ref)):
            part = jnp.dot(rows, w_ref[:, start + j:start + j + tile], preferred_element_type=F32)
            keep_ref[i, :, j:j + tile] = part[:half]
            send_ref[i, :, j:j + tile] = part[half:].astype(BF16)


def gate_up_held(tok, gate_held, up_held, start, width, tile):
    half = tok.shape[0] // 2
    held = pl.BlockSpec(memory_space=pltpu.VMEM)
    return pl.pallas_call(
        functools.partial(gate_up_held_kernel, start, width, tile),
        out_shape=[jax.ShapeDtypeStruct((2, half, width), BF16), jax.ShapeDtypeStruct((2, half, width), F32)],
        in_specs=[held] * 3,
        out_specs=[held] * 2,
        compiler_params=pltpu.CompilerParams(vmem_limit_bytes=12 * MIB),
        cost_estimate=pl.CostEstimate(flops=0, bytes_accessed=0, transcendentals=0),
        name="gate_up_held",
    )(tok, gate_held, up_held)


def join_kernel(n_handed, n_after, nx, keep_ref, got_ref, *refs):
    out_refs = refs[n_handed + n_after:][:nx]
    quarter = out_refs[0].shape[1]
    for k, out_ref in enumerate(out_refs):
        rows = pl.ds(k * quarter, quarter)
        out_ref[...] = (keep_ref[:, rows] + got_ref[:, rows].astype(F32)).astype(out_ref.dtype)


def join(keep, got, handed, after, nx):
    two, half, width = keep.shape
    shape = (two, half // nx, width)
    held, anywhere = pl.BlockSpec(memory_space=pltpu.VMEM), pl.BlockSpec(memory_space=pl.ANY)
    out = pl.pallas_call(
        functools.partial(join_kernel, len(handed), len(after), nx),
        out_shape=[jax.ShapeDtypeStruct(shape, BF16 if k else F32) for k in range(nx)]
        + [jax.ShapeDtypeStruct(a.shape, a.dtype) for a in handed],
        in_specs=[held, held] + [anywhere] * (len(handed) + len(after)),
        out_specs=[held] * nx + [anywhere] * len(handed),
        input_output_aliases={2 + i: nx + i for i in range(len(handed))},
        compiler_params=pltpu.CompilerParams(vmem_limit_bytes=8 * MIB),
        cost_estimate=pl.CostEstimate(flops=0, bytes_accessed=0, transcendentals=0),
        name="join",
    )(keep, got, *handed, *after)
    return out[0], out[1:nx], out[nx:]


def activate_kernel(n_got, n_chunks, n_unread, *refs):
    own_ref = refs[n_chunks * (1 + n_got) + n_unread]
    column = 0
    for c in range(n_chunks):
        mine_ref, *got_refs = refs[c * (1 + n_got):(c + 1) * (1 + n_got)]
        both = mine_ref[...]
        for got_ref in got_refs:
            both = both + got_ref[...].astype(F32)
        gate, up = both[0], both[1]
        own_ref[:, column:column + gate.shape[1]] = (gate / (1.0 + jnp.exp(-gate)) * up).astype(BF16)
        column += gate.shape[1]


def activate(sums, handed, after):
    held, anywhere = pl.BlockSpec(memory_space=pltpu.VMEM), pl.BlockSpec(memory_space=pl.ANY)
    flat = [a for chunk in sums for a in chunk]
    width = sum(chunk[0].shape[2] for chunk in sums)
    out = pl.pallas_call(
        functools.partial(activate_kernel, len(sums[0]) - 1, len(sums), len(handed) + len(after)),
        out_shape=[jax.ShapeDtypeStruct((flat[0].shape[1], width), BF16)]
        + [jax.ShapeDtypeStruct(a.shape, a.dtype) for a in handed],
        in_specs=[held] * len(flat) + [anywhere] * (len(handed) + len(after)),
        out_specs=[held] + [anywhere] * len(handed),
        input_output_aliases={len(flat) + i: 1 + i for i in range(len(handed))},
        compiler_params=pltpu.CompilerParams(vmem_limit_bytes=8 * MIB),
        cost_estimate=pl.CostEstimate(flops=0, bytes_accessed=0, transcendentals=0),
        name="activate",
    )(*flat, *handed, *after)
    return out[0], out[1:]


def relay_kernel(own_ref, got_ref, *refs):
    out_ref = refs[len(refs) // 2]
    out_ref[...] = (own_ref[...].astype(F32) + got_ref[...].astype(F32)).astype(BF16)


def relay(own, got, handed, after):
    held, anywhere = pl.BlockSpec(memory_space=pltpu.VMEM), pl.BlockSpec(memory_space=pl.ANY)
    out = pl.pallas_call(
        relay_kernel,
        out_shape=[jax.ShapeDtypeStruct(a.shape, a.dtype) for a in (own, *handed)],
        in_specs=[held, held] + [anywhere] * (1 + len(handed)),
        out_specs=[held] + [anywhere] * len(handed),
        input_output_aliases={2 + i: 1 + i for i in range(len(handed))},
        compiler_params=pltpu.CompilerParams(vmem_limit_bytes=8 * MIB),
        cost_estimate=pl.CostEstimate(flops=0, bytes_accessed=0, transcendentals=0),
        name="relay",
    )(own, got, *handed, after)
    return out[0], out[1:]


def put_rows(h_refs, hidden):
    row = 0
    for r in h_refs:
        hidden[row:row + r.shape[0]] = r[...]
        row += r.shape[0]


def down_kernel(n_h, *refs):
    h_refs, w_ref, out_ref, hidden = refs[:n_h], refs[n_h], refs[-2], refs[-1]

    @pl.when(pl.program_id(0) == 0)
    def _():
        put_rows(h_refs, hidden)

    out_ref[...] = jnp.dot(hidden[...], w_ref[...], preferred_element_type=F32)


def down(hidden, down_weight, after, start):
    live = sum(h.shape[0] for h in hidden)
    width = hidden[0].shape[1]
    out_width = down_weight.shape[1]
    tile = min(out_width, 512)
    weight = pl.BlockSpec((pl.Element(width), pl.Element(tile)), lambda j: (start, j * tile))
    return pl.pallas_call(
        functools.partial(down_kernel, len(hidden)),
        out_shape=jax.ShapeDtypeStruct((live, out_width), F32),
        grid=(out_width // tile,),
        in_specs=[pl.BlockSpec(h.shape, lambda j: (0, 0)) for h in hidden]
        + [weight]
        + [pl.BlockSpec(memory_space=pl.ANY)] * len(after),
        out_specs=pl.BlockSpec((live, tile), lambda j: (0, j)),
        scratch_shapes=[pltpu.VMEM((live, width), BF16)],
        compiler_params=pltpu.CompilerParams(vmem_limit_bytes=28 * MIB),
        cost_estimate=pl.CostEstimate(flops=0, bytes_accessed=0, transcendentals=0),
        name="down",
    )(*hidden, down_weight, *after)


def fetch_kernel(starts, src_ref, *refs):
    outs, sems = refs[-1 - len(starts):-1], refs[-1]
    copies = [
        pltpu.make_async_copy(src_ref.at[pl.ds(start, out.shape[0])], out, sems.at[i])
        for i, (start, out) in enumerate(zip(starts, outs))
    ]
    for copy in copies:
        copy.start()
    for copy in copies:
        copy.wait()


def fetch(down_weight, chunks, after):
    held, anywhere = pl.BlockSpec(memory_space=pltpu.VMEM), pl.BlockSpec(memory_space=pl.ANY)
    return pl.pallas_call(
        functools.partial(fetch_kernel, [start for start, _ in chunks]),
        out_shape=[jax.ShapeDtypeStruct((width, down_weight.shape[1]), BF16) for _, width in chunks],
        in_specs=[anywhere] * (1 + len(after)),
        out_specs=[held] * len(chunks),
        scratch_shapes=[pltpu.SemaphoreType.DMA((len(chunks),))],
        compiler_params=pltpu.CompilerParams(vmem_limit_bytes=28 * MIB),
        cost_estimate=pl.CostEstimate(flops=0, bytes_accessed=0, transcendentals=0),
        name="fetch",
    )(down_weight, *after)


def down_held_kernel(n_h, last, tile, *refs):
    h_refs, w_ref, total_ref, outs, hidden = refs[:n_h], refs[n_h], refs[n_h + 1], refs[n_h + 2:-1], refs[-1]
    put_rows(h_refs, hidden)
    for j in range(0, total_ref.shape[1], tile):
        total = jnp.dot(hidden[...], w_ref[:, j:j + tile], preferred_element_type=F32) + total_ref[:, j:j + tile]
        if not last:
            outs[0][:, j:j + tile] = total
            continue
        pick_ref = outs[0]
        spread = jnp.dot(pick_ref[...], total.astype(BF16), preferred_element_type=F32).astype(BF16)
        row = 0
        for out_ref in outs[1:]:
            n = out_ref.shape[0]
            out_ref[:, j:j + tile] = spread[row:row + n]
            row += n


def down_held(hidden, weight_held, total, pick, out_rows):
    live, out_width = total.shape
    held = pl.BlockSpec(memory_space=pltpu.VMEM)
    last = pick is not None
    if last:
        out_shape = [jax.ShapeDtypeStruct((n, out_width), BF16) for n in out_rows]
    else:
        out_shape = jax.ShapeDtypeStruct((live, out_width), F32)
    return pl.pallas_call(
        functools.partial(down_held_kernel, len(hidden), last, min(out_width, 512)),
        out_shape=out_shape,
        in_specs=[held] * (len(hidden) + (3 if last else 2)),
        out_specs=[held] * len(out_rows) if last else held,
        scratch_shapes=[pltpu.VMEM((live, hidden[0].shape[1]), BF16)],
        compiler_params=pltpu.CompilerParams(vmem_limit_bytes=12 * MIB),
        cost_estimate=pl.CostEstimate(flops=0, bytes_accessed=0, transcendentals=0),
        name="down_held",
    )(*hidden, weight_held, total, *([pick] if last else []))


def column_chunks(cols, tile):
    tiles = cols // tile
    shares = (3, 3, 4, 3)
    edges = [round(tiles * sum(shares[:i]) / sum(shares)) for i in range(len(shares) + 1)]
    return [(a * tile, (b - a) * tile) for a, b in zip(edges, edges[1:]) if b > a]


def local(n_gx, n_gy, tokens, gate_weight, up_weight, down_weight, lengths):
    nx = n_gy // 2
    tok_dev = tokens.shape[0]
    live = 3 * tok_dev * n_gx // 4
    cols = gate_weight.shape[1]
    tile = 512 if cols % 512 == 0 else 128
    chunks = column_chunks(cols, tile)
    line = n_gx == 4
    part = tok_dev // 2

    def over_z(block, k, among=range(n_gx)):
        return lax.ppermute(block, "gx", [(z, z ^ k) for z in among])

    def over_core(block):
        return lax.ppermute(block, "gy", [(i, i ^ 1) for i in range(n_gy)])

    def over_x(block, k):
        return lax.ppermute(block, "gy", [(i, (i + 2 * k) % n_gy) for i in range(n_gy)])

    first = sum(width for _, width in chunks[:2])
    pick_in, pick_out, held, gate_held, up_held = prepare(
        lengths, tokens, gate_weight, up_weight, first, n_gx, nx, live
    )
    blocks = [[[held]]] + [[[over_z(tokens, k)]] for k in range(1, n_gx)]
    tok = compact(pick_in, blocks)

    made = [gate_up_held(tok, gate_held, up_held, *chunk, tile) for chunk in chunks[:2]]
    sends, keeps = [list(a) for a in zip(*made)]
    sums = []

    def exchange(j, handed):
        mine, blocks, handed = join(keeps[j], over_core(sends[j]), handed, [], nx)
        sums.append([mine] + [over_x(b, k + 1) for k, b in enumerate(blocks)])
        return list(blocks), handed

    def finish(first, last, handed, after):
        own, handed = activate(sums[first:last], handed, after)
        h = [own] + [over_x(own, -k) for k in range(1, nx)]
        return h + [over_core(a) for a in h], handed

    ready, sends[1:2] = exchange(0, sends[1:2])
    ready += exchange(1, [])[0]
    for chunk in chunks[2:]:
        send, keep = gate_up(tok, gate_weight, up_weight, ready, *chunk, tile)
        sends.append(send)
        keeps.append(keep)
        ready = [send]
    hidden, sends[2:] = finish(0, 2, sends[2:], [])
    ready, sends[3:] = exchange(2, sends[3:])
    ready += exchange(3, [])[0]
    rows_held = fetch(down_weight, chunks[2:], ready)
    total = down(hidden, down_weight, [rows_held[0]], chunks[0][0])
    hidden, _ = finish(2, 3, [], [total])
    total = down_held(hidden, rows_held[0], total, None, None)
    hidden, _ = finish(3, 4, [], [])
    out_rows = [tok_dev, part, part, tok_dev, tok_dev] if line else [tok_dev] * n_gx
    spread = down_held(hidden, rows_held[1], total, pick_out, out_rows)

    if line:
        own, low, high, two, three = spread
        ends = over_z(three, 1, (0, 3))
        middle = over_z(three, 3, (1, 2))
        two, near = relay(two, ends, [low, high], middle)
        far = over_z(two, 2)
        near = [over_z(a, 1) for a in near]
        parts = [own, jnp.concatenate(near, axis=0), far, middle]
    else:
        parts = [spread[0]] + [over_z(spread[k], k) for k in range(1, n_gx)]
    return sum(p.astype(F32) for p in parts).astype(BF16)


def solution(mesh):
    placed = (P(("group", "gx"), "gy"), P("gy", "gx"), P("gy", "gx"), P("gx", "gy"), P("group"))
    return jax.shard_map(
        functools.partial(local, mesh.shape["gx"], mesh.shape["gy"]),
        mesh=mesh, in_specs=placed, out_specs=P(("group", "gx"), "gy"), check_vma=False,
    )
```

```python
import functools

import jax
import jax.numpy as jnp
from jax import lax
from jax.experimental import pallas as pl
from jax.experimental.pallas import tpu as pltpu
from jax.sharding import PartitionSpec as P

MIB = 1 << 20
BF16, F32 = jnp.bfloat16, jnp.float32


def row_sources(lengths_ref, rows, n_gx, tok_dev):
    start = jnp.int32(0)
    slot = rows
    for g in range(n_gx):
        slot = jnp.where(rows >= start, rows - start + g * tok_dev, slot)
        start = start + lengths_ref[g]
    return slot


def local_rows(shape, dim, quarter, nx):
    gy = lax.axis_index("gy")
    x, core = gy // 2, gy % 2
    j = lax.broadcasted_iota(jnp.int32, shape, dim)
    rows = jnp.zeros(shape, jnp.int32)
    for kc in range(2):
        for kx in range(nx):
            first = (kc * nx + kx) * quarter
            owner = lax.rem(x + kx, nx) * 2 + (1 - core if kc else core)
            rows = jnp.where(j >= first, owner * quarter + j - first, rows)
    return rows


def hold_kernel(tok_ref, out_ref):
    out_ref[...] = tok_ref[...]


def hold(tokens):
    held = pl.BlockSpec(memory_space=pltpu.VMEM)
    return pl.pallas_call(
        hold_kernel,
        out_shape=jax.ShapeDtypeStruct(tokens.shape, tokens.dtype),
        in_specs=[held],
        out_specs=held,
        cost_estimate=pl.CostEstimate(flops=0, bytes_accessed=0, transcendentals=0),
        compiler_params=pltpu.CompilerParams(vmem_limit_bytes=4 * MIB),
        name="hold",
    )(tokens)


def prepare_kernel(n_gx, nx, tok_dev, chunks, lengths_ref, gate_ref, up_ref, in_ref, out_ref, *refs):
    outs, sems = refs[:-1], refs[-1]
    copies = []
    for i, (start, width) in enumerate(chunks):
        for k, src in enumerate((gate_ref, up_ref)):
            copies.append(pltpu.make_async_copy(src.at[:, pl.ds(start, width)], outs[2 * i + k], sems.at[2 * i + k]))
    for copy in copies:
        copy.start()
    z = lax.axis_index("gx")
    live, slots = in_ref.shape
    quarter = live // (2 * nx)

    def slot_of(column):
        return (z ^ (column // tok_dev)) * tok_dev + column % tok_dev

    shape = (live, slots)
    source = row_sources(lengths_ref, local_rows(shape, 0, quarter, nx), n_gx, tok_dev)
    in_ref[...] = (source == slot_of(lax.broadcasted_iota(jnp.int32, shape, 1))).astype(F32).astype(BF16)
    shape = (slots, live)
    source = row_sources(lengths_ref, local_rows(shape, 1, quarter, nx), n_gx, tok_dev)
    out_ref[...] = (source == slot_of(lax.broadcasted_iota(jnp.int32, shape, 0))).astype(F32).astype(BF16)
    for copy in copies:
        copy.wait()


def prepare(lengths, gate_weight, up_weight, chunks, n_gx, nx, tok_dev, live):
    slots = n_gx * tok_dev
    held, anywhere = pl.BlockSpec(memory_space=pltpu.VMEM), pl.BlockSpec(memory_space=pl.ANY)
    weights = [jax.ShapeDtypeStruct((gate_weight.shape[0], width), BF16) for _, width in chunks for _ in range(2)]
    out = pl.pallas_call(
        functools.partial(prepare_kernel, n_gx, nx, tok_dev, chunks),
        out_shape=[jax.ShapeDtypeStruct((live, slots), BF16), jax.ShapeDtypeStruct((slots, live), BF16)] + weights,
        in_specs=[pl.BlockSpec(memory_space=pltpu.SMEM), anywhere, anywhere],
        out_specs=[held] * (2 + len(weights)),
        scratch_shapes=[pltpu.SemaphoreType.DMA((len(weights),))],
        cost_estimate=pl.CostEstimate(flops=0, bytes_accessed=0, transcendentals=0),
        compiler_params=pltpu.CompilerParams(vmem_limit_bytes=4 * MIB),
        name="prepare",
    )(lengths, gate_weight, up_weight)
    return out[0], out[1], [out[2 + 2 * i:4 + 2 * i] for i in range(len(chunks))]


def compact_kernel(pick_ref, *refs):
    rows = jnp.concatenate([r[...] for r in refs[:-1]], axis=0)
    refs[-1][...] = jnp.dot(pick_ref[...], rows, preferred_element_type=F32).astype(BF16)


def compact(pick, blocks):
    return pl.pallas_call(
        compact_kernel,
        out_shape=jax.ShapeDtypeStruct((pick.shape[0], blocks[0].shape[1]), BF16),
        compiler_params=pltpu.CompilerParams(vmem_limit_bytes=5 * MIB),
        cost_estimate=pl.CostEstimate(flops=0, bytes_accessed=0, transcendentals=0),
        name="compact",
    )(pick, *blocks)


def gate_up_kernel(tok_ref, gate_ref, up_ref, *refs):
    send_ref, keep_ref = refs[-2:]
    half = keep_ref.shape[1]
    rows = tok_ref[...]
    for i, w_ref in enumerate((gate_ref, up_ref)):
        part = jnp.dot(rows, w_ref[...], preferred_element_type=F32)
        keep_ref[i] = part[:half]
        send_ref[i] = part[half:].astype(BF16)


def gate_up(tok, gate_weight, up_weight, after, start, width, tile):
    live, depth = tok.shape
    half = live // 2
    weight = pl.BlockSpec((depth, tile), lambda j: (0, start // tile + j))
    out = pl.BlockSpec((2, half, tile), lambda j: (0, 0, j))
    return pl.pallas_call(
        gate_up_kernel,
        out_shape=[jax.ShapeDtypeStruct((2, half, width), BF16), jax.ShapeDtypeStruct((2, half, width), F32)],
        grid=(width // tile,),
        in_specs=[pl.BlockSpec((live, depth), lambda j: (0, 0)), weight, weight]
        + [pl.BlockSpec(memory_space=pl.ANY)] * len(after),
        out_specs=[out, out],
        compiler_params=pltpu.CompilerParams(vmem_limit_bytes=40 * MIB),
        cost_estimate=pl.CostEstimate(
            flops=0, bytes_accessed=0, transcendentals=0
        ),
        name="gate_up",
    )(tok, gate_weight, up_weight, *after)


def gate_up_held_kernel(tile, tok_ref, gate_ref, up_ref, *refs):
    send_ref, keep_ref = refs[-2:]
    half, width = keep_ref.shape[1:]
    rows = tok_ref[...]
    for j in range(0, width, tile):
        for i, w_ref in enumerate((gate_ref, up_ref)):
            part = jnp.dot(rows, w_ref[:, j:j + tile], preferred_element_type=F32)
            keep_ref[i, :, j:j + tile] = part[:half]
            send_ref[i, :, j:j + tile] = part[half:].astype(BF16)


def gate_up_held(tok, gate_held, up_held, after, tile):
    half, width = tok.shape[0] // 2, gate_held.shape[1]
    held, anywhere = pl.BlockSpec(memory_space=pltpu.VMEM), pl.BlockSpec(memory_space=pl.ANY)
    return pl.pallas_call(
        functools.partial(gate_up_held_kernel, tile),
        out_shape=[jax.ShapeDtypeStruct((2, half, width), BF16), jax.ShapeDtypeStruct((2, half, width), F32)],
        in_specs=[held] * 3 + [anywhere] * len(after),
        out_specs=[held] * 2,
        compiler_params=pltpu.CompilerParams(vmem_limit_bytes=6 * MIB),
        cost_estimate=pl.CostEstimate(flops=0, bytes_accessed=0, transcendentals=0),
        name="gate_up_held",
    )(tok, gate_held, up_held, *after)


def join_kernel(n_handed, n_after, nx, keep_ref, got_ref, *refs):
    out_refs = refs[n_handed + n_after:][:nx]
    quarter = out_refs[0].shape[1]
    for k, out_ref in enumerate(out_refs):
        rows = pl.ds(k * quarter, quarter)
        out_ref[...] = (keep_ref[:, rows] + got_ref[:, rows].astype(F32)).astype(out_ref.dtype)


def join(keep, got, handed, after, nx):
    two, half, width = keep.shape
    shape = (two, half // nx, width)
    held, anywhere = pl.BlockSpec(memory_space=pltpu.VMEM), pl.BlockSpec(memory_space=pl.ANY)
    out = pl.pallas_call(
        functools.partial(join_kernel, len(handed), len(after), nx),
        out_shape=[jax.ShapeDtypeStruct(shape, BF16 if k else F32) for k in range(nx)]
        + [jax.ShapeDtypeStruct(a.shape, a.dtype) for a in handed],
        in_specs=[held, held] + [anywhere] * (len(handed) + len(after)),
        out_specs=[held] * nx + [anywhere] * len(handed),
        input_output_aliases={2 + i: nx + i for i in range(len(handed))},
        compiler_params=pltpu.CompilerParams(vmem_limit_bytes=8 * MIB),
        cost_estimate=pl.CostEstimate(flops=0, bytes_accessed=0, transcendentals=0),
        name="join",
    )(keep, got, *handed, *after)
    return out[0], out[1:nx], out[nx:]


def activate_kernel(n_got, n_chunks, n_unread, *refs):
    own_ref = refs[n_chunks * (1 + n_got) + n_unread]
    column = 0
    for c in range(n_chunks):
        mine_ref, *got_refs = refs[c * (1 + n_got):(c + 1) * (1 + n_got)]
        both = mine_ref[...]
        for got_ref in got_refs:
            both = both + got_ref[...].astype(F32)
        gate, up = both[0], both[1]
        own_ref[:, column:column + gate.shape[1]] = (gate / (1.0 + jnp.exp(-gate)) * up).astype(BF16)
        column += gate.shape[1]


def activate(sums, handed, after):
    held, anywhere = pl.BlockSpec(memory_space=pltpu.VMEM), pl.BlockSpec(memory_space=pl.ANY)
    flat = [a for chunk in sums for a in chunk]
    width = sum(chunk[0].shape[2] for chunk in sums)
    out = pl.pallas_call(
        functools.partial(activate_kernel, len(sums[0]) - 1, len(sums), len(handed) + len(after)),
        out_shape=[jax.ShapeDtypeStruct((flat[0].shape[1], width), BF16)]
        + [jax.ShapeDtypeStruct(a.shape, a.dtype) for a in handed],
        in_specs=[held] * len(flat) + [anywhere] * (len(handed) + len(after)),
        out_specs=[held] + [anywhere] * len(handed),
        input_output_aliases={len(flat) + i: 1 + i for i in range(len(handed))},
        compiler_params=pltpu.CompilerParams(vmem_limit_bytes=8 * MIB),
        cost_estimate=pl.CostEstimate(flops=0, bytes_accessed=0, transcendentals=0),
        name="activate",
    )(*flat, *handed, *after)
    return out[0], out[1:]


def relay_kernel(own_ref, got_ref, *refs):
    out_ref = refs[len(refs) // 2]
    out_ref[...] = (own_ref[...].astype(F32) + got_ref[...].astype(F32)).astype(BF16)


def relay(own, got, handed, after):
    held, anywhere = pl.BlockSpec(memory_space=pltpu.VMEM), pl.BlockSpec(memory_space=pl.ANY)
    out = pl.pallas_call(
        relay_kernel,
        out_shape=[jax.ShapeDtypeStruct(a.shape, a.dtype) for a in (own, *handed)],
        in_specs=[held, held] + [anywhere] * (1 + len(handed)),
        out_specs=[held] + [anywhere] * len(handed),
        input_output_aliases={2 + i: 1 + i for i in range(len(handed))},
        compiler_params=pltpu.CompilerParams(vmem_limit_bytes=8 * MIB),
        cost_estimate=pl.CostEstimate(flops=0, bytes_accessed=0, transcendentals=0),
        name="relay",
    )(own, got, *handed, after)
    return out[0], out[1:]


def put_rows(h_refs, hidden):
    row = 0
    for r in h_refs:
        hidden[row:row + r.shape[0]] = r[...]
        row += r.shape[0]


def down_kernel(n_h, *refs):
    h_refs, w_ref, out_ref, hidden = refs[:n_h], refs[n_h], refs[-2], refs[-1]

    @pl.when(pl.program_id(0) == 0)
    def _():
        put_rows(h_refs, hidden)

    out_ref[...] = jnp.dot(hidden[...], w_ref[...], preferred_element_type=F32)


def down(hidden, down_weight, after, start):
    live = sum(h.shape[0] for h in hidden)
    width = hidden[0].shape[1]
    out_width = down_weight.shape[1]
    tile = min(out_width, 512)
    weight = pl.BlockSpec((pl.Element(width), pl.Element(tile)), lambda j: (start, j * tile))
    return pl.pallas_call(
        functools.partial(down_kernel, len(hidden)),
        out_shape=jax.ShapeDtypeStruct((live, out_width), F32),
        grid=(out_width // tile,),
        in_specs=[pl.BlockSpec(h.shape, lambda j: (0, 0)) for h in hidden]
        + [weight]
        + [pl.BlockSpec(memory_space=pl.ANY)] * len(after),
        out_specs=pl.BlockSpec((live, tile), lambda j: (0, j)),
        scratch_shapes=[pltpu.VMEM((live, width), BF16)],
        compiler_params=pltpu.CompilerParams(vmem_limit_bytes=28 * MIB),
        cost_estimate=pl.CostEstimate(flops=0, bytes_accessed=0, transcendentals=0),
        name="down",
    )(*hidden, down_weight, *after)


def fetch_kernel(starts, src_ref, *refs):
    outs, sems = refs[-1 - len(starts):-1], refs[-1]
    copies = [
        pltpu.make_async_copy(src_ref.at[pl.ds(start, out.shape[0])], out, sems.at[i])
        for i, (start, out) in enumerate(zip(starts, outs))
    ]
    for copy in copies:
        copy.start()
    for copy in copies:
        copy.wait()


def fetch(down_weight, chunks, after):
    held, anywhere = pl.BlockSpec(memory_space=pltpu.VMEM), pl.BlockSpec(memory_space=pl.ANY)
    return pl.pallas_call(
        functools.partial(fetch_kernel, [start for start, _ in chunks]),
        out_shape=[jax.ShapeDtypeStruct((width, down_weight.shape[1]), BF16) for _, width in chunks],
        in_specs=[anywhere] * (1 + len(after)),
        out_specs=[held] * len(chunks),
        scratch_shapes=[pltpu.SemaphoreType.DMA((len(chunks),))],
        compiler_params=pltpu.CompilerParams(vmem_limit_bytes=28 * MIB),
        cost_estimate=pl.CostEstimate(flops=0, bytes_accessed=0, transcendentals=0),
        name="fetch",
    )(down_weight, *after)


def down_held_kernel(n_h, last, tile, *refs):
    h_refs, w_ref, total_ref, outs, hidden = refs[:n_h], refs[n_h], refs[n_h + 1], refs[n_h + 2:-1], refs[-1]
    put_rows(h_refs, hidden)
    for j in range(0, total_ref.shape[1], tile):
        total = jnp.dot(hidden[...], w_ref[:, j:j + tile], preferred_element_type=F32) + total_ref[:, j:j + tile]
        if not last:
            outs[0][:, j:j + tile] = total
            continue
        pick_ref = outs[0]
        spread = jnp.dot(pick_ref[...], total.astype(BF16), preferred_element_type=F32).astype(BF16)
        row = 0
        for out_ref in outs[1:]:
            n = out_ref.shape[0]
            out_ref[:, j:j + tile] = spread[row:row + n]
            row += n


def down_held(hidden, weight_held, total, pick, out_rows):
    live, out_width = total.shape
    held = pl.BlockSpec(memory_space=pltpu.VMEM)
    last = pick is not None
    if last:
        out_shape = [jax.ShapeDtypeStruct((n, out_width), BF16) for n in out_rows]
    else:
        out_shape = jax.ShapeDtypeStruct((live, out_width), F32)
    return pl.pallas_call(
        functools.partial(down_held_kernel, len(hidden), last, min(out_width, 512)),
        out_shape=out_shape,
        in_specs=[held] * (len(hidden) + (3 if last else 2)),
        out_specs=[held] * len(out_rows) if last else held,
        scratch_shapes=[pltpu.VMEM((live, hidden[0].shape[1]), BF16)],
        compiler_params=pltpu.CompilerParams(vmem_limit_bytes=12 * MIB),
        cost_estimate=pl.CostEstimate(flops=0, bytes_accessed=0, transcendentals=0),
        name="down_held",
    )(*hidden, weight_held, total, *([pick] if last else []))


def column_chunks(cols, tile):
    tiles = cols // tile
    shares = (3, 3, 4, 3)
    edges = [round(tiles * sum(shares[:i]) / sum(shares)) for i in range(len(shares) + 1)]
    return [(a * tile, (b - a) * tile) for a, b in zip(edges, edges[1:]) if b > a]


def local(n_gx, n_gy, tokens, gate_weight, up_weight, down_weight, lengths):
    nx = n_gy // 2
    tok_dev = tokens.shape[0]
    live = 3 * tok_dev * n_gx // 4
    cols = gate_weight.shape[1]
    tile = 512 if cols % 512 == 0 else 128
    chunks = column_chunks(cols, tile)
    line = n_gx == 4
    part = tok_dev // 2

    def over_z(block, k, among=range(n_gx)):
        return lax.ppermute(block, "gx", [(z, z ^ k) for z in among])

    def over_core(block):
        return lax.ppermute(block, "gy", [(i, i ^ 1) for i in range(n_gy)])

    def over_x(block, k):
        return lax.ppermute(block, "gy", [(i, (i + 2 * k) % n_gy) for i in range(n_gy)])

    mine = hold(tokens)
    blocks = [mine] + [over_z(mine, k) for k in range(1, n_gx)]
    pick_in, pick_out, weights = prepare(lengths, gate_weight, up_weight, chunks[:3], n_gx, nx, tok_dev, live)
    tok = compact(pick_in, blocks)

    made = [gate_up_held(tok, *weights[i], [], tile) for i in range(2)]
    sends, keeps = [list(a) for a in zip(*made)]
    sums = []

    def exchange(j, handed):
        mine, blocks, handed = join(keeps[j], over_core(sends[j]), handed, [], nx)
        sums.append([mine] + [over_x(b, k + 1) for k, b in enumerate(blocks)])
        return list(blocks), handed

    def finish(first, last, handed, after):
        own, handed = activate(sums[first:last], handed, after)
        h = [own] + [over_x(own, -k) for k in range(1, nx)]
        return h + [over_core(a) for a in h], handed

    ready, sends[1:2] = exchange(0, sends[1:2])
    ready += exchange(1, [])[0]
    made = [gate_up_held(tok, *weights[2], ready, tile)]
    made.append(gate_up(tok, gate_weight, up_weight, made[0][:1], *chunks[3], tile))
    for send, keep in made:
        sends.append(send)
        keeps.append(keep)
    hidden, sends[2:] = finish(0, 2, sends[2:], [])
    ready, sends[3:] = exchange(2, sends[3:])
    ready += exchange(3, [])[0]
    rows_held = fetch(down_weight, chunks[2:], ready)
    total = down(hidden, down_weight, [rows_held[0]], chunks[0][0])
    hidden, _ = finish(2, 3, [], [total])
    total = down_held(hidden, rows_held[0], total, None, None)
    hidden, _ = finish(3, 4, [], [])
    out_rows = [tok_dev, part, part, tok_dev, tok_dev] if line else [tok_dev] * n_gx
    spread = down_held(hidden, rows_held[1], total, pick_out, out_rows)

    if line:
        own, low, high, two, three = spread
        ends = over_z(three, 1, (0, 3))
        middle = over_z(three, 3, (1, 2))
        two, near = relay(two, ends, [low, high], middle)
        far = over_z(two, 2)
        near = [over_z(a, 1) for a in near]
        parts = [own, jnp.concatenate(near, axis=0), far, middle]
    else:
        parts = [spread[0]] + [over_z(spread[k], k) for k in range(1, n_gx)]
    return sum(p.astype(F32) for p in parts).astype(BF16)


def solution(mesh):
    placed = (P(("group", "gx"), "gy"), P("gy", "gx"), P("gy", "gx"), P("gx", "gy"), P("group"))
    return jax.shard_map(
        functools.partial(local, mesh.shape["gx"], mesh.shape["gy"]),
        mesh=mesh, in_specs=placed, out_specs=P(("group", "gx"), "gy"), check_vma=False,
    )
```

```python
import functools

import jax
import jax.numpy as jnp
from jax import lax
from jax.experimental import pallas as pl
from jax.experimental.pallas import tpu as pltpu
from jax.sharding import PartitionSpec as P

MIB = 1 << 20
BF16, F32 = jnp.bfloat16, jnp.float32


def row_sources(lengths_ref, rows, n_gx, tok_dev):
    start = jnp.int32(0)
    slot = rows
    for g in range(n_gx):
        slot = jnp.where(rows >= start, rows - start + g * tok_dev, slot)
        start = start + lengths_ref[g]
    return slot


def local_rows(shape, dim, quarter, nx):
    gy = lax.axis_index("gy")
    x, core = gy // 2, gy % 2
    j = lax.broadcasted_iota(jnp.int32, shape, dim)
    rows = jnp.zeros(shape, jnp.int32)
    for kc in range(2):
        for kx in range(nx):
            first = (kc * nx + kx) * quarter
            owner = lax.rem(x + kx, nx) * 2 + (1 - core if kc else core)
            rows = jnp.where(j >= first, owner * quarter + j - first, rows)
    return rows


def prepare_kernel(n_gx, nx, chunks, lengths_ref, tok_ref, gate_ref, up_ref, in_ref, out_ref, held_ref, *refs):
    outs, sems = refs[:-1], refs[-1]
    copies = []
    for i, (start, width) in enumerate(chunks):
        for k, src in enumerate((gate_ref, up_ref)):
            copies.append(pltpu.make_async_copy(src.at[:, pl.ds(start, width)], outs[2 * i + k], sems.at[2 * i + k]))
    for copy in copies:
        copy.start()
    held_ref[...] = tok_ref[...]
    tok_dev = tok_ref.shape[0]
    z = lax.axis_index("gx")
    live, slots = in_ref.shape
    quarter = live // (2 * nx)

    def slot_of(column):
        return (z ^ (column // tok_dev)) * tok_dev + column % tok_dev

    shape = (live, slots)
    source = row_sources(lengths_ref, local_rows(shape, 0, quarter, nx), n_gx, tok_dev)
    in_ref[...] = (source == slot_of(lax.broadcasted_iota(jnp.int32, shape, 1))).astype(F32).astype(BF16)
    shape = (slots, live)
    source = row_sources(lengths_ref, local_rows(shape, 1, quarter, nx), n_gx, tok_dev)
    out_ref[...] = (source == slot_of(lax.broadcasted_iota(jnp.int32, shape, 0))).astype(F32).astype(BF16)
    for copy in copies:
        copy.wait()


def prepare(lengths, tokens, gate_weight, up_weight, chunks, n_gx, nx, live):
    slots = n_gx * tokens.shape[0]
    held, anywhere = pl.BlockSpec(memory_space=pltpu.VMEM), pl.BlockSpec(memory_space=pl.ANY)
    weights = [jax.ShapeDtypeStruct((gate_weight.shape[0], width), BF16) for _, width in chunks for _ in range(2)]
    out = pl.pallas_call(
        functools.partial(prepare_kernel, n_gx, nx, chunks),
        out_shape=[
            jax.ShapeDtypeStruct((live, slots), BF16),
            jax.ShapeDtypeStruct((slots, live), BF16),
            jax.ShapeDtypeStruct(tokens.shape, tokens.dtype),
        ]
        + weights,
        in_specs=[pl.BlockSpec(memory_space=pltpu.SMEM), held, anywhere, anywhere],
        out_specs=[held] * (3 + len(weights)),
        scratch_shapes=[pltpu.SemaphoreType.DMA((len(weights),))],
        cost_estimate=pl.CostEstimate(flops=0, bytes_accessed=0, transcendentals=0),
        compiler_params=pltpu.CompilerParams(vmem_limit_bytes=4 * MIB),
        name="prepare",
    )(lengths, tokens, gate_weight, up_weight)
    return out[0], out[1], out[2], [out[3 + 2 * i:5 + 2 * i] for i in range(len(chunks))]


def compact_kernel(pick_ref, *refs):
    rows = jnp.concatenate([r[...] for r in refs[:-1]], axis=0)
    refs[-1][...] = jnp.dot(pick_ref[...], rows, preferred_element_type=F32).astype(BF16)


def compact(pick, blocks):
    return pl.pallas_call(
        compact_kernel,
        out_shape=jax.ShapeDtypeStruct((pick.shape[0], blocks[0].shape[1]), BF16),
        compiler_params=pltpu.CompilerParams(vmem_limit_bytes=5 * MIB),
        cost_estimate=pl.CostEstimate(flops=0, bytes_accessed=0, transcendentals=0),
        name="compact",
    )(pick, *blocks)


def send_shapes(half, nx, width):
    return [jax.ShapeDtypeStruct((half // nx, width), BF16)] * (2 * nx)


def put_part(i, part, columns, keep_ref, send_refs):
    half = keep_ref.shape[1]
    nx = len(send_refs) // 2
    quarter = half // nx
    keep_ref[i, :, columns] = part[:half]
    for k in range(nx):
        first = half + k * quarter
        send_refs[i * nx + k][:, columns] = part[first:first + quarter].astype(BF16)


def gate_up_held_kernel(n_after, tile, tok_ref, gate_ref, up_ref, *refs):
    keep_ref, *send_refs = refs[n_after:]
    rows = tok_ref[...]
    for j in range(0, keep_ref.shape[2], tile):
        columns = slice(j, j + tile)
        for i, w_ref in enumerate((gate_ref, up_ref)):
            part = jnp.dot(rows, w_ref[:, columns], preferred_element_type=F32)
            put_part(i, part, columns, keep_ref, send_refs)


def gate_up_held(tok, gate_held, up_held, after, nx, tile):
    half, width = tok.shape[0] // 2, gate_held.shape[1]
    held, anywhere = pl.BlockSpec(memory_space=pltpu.VMEM), pl.BlockSpec(memory_space=pl.ANY)
    keep, *send = pl.pallas_call(
        functools.partial(gate_up_held_kernel, len(after), tile),
        out_shape=[jax.ShapeDtypeStruct((2, half, width), F32)] + send_shapes(half, nx, width),
        in_specs=[held] * 3 + [anywhere] * len(after),
        out_specs=[held] * (1 + 2 * nx),
        compiler_params=pltpu.CompilerParams(vmem_limit_bytes=6 * MIB),
        cost_estimate=pl.CostEstimate(flops=0, bytes_accessed=0, transcendentals=0),
        name="gate_up_held",
    )(tok, gate_held, up_held, *after)
    return send, keep


def gate_up_kernel(n_after, tok_ref, gate_ref, up_ref, *refs):
    keep_ref, *send_refs = refs[n_after:]
    rows = tok_ref[...]
    for i, w_ref in enumerate((gate_ref, up_ref)):
        part = jnp.dot(rows, w_ref[...], preferred_element_type=F32)
        put_part(i, part, slice(None), keep_ref, send_refs)


def gate_up(tok, gate_weight, up_weight, after, start, width, nx, tile):
    live, depth = tok.shape
    half = live // 2
    weight = pl.BlockSpec((depth, tile), lambda j: (0, start // tile + j))
    keep, *send = pl.pallas_call(
        functools.partial(gate_up_kernel, len(after)),
        out_shape=[jax.ShapeDtypeStruct((2, half, width), F32)] + send_shapes(half, nx, width),
        grid=(width // tile,),
        in_specs=[pl.BlockSpec((live, depth), lambda j: (0, 0)), weight, weight]
        + [pl.BlockSpec(memory_space=pl.ANY)] * len(after),
        out_specs=[pl.BlockSpec((2, half, tile), lambda j: (0, 0, j))]
        + [pl.BlockSpec((half // nx, tile), lambda j: (0, j))] * (2 * nx),
        compiler_params=pltpu.CompilerParams(vmem_limit_bytes=40 * MIB),
        cost_estimate=pl.CostEstimate(flops=0, bytes_accessed=0, transcendentals=0),
        name="gate_up",
    )(tok, gate_weight, up_weight, *after)
    return send, keep


def join_kernel(n_unread, nx, keep_ref, *refs):
    got_refs, out_refs = refs[:2 * nx], refs[2 * nx + n_unread:][:nx]
    quarter = out_refs[0].shape[1]
    for i in range(2):
        for k, out_ref in enumerate(out_refs):
            rows = pl.ds(k * quarter, quarter)
            out_ref[i] = (keep_ref[i, rows] + got_refs[i * nx + k][...].astype(F32)).astype(out_ref.dtype)


def join(keep, got, handed, nx):
    two, half, width = keep.shape
    shape = (two, half // nx, width)
    held, anywhere = pl.BlockSpec(memory_space=pltpu.VMEM), pl.BlockSpec(memory_space=pl.ANY)
    out = pl.pallas_call(
        functools.partial(join_kernel, len(handed), nx),
        out_shape=[jax.ShapeDtypeStruct(shape, BF16 if k else F32) for k in range(nx)]
        + [jax.ShapeDtypeStruct(a.shape, a.dtype) for a in handed],
        in_specs=[held] * (1 + len(got)) + [anywhere] * len(handed),
        out_specs=[held] * nx + [anywhere] * len(handed),
        input_output_aliases={1 + len(got) + i: nx + i for i in range(len(handed))},
        compiler_params=pltpu.CompilerParams(vmem_limit_bytes=8 * MIB),
        cost_estimate=pl.CostEstimate(flops=0, bytes_accessed=0, transcendentals=0),
        name="join",
    )(keep, *got, *handed)
    return out[0], list(out[1:nx]), list(out[nx:])


def activate_kernel(n_got, n_chunks, n_unread, *refs):
    own_ref = refs[n_chunks * (1 + n_got) + n_unread]
    column = 0
    for c in range(n_chunks):
        mine_ref, *got_refs = refs[c * (1 + n_got):(c + 1) * (1 + n_got)]
        both = mine_ref[...]
        for got_ref in got_refs:
            both = both + got_ref[...].astype(F32)
        gate, up = both[0], both[1]
        own_ref[:, column:column + gate.shape[1]] = (gate / (1.0 + jnp.exp(-gate)) * up).astype(BF16)
        column += gate.shape[1]


def activate(sums, handed, after):
    held, anywhere = pl.BlockSpec(memory_space=pltpu.VMEM), pl.BlockSpec(memory_space=pl.ANY)
    flat = [a for chunk in sums for a in chunk]
    width = sum(chunk[0].shape[2] for chunk in sums)
    out = pl.pallas_call(
        functools.partial(activate_kernel, len(sums[0]) - 1, len(sums), len(handed) + len(after)),
        out_shape=[jax.ShapeDtypeStruct((flat[0].shape[1], width), BF16)]
        + [jax.ShapeDtypeStruct(a.shape, a.dtype) for a in handed],
        in_specs=[held] * len(flat) + [anywhere] * (len(handed) + len(after)),
        out_specs=[held] + [anywhere] * len(handed),
        input_output_aliases={len(flat) + i: 1 + i for i in range(len(handed))},
        compiler_params=pltpu.CompilerParams(vmem_limit_bytes=8 * MIB),
        cost_estimate=pl.CostEstimate(flops=0, bytes_accessed=0, transcendentals=0),
        name="activate",
    )(*flat, *handed, *after)
    return out[0], out[1:]


def relay_kernel(own_ref, got_ref, *refs):
    out_ref = refs[len(refs) // 2]
    out_ref[...] = (own_ref[...].astype(F32) + got_ref[...].astype(F32)).astype(BF16)


def relay(own, got, handed, after):
    held, anywhere = pl.BlockSpec(memory_space=pltpu.VMEM), pl.BlockSpec(memory_space=pl.ANY)
    out = pl.pallas_call(
        relay_kernel,
        out_shape=[jax.ShapeDtypeStruct(a.shape, a.dtype) for a in (own, *handed)],
        in_specs=[held, held] + [anywhere] * (1 + len(handed)),
        out_specs=[held] + [anywhere] * len(handed),
        input_output_aliases={2 + i: 1 + i for i in range(len(handed))},
        compiler_params=pltpu.CompilerParams(vmem_limit_bytes=8 * MIB),
        cost_estimate=pl.CostEstimate(flops=0, bytes_accessed=0, transcendentals=0),
        name="relay",
    )(own, got, *handed, after)
    return out[0], out[1:]


def put_rows(h_refs, hidden):
    row = 0
    for r in h_refs:
        hidden[row:row + r.shape[0]] = r[...]
        row += r.shape[0]


def down_kernel(n_h, *refs):
    h_refs, w_ref, out_ref, hidden = refs[:n_h], refs[n_h], refs[-2], refs[-1]

    @pl.when(pl.program_id(0) == 0)
    def _():
        put_rows(h_refs, hidden)

    out_ref[...] = jnp.dot(hidden[...], w_ref[...], preferred_element_type=F32)


def down(hidden, down_weight, after, start):
    live = sum(h.shape[0] for h in hidden)
    width = hidden[0].shape[1]
    out_width = down_weight.shape[1]
    tile = min(out_width, 512)
    weight = pl.BlockSpec((pl.Element(width), pl.Element(tile)), lambda j: (start, j * tile))
    return pl.pallas_call(
        functools.partial(down_kernel, len(hidden)),
        out_shape=jax.ShapeDtypeStruct((live, out_width), F32),
        grid=(out_width // tile,),
        in_specs=[pl.BlockSpec(h.shape, lambda j: (0, 0)) for h in hidden]
        + [weight]
        + [pl.BlockSpec(memory_space=pl.ANY)] * len(after),
        out_specs=pl.BlockSpec((live, tile), lambda j: (0, j)),
        scratch_shapes=[pltpu.VMEM((live, width), BF16)],
        compiler_params=pltpu.CompilerParams(vmem_limit_bytes=28 * MIB),
        cost_estimate=pl.CostEstimate(flops=0, bytes_accessed=0, transcendentals=0),
        name="down",
    )(*hidden, down_weight, *after)


def fetch_kernel(starts, src_ref, *refs):
    outs, sems = refs[-1 - len(starts):-1], refs[-1]
    copies = [
        pltpu.make_async_copy(src_ref.at[pl.ds(start, out.shape[0])], out, sems.at[i])
        for i, (start, out) in enumerate(zip(starts, outs))
    ]
    for copy in copies:
        copy.start()
    for copy in copies:
        copy.wait()


def fetch(down_weight, chunks, after):
    held, anywhere = pl.BlockSpec(memory_space=pltpu.VMEM), pl.BlockSpec(memory_space=pl.ANY)
    return pl.pallas_call(
        functools.partial(fetch_kernel, [start for start, _ in chunks]),
        out_shape=[jax.ShapeDtypeStruct((width, down_weight.shape[1]), BF16) for _, width in chunks],
        in_specs=[anywhere] * (1 + len(after)),
        out_specs=[held] * len(chunks),
        scratch_shapes=[pltpu.SemaphoreType.DMA((len(chunks),))],
        compiler_params=pltpu.CompilerParams(vmem_limit_bytes=28 * MIB),
        cost_estimate=pl.CostEstimate(flops=0, bytes_accessed=0, transcendentals=0),
        name="fetch",
    )(down_weight, *after)


def down_held_kernel(n_h, last, tile, *refs):
    h_refs, w_ref, total_ref, outs, hidden = refs[:n_h], refs[n_h], refs[n_h + 1], refs[n_h + 2:-1], refs[-1]
    put_rows(h_refs, hidden)
    for j in range(0, total_ref.shape[1], tile):
        total = jnp.dot(hidden[...], w_ref[:, j:j + tile], preferred_element_type=F32) + total_ref[:, j:j + tile]
        if not last:
            outs[0][:, j:j + tile] = total
            continue
        pick_ref = outs[0]
        spread = jnp.dot(pick_ref[...], total.astype(BF16), preferred_element_type=F32).astype(BF16)
        row = 0
        for out_ref in outs[1:]:
            n = out_ref.shape[0]
            out_ref[:, j:j + tile] = spread[row:row + n]
            row += n


def down_held(hidden, weight_held, total, pick, out_rows):
    live, out_width = total.shape
    held = pl.BlockSpec(memory_space=pltpu.VMEM)
    last = pick is not None
    if last:
        out_shape = [jax.ShapeDtypeStruct((n, out_width), BF16) for n in out_rows]
    else:
        out_shape = jax.ShapeDtypeStruct((live, out_width), F32)
    return pl.pallas_call(
        functools.partial(down_held_kernel, len(hidden), last, min(out_width, 512)),
        out_shape=out_shape,
        in_specs=[held] * (len(hidden) + (3 if last else 2)),
        out_specs=[held] * len(out_rows) if last else held,
        scratch_shapes=[pltpu.VMEM((live, hidden[0].shape[1]), BF16)],
        compiler_params=pltpu.CompilerParams(vmem_limit_bytes=12 * MIB),
        cost_estimate=pl.CostEstimate(flops=0, bytes_accessed=0, transcendentals=0),
        name="down_held",
    )(*hidden, weight_held, total, *([pick] if last else []))


def column_chunks(cols, tile):
    tiles = cols // tile
    shares = (3, 3, 4, 3)
    edges = [round(tiles * sum(shares[:i]) / sum(shares)) for i in range(len(shares) + 1)]
    return [(a * tile, (b - a) * tile) for a, b in zip(edges, edges[1:]) if b > a]


def local(n_gx, n_gy, tokens, gate_weight, up_weight, down_weight, lengths):
    nx = n_gy // 2
    tok_dev = tokens.shape[0]
    live = 3 * tok_dev * n_gx // 4
    cols = gate_weight.shape[1]
    tile = 512 if cols % 512 == 0 else 128
    chunks = column_chunks(cols, tile)
    line = n_gx == 4
    part = tok_dev // 2

    def over_z(block, k, among=range(n_gx)):
        return lax.ppermute(block, "gx", [(z, z ^ k) for z in among])

    def over_core(block):
        return lax.ppermute(block, "gy", [(i, i ^ 1) for i in range(n_gy)])

    def over_x(block, k):
        return lax.ppermute(block, "gy", [(i, (i + 2 * k) % n_gy) for i in range(n_gy)])

    far = [over_z(tokens, k) for k in range(1, n_gx)]
    pick_in, pick_out, held, weights = prepare(lengths, tokens, gate_weight, up_weight, chunks[:3], n_gx, nx, live)
    blocks = [held] + far
    tok = compact(pick_in, blocks)

    made = [gate_up_held(tok, *weights[i], [], nx, tile) for i in range(2)]
    sends, keeps = [list(a) for a in zip(*made)]
    sums = []

    def exchange(j, handed):
        mine, blocks, handed = join(keeps[j], [over_core(a) for a in sends[j]], handed, nx)
        sums.append([mine] + [over_x(b, k + 1) for k, b in enumerate(blocks)])
        return blocks, handed

    def finish(first, last, handed, after):
        own, handed = activate(sums[first:last], handed, after)
        h = [own] + [over_x(own, -k) for k in range(1, nx)]
        return h + [over_core(a) for a in h], handed

    ready, sends[1] = exchange(0, sends[1])
    ready = ready + exchange(1, [])[0]
    made = [gate_up_held(tok, *weights[2], ready, nx, tile)]
    made.append(gate_up(tok, gate_weight, up_weight, made[0][0][:1], *chunks[3], nx, tile))
    pieces = len(sends[0])
    hidden, handed = finish(0, 2, made[0][0] + made[1][0], [])
    sends += [handed[:pieces], handed[pieces:]]
    keeps += [keep for _, keep in made]
    ready, sends[3] = exchange(2, sends[3])
    ready = ready + exchange(3, [])[0]
    rows_held = fetch(down_weight, chunks[2:], ready)
    total = down(hidden, down_weight, [rows_held[0]], chunks[0][0])
    hidden, _ = finish(2, 3, [], [total])
    total = down_held(hidden, rows_held[0], total, None, None)
    hidden, _ = finish(3, 4, [], [])
    out_rows = [tok_dev, part, part, tok_dev, tok_dev] if line else [tok_dev] * n_gx
    spread = down_held(hidden, rows_held[1], total, pick_out, out_rows)

    if line:
        own, low, high, two, three = spread
        ends = over_z(three, 1, (0, 3))
        middle = over_z(three, 3, (1, 2))
        two, near = relay(two, ends, [low, high], middle)
        far = over_z(two, 2)
        near = [over_z(a, 1) for a in near]
        parts = [own, jnp.concatenate(near, axis=0), far, middle]
    else:
        parts = [spread[0]] + [over_z(spread[k], k) for k in range(1, n_gx)]
    return sum(p.astype(F32) for p in parts).astype(BF16)


def solution(mesh):
    placed = (P(("group", "gx"), "gy"), P("gy", "gx"), P("gy", "gx"), P("gx", "gy"), P("group"))
    return jax.shard_map(
        functools.partial(local, mesh.shape["gx"], mesh.shape["gy"]),
        mesh=mesh, in_specs=placed, out_specs=P(("group", "gx"), "gy"), check_vma=False,
    )
```

```python
import functools

import jax
import jax.numpy as jnp
from jax import lax
from jax.experimental import pallas as pl
from jax.experimental.pallas import tpu as pltpu
from jax.sharding import PartitionSpec as P

MIB = 1 << 20
BF16, F32 = jnp.bfloat16, jnp.float32


def row_sources(lengths_ref, rows, n_gx, tok_dev):
    start = jnp.int32(0)
    slot = rows
    for g in range(n_gx):
        slot = jnp.where(rows >= start, rows - start + g * tok_dev, slot)
        start = start + lengths_ref[g]
    return slot


def local_rows(shape, dim, quarter, nx):
    gy = lax.axis_index("gy")
    x, core = gy // 2, gy % 2
    j = lax.broadcasted_iota(jnp.int32, shape, dim)
    rows = jnp.zeros(shape, jnp.int32)
    for kc in range(2):
        for kx in range(nx):
            first = (kc * nx + kx) * quarter
            owner = lax.rem(x + kx, nx) * 2 + (1 - core if kc else core)
            rows = jnp.where(j >= first, owner * quarter + j - first, rows)
    return rows


def prepare_kernel(n_gx, nx, chunks, lengths_ref, tok_ref, gate_ref, up_ref, in_ref, out_ref, held_ref, *refs):
    outs, sems = refs[:-1], refs[-1]
    copies = []
    for i, (start, width) in enumerate(chunks):
        for k, src in enumerate((gate_ref, up_ref)):
            copies.append(pltpu.make_async_copy(src.at[:, pl.ds(start, width)], outs[2 * i + k], sems.at[2 * i + k]))
    for copy in copies:
        copy.start()
    held_ref[...] = tok_ref[...]
    tok_dev = tok_ref.shape[0]
    z = lax.axis_index("gx")
    live, slots = in_ref.shape
    quarter = live // (2 * nx)

    def slot_of(column):
        return (z ^ (column // tok_dev)) * tok_dev + column % tok_dev

    shape = (live, slots)
    source = row_sources(lengths_ref, local_rows(shape, 0, quarter, nx), n_gx, tok_dev)
    in_ref[...] = (source == slot_of(lax.broadcasted_iota(jnp.int32, shape, 1))).astype(F32).astype(BF16)
    shape = (slots, live)
    source = row_sources(lengths_ref, local_rows(shape, 1, quarter, nx), n_gx, tok_dev)
    out_ref[...] = (source == slot_of(lax.broadcasted_iota(jnp.int32, shape, 0))).astype(F32).astype(BF16)
    for copy in copies:
        copy.wait()


def prepare(lengths, tokens, gate_weight, up_weight, chunks, n_gx, nx, live):
    slots = n_gx * tokens.shape[0]
    held, anywhere = pl.BlockSpec(memory_space=pltpu.VMEM), pl.BlockSpec(memory_space=pl.ANY)
    weights = [jax.ShapeDtypeStruct((gate_weight.shape[0], width), BF16) for _, width in chunks for _ in range(2)]
    out = pl.pallas_call(
        functools.partial(prepare_kernel, n_gx, nx, chunks),
        out_shape=[
            jax.ShapeDtypeStruct((live, slots), BF16),
            jax.ShapeDtypeStruct((slots, live), BF16),
            jax.ShapeDtypeStruct(tokens.shape, tokens.dtype),
        ]
        + weights,
        in_specs=[pl.BlockSpec(memory_space=pltpu.SMEM), held, anywhere, anywhere],
        out_specs=[held] * (3 + len(weights)),
        scratch_shapes=[pltpu.SemaphoreType.DMA((len(weights),))],
        cost_estimate=pl.CostEstimate(flops=0, bytes_accessed=0, transcendentals=0),
        compiler_params=pltpu.CompilerParams(vmem_limit_bytes=4 * MIB),
        name="prepare",
    )(lengths, tokens, gate_weight, up_weight)
    return out[0], out[1], out[2], [out[3 + 2 * i:5 + 2 * i] for i in range(len(chunks))]


def compact_kernel(pick_ref, *refs):
    rows = jnp.concatenate([r[...] for r in refs[:-1]], axis=0)
    refs[-1][...] = jnp.dot(pick_ref[...], rows, preferred_element_type=F32).astype(BF16)


def compact(pick, blocks):
    return pl.pallas_call(
        compact_kernel,
        out_shape=jax.ShapeDtypeStruct((pick.shape[0], blocks[0].shape[1]), BF16),
        compiler_params=pltpu.CompilerParams(vmem_limit_bytes=5 * MIB),
        cost_estimate=pl.CostEstimate(flops=0, bytes_accessed=0, transcendentals=0),
        name="compact",
    )(pick, *blocks)


def send_shapes(half, nx, width, split):
    if split:
        return [jax.ShapeDtypeStruct((half // nx, width), BF16)] * (2 * nx)
    return [jax.ShapeDtypeStruct((2, half, width), BF16)]


def put_part(i, part, columns, keep_ref, send_refs):
    half = keep_ref.shape[1]
    keep_ref[i, :, columns] = part[:half]
    if len(send_refs) == 1:
        send_refs[0][i, :, columns] = part[half:].astype(BF16)
        return
    nx = len(send_refs) // 2
    quarter = half // nx
    for k in range(nx):
        first = half + k * quarter
        send_refs[i * nx + k][:, columns] = part[first:first + quarter].astype(BF16)


def gate_up_held_kernel(n_after, tile, tok_ref, gate_ref, up_ref, *refs):
    keep_ref, *send_refs = refs[n_after:]
    rows = tok_ref[...]
    for j in range(0, keep_ref.shape[2], tile):
        columns = slice(j, j + tile)
        for i, w_ref in enumerate((gate_ref, up_ref)):
            part = jnp.dot(rows, w_ref[:, columns], preferred_element_type=F32)
            put_part(i, part, columns, keep_ref, send_refs)


def gate_up_held(tok, gate_held, up_held, after, nx, tile, split=False):
    half, width = tok.shape[0] // 2, gate_held.shape[1]
    held, anywhere = pl.BlockSpec(memory_space=pltpu.VMEM), pl.BlockSpec(memory_space=pl.ANY)
    keep, *send = pl.pallas_call(
        functools.partial(gate_up_held_kernel, len(after), tile),
        out_shape=[jax.ShapeDtypeStruct((2, half, width), F32)] + send_shapes(half, nx, width, split),
        in_specs=[held] * 3 + [anywhere] * len(after),
        out_specs=[held] * (1 + (2 * nx if split else 1)),
        compiler_params=pltpu.CompilerParams(vmem_limit_bytes=6 * MIB),
        cost_estimate=pl.CostEstimate(flops=0, bytes_accessed=0, transcendentals=0),
        name="gate_up_held",
    )(tok, gate_held, up_held, *after)
    return send, keep


def gate_up_kernel(n_after, tok_ref, gate_ref, up_ref, *refs):
    keep_ref, *send_refs = refs[n_after:]
    rows = tok_ref[...]
    for i, w_ref in enumerate((gate_ref, up_ref)):
        part = jnp.dot(rows, w_ref[...], preferred_element_type=F32)
        put_part(i, part, slice(None), keep_ref, send_refs)


def gate_up(tok, gate_weight, up_weight, after, start, width, nx, tile):
    live, depth = tok.shape
    half = live // 2
    weight = pl.BlockSpec((depth, tile), lambda j: (0, start // tile + j))
    keep, *send = pl.pallas_call(
        functools.partial(gate_up_kernel, len(after)),
        out_shape=[jax.ShapeDtypeStruct((2, half, width), F32)] + send_shapes(half, nx, width, True),
        grid=(width // tile,),
        in_specs=[pl.BlockSpec((live, depth), lambda j: (0, 0)), weight, weight]
        + [pl.BlockSpec(memory_space=pl.ANY)] * len(after),
        out_specs=[pl.BlockSpec((2, half, tile), lambda j: (0, 0, j))]
        + [pl.BlockSpec((half // nx, tile), lambda j: (0, j))] * (2 * nx),
        compiler_params=pltpu.CompilerParams(vmem_limit_bytes=40 * MIB),
        cost_estimate=pl.CostEstimate(flops=0, bytes_accessed=0, transcendentals=0),
        name="gate_up",
    )(tok, gate_weight, up_weight, *after)
    return send, keep


def join_kernel(n_got, n_unread, nx, keep_ref, *refs):
    got_refs, out_refs = refs[:n_got], refs[n_got + n_unread:][:nx]
    quarter = out_refs[0].shape[1]
    for i in range(2):
        for k, out_ref in enumerate(out_refs):
            rows = pl.ds(k * quarter, quarter)
            got = got_refs[0][i, rows] if n_got == 1 else got_refs[i * nx + k][...]
            out_ref[i] = (keep_ref[i, rows] + got.astype(F32)).astype(out_ref.dtype)


def join(keep, got, handed, after, nx):
    two, half, width = keep.shape
    shape = (two, half // nx, width)
    held, anywhere = pl.BlockSpec(memory_space=pltpu.VMEM), pl.BlockSpec(memory_space=pl.ANY)
    out = pl.pallas_call(
        functools.partial(join_kernel, len(got), len(handed) + len(after), nx),
        out_shape=[jax.ShapeDtypeStruct(shape, BF16 if k else F32) for k in range(nx)]
        + [jax.ShapeDtypeStruct(a.shape, a.dtype) for a in handed],
        in_specs=[held] * (1 + len(got)) + [anywhere] * (len(handed) + len(after)),
        out_specs=[held] * nx + [anywhere] * len(handed),
        input_output_aliases={1 + len(got) + i: nx + i for i in range(len(handed))},
        compiler_params=pltpu.CompilerParams(vmem_limit_bytes=8 * MIB),
        cost_estimate=pl.CostEstimate(flops=0, bytes_accessed=0, transcendentals=0),
        name="join",
    )(keep, *got, *handed, *after)
    return out[0], list(out[1:nx]), list(out[nx:])


def activate_kernel(n_got, n_chunks, n_unread, *refs):
    own_ref = refs[n_chunks * (1 + n_got) + n_unread]
    column = 0
    for c in range(n_chunks):
        mine_ref, *got_refs = refs[c * (1 + n_got):(c + 1) * (1 + n_got)]
        both = mine_ref[...]
        for got_ref in got_refs:
            both = both + got_ref[...].astype(F32)
        gate, up = both[0], both[1]
        own_ref[:, column:column + gate.shape[1]] = (gate / (1.0 + jnp.exp(-gate)) * up).astype(BF16)
        column += gate.shape[1]


def activate(sums, handed, after):
    held, anywhere = pl.BlockSpec(memory_space=pltpu.VMEM), pl.BlockSpec(memory_space=pl.ANY)
    flat = [a for chunk in sums for a in chunk]
    width = sum(chunk[0].shape[2] for chunk in sums)
    out = pl.pallas_call(
        functools.partial(activate_kernel, len(sums[0]) - 1, len(sums), len(handed) + len(after)),
        out_shape=[jax.ShapeDtypeStruct((flat[0].shape[1], width), BF16)]
        + [jax.ShapeDtypeStruct(a.shape, a.dtype) for a in handed],
        in_specs=[held] * len(flat) + [anywhere] * (len(handed) + len(after)),
        out_specs=[held] + [anywhere] * len(handed),
        input_output_aliases={len(flat) + i: 1 + i for i in range(len(handed))},
        compiler_params=pltpu.CompilerParams(vmem_limit_bytes=8 * MIB),
        cost_estimate=pl.CostEstimate(flops=0, bytes_accessed=0, transcendentals=0),
        name="activate",
    )(*flat, *handed, *after)
    return out[0], out[1:]


def relay_kernel(own_ref, got_ref, *refs):
    out_ref = refs[len(refs) // 2]
    out_ref[...] = (own_ref[...].astype(F32) + got_ref[...].astype(F32)).astype(BF16)


def relay(own, got, handed, after):
    held, anywhere = pl.BlockSpec(memory_space=pltpu.VMEM), pl.BlockSpec(memory_space=pl.ANY)
    out = pl.pallas_call(
        relay_kernel,
        out_shape=[jax.ShapeDtypeStruct(a.shape, a.dtype) for a in (own, *handed)],
        in_specs=[held, held] + [anywhere] * (1 + len(handed)),
        out_specs=[held] + [anywhere] * len(handed),
        input_output_aliases={2 + i: 1 + i for i in range(len(handed))},
        compiler_params=pltpu.CompilerParams(vmem_limit_bytes=8 * MIB),
        cost_estimate=pl.CostEstimate(flops=0, bytes_accessed=0, transcendentals=0),
        name="relay",
    )(own, got, *handed, after)
    return out[0], out[1:]


def put_rows(h_refs, hidden):
    row = 0
    for r in h_refs:
        hidden[row:row + r.shape[0]] = r[...]
        row += r.shape[0]


def down_kernel(n_h, *refs):
    h_refs, w_ref, out_ref, hidden = refs[:n_h], refs[n_h], refs[-2], refs[-1]

    @pl.when(pl.program_id(0) == 0)
    def _():
        put_rows(h_refs, hidden)

    out_ref[...] = jnp.dot(hidden[...], w_ref[...], preferred_element_type=F32)


def down(hidden, down_weight, after, start):
    live = sum(h.shape[0] for h in hidden)
    width = hidden[0].shape[1]
    out_width = down_weight.shape[1]
    tile = min(out_width, 512)
    weight = pl.BlockSpec((pl.Element(width), pl.Element(tile)), lambda j: (start, j * tile))
    return pl.pallas_call(
        functools.partial(down_kernel, len(hidden)),
        out_shape=jax.ShapeDtypeStruct((live, out_width), F32),
        grid=(out_width // tile,),
        in_specs=[pl.BlockSpec(h.shape, lambda j: (0, 0)) for h in hidden]
        + [weight]
        + [pl.BlockSpec(memory_space=pl.ANY)] * len(after),
        out_specs=pl.BlockSpec((live, tile), lambda j: (0, j)),
        scratch_shapes=[pltpu.VMEM((live, width), BF16)],
        compiler_params=pltpu.CompilerParams(vmem_limit_bytes=28 * MIB),
        cost_estimate=pl.CostEstimate(flops=0, bytes_accessed=0, transcendentals=0),
        name="down",
    )(*hidden, down_weight, *after)


def fetch_kernel(starts, src_ref, *refs):
    outs, sems = refs[-1 - len(starts):-1], refs[-1]
    copies = [
        pltpu.make_async_copy(src_ref.at[pl.ds(start, out.shape[0])], out, sems.at[i])
        for i, (start, out) in enumerate(zip(starts, outs))
    ]
    for copy in copies:
        copy.start()
    for copy in copies:
        copy.wait()


def fetch(down_weight, chunks, after):
    held, anywhere = pl.BlockSpec(memory_space=pltpu.VMEM), pl.BlockSpec(memory_space=pl.ANY)
    return pl.pallas_call(
        functools.partial(fetch_kernel, [start for start, _ in chunks]),
        out_shape=[jax.ShapeDtypeStruct((width, down_weight.shape[1]), BF16) for _, width in chunks],
        in_specs=[anywhere] * (1 + len(after)),
        out_specs=[held] * len(chunks),
        scratch_shapes=[pltpu.SemaphoreType.DMA((len(chunks),))],
        compiler_params=pltpu.CompilerParams(vmem_limit_bytes=28 * MIB),
        cost_estimate=pl.CostEstimate(flops=0, bytes_accessed=0, transcendentals=0),
        name="fetch",
    )(down_weight, *after)


def down_held_kernel(n_h, last, tile, *refs):
    h_refs, w_ref, total_ref, outs, hidden = refs[:n_h], refs[n_h], refs[n_h + 1], refs[n_h + 2:-1], refs[-1]
    put_rows(h_refs, hidden)
    for j in range(0, total_ref.shape[1], tile):
        total = jnp.dot(hidden[...], w_ref[:, j:j + tile], preferred_element_type=F32) + total_ref[:, j:j + tile]
        if not last:
            outs[0][:, j:j + tile] = total
            continue
        pick_ref = outs[0]
        spread = jnp.dot(pick_ref[...], total.astype(BF16), preferred_element_type=F32).astype(BF16)
        row = 0
        for out_ref in outs[1:]:
            n = out_ref.shape[0]
            out_ref[:, j:j + tile] = spread[row:row + n]
            row += n


def down_held(hidden, weight_held, total, pick, out_rows):
    live, out_width = total.shape
    held = pl.BlockSpec(memory_space=pltpu.VMEM)
    last = pick is not None
    if last:
        out_shape = [jax.ShapeDtypeStruct((n, out_width), BF16) for n in out_rows]
    else:
        out_shape = jax.ShapeDtypeStruct((live, out_width), F32)
    return pl.pallas_call(
        functools.partial(down_held_kernel, len(hidden), last, min(out_width, 512)),
        out_shape=out_shape,
        in_specs=[held] * (len(hidden) + (3 if last else 2)),
        out_specs=[held] * len(out_rows) if last else held,
        scratch_shapes=[pltpu.VMEM((live, hidden[0].shape[1]), BF16)],
        compiler_params=pltpu.CompilerParams(vmem_limit_bytes=12 * MIB),
        cost_estimate=pl.CostEstimate(flops=0, bytes_accessed=0, transcendentals=0),
        name="down_held",
    )(*hidden, weight_held, total, *([pick] if last else []))


def column_chunks(cols, tile):
    tiles = cols // tile
    shares = (3, 3, 4, 3)
    edges = [round(tiles * sum(shares[:i]) / sum(shares)) for i in range(len(shares) + 1)]
    return [(a * tile, (b - a) * tile) for a, b in zip(edges, edges[1:]) if b > a]


def local(n_gx, n_gy, tokens, gate_weight, up_weight, down_weight, lengths):
    nx = n_gy // 2
    tok_dev = tokens.shape[0]
    live = 3 * tok_dev * n_gx // 4
    cols = gate_weight.shape[1]
    tile = 512 if cols % 512 == 0 else 128
    chunks = column_chunks(cols, tile)
    line = n_gx == 4
    part = tok_dev // 2

    def over_z(block, k, among=range(n_gx)):
        return lax.ppermute(block, "gx", [(z, z ^ k) for z in among])

    def over_core(block):
        return lax.ppermute(block, "gy", [(i, i ^ 1) for i in range(n_gy)])

    def over_x(block, k):
        return lax.ppermute(block, "gy", [(i, (i + 2 * k) % n_gy) for i in range(n_gy)])

    far = [over_z(tokens, k) for k in range(1, n_gx)]
    pick_in, pick_out, held, weights = prepare(lengths, tokens, gate_weight, up_weight, chunks[:3], n_gx, nx, live)
    blocks = [held] + far
    tok = compact(pick_in, blocks)

    made = [gate_up_held(tok, *weights[i], [], nx, tile) for i in range(2)]
    sends, keeps = [list(a) for a in zip(*made)]
    sums = []

    def exchange(j, handed, after):
        mine, blocks, handed = join(keeps[j], [over_core(a) for a in sends[j]], handed, after, nx)
        sums.append([mine] + [over_x(b, k + 1) for k, b in enumerate(blocks)])
        return blocks, handed

    def finish(first, last, handed, after):
        own, handed = activate(sums[first:last], handed, after)
        return [own] + [over_x(own, -k) for k in range(1, nx)], handed

    def with_other_core(h):
        return h + [over_core(a) for a in h]

    ready, sends[1] = exchange(0, sends[1], [])
    ready = ready + exchange(1, [], [])[0]
    made = [gate_up_held(tok, *weights[2], ready, nx, tile, True)]
    made.append(gate_up(tok, gate_weight, up_weight, made[0][0][:1], *chunks[3], nx, tile))
    pieces = len(made[0][0])
    hidden, handed = finish(0, 2, made[0][0] + made[1][0], [])
    sends += [handed[:pieces], handed[pieces:]]
    keeps += [keep for _, keep in made]
    ready, sends[3] = exchange(2, sends[3], [])
    ready = ready + exchange(3, [], [])[0]
    rows_held = fetch(down_weight, chunks[2:], ready)
    total = down(with_other_core(hidden), down_weight, [rows_held[0]], chunks[0][0])
    hidden, _ = finish(2, 3, [], [total])
    total = down_held(with_other_core(hidden), rows_held[0], total, None, None)
    hidden, _ = finish(3, 4, [], [])
    hidden = with_other_core(hidden)
    out_rows = [tok_dev, part, part, tok_dev, tok_dev] if line else [tok_dev] * n_gx
    spread = down_held(hidden, rows_held[1], total, pick_out, out_rows)

    if line:
        own, low, high, two, three = spread
        ends = over_z(three, 1, (0, 3))
        middle = over_z(three, 3, (1, 2))
        two, near = relay(two, ends, [low, high], middle)
        far = over_z(two, 2)
        near = [over_z(a, 1) for a in near]
        parts = [own, jnp.concatenate(near, axis=0), far, middle]
    else:
        parts = [spread[0]] + [over_z(spread[k], k) for k in range(1, n_gx)]
    return sum(p.astype(F32) for p in parts).astype(BF16)


def solution(mesh):
    placed = (P(("group", "gx"), "gy"), P("gy", "gx"), P("gy", "gx"), P("gx", "gy"), P("group"))
    return jax.shard_map(
        functools.partial(local, mesh.shape["gx"], mesh.shape["gy"]),
        mesh=mesh, in_specs=placed, out_specs=P(("group", "gx"), "gy"), check_vma=False,
    )
```

```python
import functools

import jax
import jax.numpy as jnp
from jax import lax
from jax.experimental import pallas as pl
from jax.experimental.pallas import tpu as pltpu
from jax.sharding import PartitionSpec as P

MIB = 1 << 20
BF16, F32 = jnp.bfloat16, jnp.float32


def row_sources(lengths_ref, rows, n_gx, tok_dev):
    start = jnp.int32(0)
    slot = rows
    for g in range(n_gx):
        slot = jnp.where(rows >= start, rows - start + g * tok_dev, slot)
        start = start + lengths_ref[g]
    return slot


def local_rows(shape, dim, quarter, nx):
    gy = lax.axis_index("gy")
    x, core = gy // 2, gy % 2
    j = lax.broadcasted_iota(jnp.int32, shape, dim)
    rows = jnp.zeros(shape, jnp.int32)
    for kc in range(2):
        for kx in range(nx):
            first = (kc * nx + kx) * quarter
            owner = lax.rem(x + kx, nx) * 2 + (1 - core if kc else core)
            rows = jnp.where(j >= first, owner * quarter + j - first, rows)
    return rows


def prepare_kernel(n_gx, nx, chunks, lengths_ref, tok_ref, gate_ref, up_ref, in_ref, out_ref, held_ref, *refs):
    outs, sems = refs[:-1], refs[-1]
    copies = []
    for i, (start, width) in enumerate(chunks):
        for k, src in enumerate((gate_ref, up_ref)):
            copies.append(pltpu.make_async_copy(src.at[:, pl.ds(start, width)], outs[2 * i + k], sems.at[2 * i + k]))
    for copy in copies:
        copy.start()
    held_ref[...] = tok_ref[...]
    tok_dev = tok_ref.shape[0]
    z = lax.axis_index("gx")
    live, slots = in_ref.shape
    quarter = live // (2 * nx)

    def slot_of(column):
        return (z ^ (column // tok_dev)) * tok_dev + column % tok_dev

    shape = (live, slots)
    source = row_sources(lengths_ref, local_rows(shape, 0, quarter, nx), n_gx, tok_dev)
    in_ref[...] = (source == slot_of(lax.broadcasted_iota(jnp.int32, shape, 1))).astype(F32).astype(BF16)
    shape = (slots, live)
    source = row_sources(lengths_ref, local_rows(shape, 1, quarter, nx), n_gx, tok_dev)
    out_ref[...] = (source == slot_of(lax.broadcasted_iota(jnp.int32, shape, 0))).astype(F32).astype(BF16)
    for copy in copies:
        copy.wait()


def prepare(lengths, tokens, gate_weight, up_weight, chunks, n_gx, nx, live):
    slots = n_gx * tokens.shape[0]
    held, anywhere = pl.BlockSpec(memory_space=pltpu.VMEM), pl.BlockSpec(memory_space=pl.ANY)
    weights = [jax.ShapeDtypeStruct((gate_weight.shape[0], width), BF16) for _, width in chunks for _ in range(2)]
    out = pl.pallas_call(
        functools.partial(prepare_kernel, n_gx, nx, chunks),
        out_shape=[
            jax.ShapeDtypeStruct((live, slots), BF16),
            jax.ShapeDtypeStruct((slots, live), BF16),
            jax.ShapeDtypeStruct(tokens.shape, tokens.dtype),
        ]
        + weights,
        in_specs=[pl.BlockSpec(memory_space=pltpu.SMEM), held, anywhere, anywhere],
        out_specs=[held] * (3 + len(weights)),
        scratch_shapes=[pltpu.SemaphoreType.DMA((len(weights),))],
        cost_estimate=pl.CostEstimate(flops=0, bytes_accessed=0, transcendentals=0),
        compiler_params=pltpu.CompilerParams(vmem_limit_bytes=4 * MIB),
        name="prepare",
    )(lengths, tokens, gate_weight, up_weight)
    return out[0], out[1], out[2], [out[3 + 2 * i:5 + 2 * i] for i in range(len(chunks))]


def compact_kernel(pick_ref, *refs):
    rows = jnp.concatenate([r[...] for r in refs[:-1]], axis=0)
    refs[-1][...] = jnp.dot(pick_ref[...], rows, preferred_element_type=F32).astype(BF16)


def compact(pick, blocks):
    return pl.pallas_call(
        compact_kernel,
        out_shape=jax.ShapeDtypeStruct((pick.shape[0], blocks[0].shape[1]), BF16),
        compiler_params=pltpu.CompilerParams(vmem_limit_bytes=5 * MIB),
        cost_estimate=pl.CostEstimate(flops=0, bytes_accessed=0, transcendentals=0),
        name="compact",
    )(pick, *blocks)


def send_shapes(half, nx, width, split):
    if split:
        return [jax.ShapeDtypeStruct((half // nx, width), BF16)] * (2 * nx)
    return [jax.ShapeDtypeStruct((2, half, width), BF16)]


def put_part(i, part, columns, keep_ref, send_refs):
    half = keep_ref.shape[1]
    keep_ref[i, :, columns] = part[:half]
    if len(send_refs) == 1:
        send_refs[0][i, :, columns] = part[half:].astype(BF16)
        return
    nx = len(send_refs) // 2
    quarter = half // nx
    for k in range(nx):
        first = half + k * quarter
        send_refs[i * nx + k][:, columns] = part[first:first + quarter].astype(BF16)


def gate_up_held_kernel(n_after, tile, tok_ref, gate_ref, up_ref, *refs):
    keep_ref, *send_refs = refs[n_after:]
    rows = tok_ref[...]
    for j in range(0, keep_ref.shape[2], tile):
        columns = slice(j, j + tile)
        for i, w_ref in enumerate((gate_ref, up_ref)):
            part = jnp.dot(rows, w_ref[:, columns], preferred_element_type=F32)
            put_part(i, part, columns, keep_ref, send_refs)


def gate_up_held(tok, gate_held, up_held, after, nx, tile, split=False):
    half, width = tok.shape[0] // 2, gate_held.shape[1]
    held, anywhere = pl.BlockSpec(memory_space=pltpu.VMEM), pl.BlockSpec(memory_space=pl.ANY)
    keep, *send = pl.pallas_call(
        functools.partial(gate_up_held_kernel, len(after), tile),
        out_shape=[jax.ShapeDtypeStruct((2, half, width), F32)] + send_shapes(half, nx, width, split),
        in_specs=[held] * 3 + [anywhere] * len(after),
        out_specs=[held] * (1 + (2 * nx if split else 1)),
        compiler_params=pltpu.CompilerParams(vmem_limit_bytes=6 * MIB),
        cost_estimate=pl.CostEstimate(flops=0, bytes_accessed=0, transcendentals=0),
        name="gate_up_held",
    )(tok, gate_held, up_held, *after)
    return send, keep


def gate_up_kernel(n_after, tok_ref, gate_ref, up_ref, *refs):
    keep_ref, *send_refs = refs[n_after:]
    rows = tok_ref[...]
    for i, w_ref in enumerate((gate_ref, up_ref)):
        part = jnp.dot(rows, w_ref[...], preferred_element_type=F32)
        put_part(i, part, slice(None), keep_ref, send_refs)


def gate_up(tok, gate_weight, up_weight, after, start, width, nx, tile):
    live, depth = tok.shape
    half = live // 2
    weight = pl.BlockSpec((depth, tile), lambda j: (0, start // tile + j))
    keep, *send = pl.pallas_call(
        functools.partial(gate_up_kernel, len(after)),
        out_shape=[jax.ShapeDtypeStruct((2, half, width), F32)] + send_shapes(half, nx, width, True),
        grid=(width // tile,),
        in_specs=[pl.BlockSpec((live, depth), lambda j: (0, 0)), weight, weight]
        + [pl.BlockSpec(memory_space=pl.ANY)] * len(after),
        out_specs=[pl.BlockSpec((2, half, tile), lambda j: (0, 0, j))]
        + [pl.BlockSpec((half // nx, tile), lambda j: (0, j))] * (2 * nx),
        compiler_params=pltpu.CompilerParams(vmem_limit_bytes=40 * MIB),
        cost_estimate=pl.CostEstimate(flops=0, bytes_accessed=0, transcendentals=0),
        name="gate_up",
    )(tok, gate_weight, up_weight, *after)
    return send, keep


def join_kernel(n_got, n_unread, nx, keep_ref, *refs):
    got_refs, out_refs = refs[:n_got], refs[n_got + n_unread:][:nx]
    quarter = out_refs[0].shape[1]
    for i in range(2):
        for k, out_ref in enumerate(out_refs):
            rows = pl.ds(k * quarter, quarter)
            got = got_refs[0][i, rows] if n_got == 1 else got_refs[i * nx + k][...]
            out_ref[i] = (keep_ref[i, rows] + got.astype(F32)).astype(out_ref.dtype)


def join(keep, got, handed, after, nx):
    two, half, width = keep.shape
    shape = (two, half // nx, width)
    held, anywhere = pl.BlockSpec(memory_space=pltpu.VMEM), pl.BlockSpec(memory_space=pl.ANY)
    out = pl.pallas_call(
        functools.partial(join_kernel, len(got), len(handed) + len(after), nx),
        out_shape=[jax.ShapeDtypeStruct(shape, BF16 if k else F32) for k in range(nx)]
        + [jax.ShapeDtypeStruct(a.shape, a.dtype) for a in handed],
        in_specs=[held] * (1 + len(got)) + [anywhere] * (len(handed) + len(after)),
        out_specs=[held] * nx + [anywhere] * len(handed),
        input_output_aliases={1 + len(got) + i: nx + i for i in range(len(handed))},
        compiler_params=pltpu.CompilerParams(vmem_limit_bytes=8 * MIB),
        cost_estimate=pl.CostEstimate(flops=0, bytes_accessed=0, transcendentals=0),
        name="join",
    )(keep, *got, *handed, *after)
    return out[0], list(out[1:nx]), list(out[nx:])


def activate_kernel(n_got, n_chunks, n_unread, *refs):
    own_ref = refs[n_chunks * (1 + n_got) + n_unread]
    column = 0
    for c in range(n_chunks):
        mine_ref, *got_refs = refs[c * (1 + n_got):(c + 1) * (1 + n_got)]
        both = mine_ref[...]
        for got_ref in got_refs:
            both = both + got_ref[...].astype(F32)
        gate, up = both[0], both[1]
        own_ref[:, column:column + gate.shape[1]] = (gate / (1.0 + jnp.exp(-gate)) * up).astype(BF16)
        column += gate.shape[1]


def activate(sums, handed, after):
    held, anywhere = pl.BlockSpec(memory_space=pltpu.VMEM), pl.BlockSpec(memory_space=pl.ANY)
    flat = [a for chunk in sums for a in chunk]
    width = sum(chunk[0].shape[2] for chunk in sums)
    out = pl.pallas_call(
        functools.partial(activate_kernel, len(sums[0]) - 1, len(sums), len(handed) + len(after)),
        out_shape=[jax.ShapeDtypeStruct((flat[0].shape[1], width), BF16)]
        + [jax.ShapeDtypeStruct(a.shape, a.dtype) for a in handed],
        in_specs=[held] * len(flat) + [anywhere] * (len(handed) + len(after)),
        out_specs=[held] + [anywhere] * len(handed),
        input_output_aliases={len(flat) + i: 1 + i for i in range(len(handed))},
        compiler_params=pltpu.CompilerParams(vmem_limit_bytes=8 * MIB),
        cost_estimate=pl.CostEstimate(flops=0, bytes_accessed=0, transcendentals=0),
        name="activate",
    )(*flat, *handed, *after)
    return out[0], out[1:]


def relay_kernel(n_unread, own_ref, got_ref, *refs):
    out_ref = refs[n_unread]
    out_ref[...] = (own_ref[...].astype(F32) + got_ref[...].astype(F32)).astype(BF16)


def relay(own, got, handed, after):
    held, anywhere = pl.BlockSpec(memory_space=pltpu.VMEM), pl.BlockSpec(memory_space=pl.ANY)
    out = pl.pallas_call(
        functools.partial(relay_kernel, len(handed) + len(after)),
        out_shape=[jax.ShapeDtypeStruct(a.shape, a.dtype) for a in (own, *handed)],
        in_specs=[held, held] + [anywhere] * (len(handed) + len(after)),
        out_specs=[held] + [anywhere] * len(handed),
        input_output_aliases={2 + i: 1 + i for i in range(len(handed))},
        compiler_params=pltpu.CompilerParams(vmem_limit_bytes=8 * MIB),
        cost_estimate=pl.CostEstimate(flops=0, bytes_accessed=0, transcendentals=0),
        name="relay",
    )(own, got, *handed, *after)
    return out[0], out[1:]


def put_rows(h_refs, hidden):
    row = 0
    for r in h_refs:
        hidden[row:row + r.shape[0]] = r[...]
        row += r.shape[0]


def down_kernel(n_h, *refs):
    h_refs, w_ref, out_ref, hidden = refs[:n_h], refs[n_h], refs[-2], refs[-1]

    @pl.when(pl.program_id(0) == 0)
    def _():
        put_rows(h_refs, hidden)

    out_ref[...] = jnp.dot(hidden[...], w_ref[...], preferred_element_type=F32)


def down(hidden, down_weight, after, start):
    live = sum(h.shape[0] for h in hidden)
    width = hidden[0].shape[1]
    out_width = down_weight.shape[1]
    tile = min(out_width, 512)
    weight = pl.BlockSpec((pl.Element(width), pl.Element(tile)), lambda j: (start, j * tile))
    return pl.pallas_call(
        functools.partial(down_kernel, len(hidden)),
        out_shape=jax.ShapeDtypeStruct((live, out_width), F32),
        grid=(out_width // tile,),
        in_specs=[pl.BlockSpec(h.shape, lambda j: (0, 0)) for h in hidden]
        + [weight]
        + [pl.BlockSpec(memory_space=pl.ANY)] * len(after),
        out_specs=pl.BlockSpec((live, tile), lambda j: (0, j)),
        scratch_shapes=[pltpu.VMEM((live, width), BF16)],
        compiler_params=pltpu.CompilerParams(vmem_limit_bytes=28 * MIB),
        cost_estimate=pl.CostEstimate(flops=0, bytes_accessed=0, transcendentals=0),
        name="down",
    )(*hidden, down_weight, *after)


def fetch_kernel(starts, src_ref, *refs):
    outs, sems = refs[-1 - len(starts):-1], refs[-1]
    copies = [
        pltpu.make_async_copy(src_ref.at[pl.ds(start, out.shape[0])], out, sems.at[i])
        for i, (start, out) in enumerate(zip(starts, outs))
    ]
    for copy in copies:
        copy.start()
    for copy in copies:
        copy.wait()


def fetch(down_weight, chunks, after):
    held, anywhere = pl.BlockSpec(memory_space=pltpu.VMEM), pl.BlockSpec(memory_space=pl.ANY)
    return pl.pallas_call(
        functools.partial(fetch_kernel, [start for start, _ in chunks]),
        out_shape=[jax.ShapeDtypeStruct((width, down_weight.shape[1]), BF16) for _, width in chunks],
        in_specs=[anywhere] * (1 + len(after)),
        out_specs=[held] * len(chunks),
        scratch_shapes=[pltpu.SemaphoreType.DMA((len(chunks),))],
        compiler_params=pltpu.CompilerParams(vmem_limit_bytes=28 * MIB),
        cost_estimate=pl.CostEstimate(flops=0, bytes_accessed=0, transcendentals=0),
        name="fetch",
    )(down_weight, *after)


def down_held_kernel(n_h, last, out_rows, tile, *refs):
    h_refs, w_ref, total_ref, outs, hidden = refs[:n_h], refs[n_h], refs[n_h + 1], refs[n_h + 2:-1], refs[-1]
    put_rows(h_refs, hidden)
    for j in range(0, total_ref.shape[1], tile):
        total = jnp.dot(hidden[...], w_ref[:, j:j + tile], preferred_element_type=F32) + total_ref[:, j:j + tile]
        if not last:
            outs[0][:, j:j + tile] = total
            continue
        pick_ref = outs[0]
        spread = jnp.dot(pick_ref[...], total.astype(BF16), preferred_element_type=F32).astype(BF16)
        for row, out_ref in zip(out_rows, outs[1:]):
            out_ref[:, j:j + tile] = spread[row:row + out_ref.shape[0]]


def down_held(hidden, weight_held, total, pick, out_rows):
    live, out_width = total.shape
    held = pl.BlockSpec(memory_space=pltpu.VMEM)
    last = pick is not None
    if last:
        out_shape = [jax.ShapeDtypeStruct((n, out_width), BF16) for _, n in out_rows]
    else:
        out_shape = jax.ShapeDtypeStruct((live, out_width), F32)
    return pl.pallas_call(
        functools.partial(down_held_kernel, len(hidden), last, [row for row, _ in out_rows or []], min(out_width, 512)),
        out_shape=out_shape,
        in_specs=[held] * (len(hidden) + (3 if last else 2)),
        out_specs=[held] * len(out_rows) if last else held,
        scratch_shapes=[pltpu.VMEM((live, hidden[0].shape[1]), BF16)],
        compiler_params=pltpu.CompilerParams(vmem_limit_bytes=12 * MIB),
        cost_estimate=pl.CostEstimate(flops=0, bytes_accessed=0, transcendentals=0),
        name="down_held",
    )(*hidden, weight_held, total, *([pick] if last else []))


def column_chunks(cols, tile):
    tiles = cols // tile
    shares = (3, 3, 4, 3)
    edges = [round(tiles * sum(shares[:i]) / sum(shares)) for i in range(len(shares) + 1)]
    return [(a * tile, (b - a) * tile) for a, b in zip(edges, edges[1:]) if b > a]


def local(n_gx, n_gy, tokens, gate_weight, up_weight, down_weight, lengths):
    nx = n_gy // 2
    tok_dev = tokens.shape[0]
    live = 3 * tok_dev * n_gx // 4
    cols = gate_weight.shape[1]
    tile = 512 if cols % 512 == 0 else 128
    chunks = column_chunks(cols, tile)
    line = n_gx == 4
    part = tok_dev // 2

    def over_z(block, k, among=range(n_gx)):
        return lax.ppermute(block, "gx", [(z, z ^ k) for z in among])

    def over_core(block):
        return lax.ppermute(block, "gy", [(i, i ^ 1) for i in range(n_gy)])

    def over_x(block, k):
        return lax.ppermute(block, "gy", [(i, (i + 2 * k) % n_gy) for i in range(n_gy)])

    far = [over_z(tokens, k) for k in range(1, n_gx)]
    pick_in, pick_out, held, weights = prepare(lengths, tokens, gate_weight, up_weight, chunks[:3], n_gx, nx, live)
    blocks = [held] + far
    tok = compact(pick_in, blocks)

    made = [gate_up_held(tok, *weights[i], [], nx, tile) for i in range(2)]
    sends, keeps = [list(a) for a in zip(*made)]
    sums = []

    def exchange(j, handed, after):
        mine, blocks, handed = join(keeps[j], [over_core(a) for a in sends[j]], handed, after, nx)
        sums.append([mine] + [over_x(b, k + 1) for k, b in enumerate(blocks)])
        return blocks, handed

    def finish(first, last, handed, after):
        own, handed = activate(sums[first:last], handed, after)
        return [own] + [over_x(own, -k) for k in range(1, nx)], handed

    def with_other_core(h):
        return h + [over_core(a) for a in h]

    ready, sends[1] = exchange(0, sends[1], [])
    ready = ready + exchange(1, [], [])[0]
    made = [gate_up_held(tok, *weights[2], ready, nx, tile, True)]
    made.append(gate_up(tok, gate_weight, up_weight, made[0][0][:1], *chunks[3], nx, tile))
    pieces = len(made[0][0])
    hidden, handed = finish(0, 2, made[0][0] + made[1][0], [])
    sends += [handed[:pieces], handed[pieces:]]
    keeps += [keep for _, keep in made]
    rows_held = fetch(down_weight, chunks[2:], hidden[:1])
    _, sends[3] = exchange(2, sends[3], [rows_held[0]])
    ready, _ = exchange(3, [], [])
    total = down(with_other_core(hidden), down_weight, ready, chunks[0][0])
    hidden, _ = finish(2, 3, [], [total])
    total = down_held(with_other_core(hidden), rows_held[0], total, None, None)
    hidden, _ = finish(3, 4, [], [])
    hidden = with_other_core(hidden)
    out_rows = [(k * tok_dev, tok_dev) for k in range(n_gx)]
    if line:
        halves = [(row, part) for row in range(tok_dev, n_gx * tok_dev, part)]
        out_rows = out_rows[:1] + out_rows[3:] + halves
    spread = down_held(hidden, rows_held[1], total, pick_out, out_rows)

    if line:
        own, three, *halves = spread
        ends = [over_z(piece, 1, (0, 3)) for piece in halves[4:]]
        middle = over_z(three, 3, (1, 2))
        low, _ = relay(halves[2], ends[0], [], [])
        high, near = relay(halves[3], ends[1], halves[:2], [middle])
        far = jnp.concatenate([over_z(low, 2), over_z(high, 2)], axis=0)
        near = jnp.concatenate([over_z(piece, 1) for piece in near], axis=0)
        parts = [own, near, far, middle]
    else:
        parts = [spread[0]] + [over_z(spread[k], k) for k in range(1, n_gx)]
    return sum(p.astype(F32) for p in parts).astype(BF16)


def solution(mesh):
    placed = (P(("group", "gx"), "gy"), P("gy", "gx"), P("gy", "gx"), P("gx", "gy"), P("group"))
    return jax.shard_map(
        functools.partial(local, mesh.shape["gx"], mesh.shape["gy"]),
        mesh=mesh, in_specs=placed, out_specs=P(("group", "gx"), "gy"), check_vma=False,
    )
```

```python
import functools

import jax
import jax.numpy as jnp
from jax import lax
from jax.experimental import pallas as pl
from jax.experimental.pallas import tpu as pltpu
from jax.sharding import PartitionSpec as P

MIB = 1 << 20
BF16, F32 = jnp.bfloat16, jnp.float32


def row_sources(lengths_ref, rows, n_gx, tok_dev):
    start = jnp.int32(0)
    slot = rows
    for g in range(n_gx):
        slot = jnp.where(rows >= start, rows - start + g * tok_dev, slot)
        start = start + lengths_ref[g]
    return slot


def local_rows(shape, dim, quarter, nx):
    gy = lax.axis_index("gy")
    x, core = gy // 2, gy % 2
    j = lax.broadcasted_iota(jnp.int32, shape, dim)
    rows = jnp.zeros(shape, jnp.int32)
    for kc in range(2):
        for kx in range(nx):
            first = (kc * nx + kx) * quarter
            owner = lax.rem(x + kx, nx) * 2 + (1 - core if kc else core)
            rows = jnp.where(j >= first, owner * quarter + j - first, rows)
    return rows


def gathered_block(k):
    return k ^ (k >> 1)


def prepare_kernel(n_gx, nx, chunks, lengths_ref, tok_ref, gate_ref, up_ref, in_ref, out_ref, held_ref, *refs):
    outs, sems = refs[:-1], refs[-1]
    copies = []
    for i, (start, width) in enumerate(chunks):
        for k, src in enumerate((gate_ref, up_ref)):
            copies.append(pltpu.make_async_copy(src.at[:, pl.ds(start, width)], outs[2 * i + k], sems.at[2 * i + k]))
    for copy in copies:
        copy.start()
    held_ref[...] = tok_ref[...]
    tok_dev = tok_ref.shape[0]
    z = lax.axis_index("gx")
    live, slots = in_ref.shape
    quarter = live // (2 * nx)

    def slot_of(column, block_of):
        return (z ^ block_of(column // tok_dev)) * tok_dev + column % tok_dev

    shape = (live, slots)
    source = row_sources(lengths_ref, local_rows(shape, 0, quarter, nx), n_gx, tok_dev)
    slot = slot_of(lax.broadcasted_iota(jnp.int32, shape, 1), gathered_block)
    in_ref[...] = (source == slot).astype(F32).astype(BF16)
    shape = (slots, live)
    source = row_sources(lengths_ref, local_rows(shape, 1, quarter, nx), n_gx, tok_dev)
    slot = slot_of(lax.broadcasted_iota(jnp.int32, shape, 0), lambda k: k)
    out_ref[...] = (source == slot).astype(F32).astype(BF16)
    for copy in copies:
        copy.wait()


def prepare(lengths, tokens, gate_weight, up_weight, chunks, n_gx, nx, live):
    slots = n_gx * tokens.shape[0]
    held, anywhere = pl.BlockSpec(memory_space=pltpu.VMEM), pl.BlockSpec(memory_space=pl.ANY)
    weights = [jax.ShapeDtypeStruct((gate_weight.shape[0], width), BF16) for _, width in chunks for _ in range(2)]
    out = pl.pallas_call(
        functools.partial(prepare_kernel, n_gx, nx, chunks),
        out_shape=[
            jax.ShapeDtypeStruct((live, slots), BF16),
            jax.ShapeDtypeStruct((slots, live), BF16),
            jax.ShapeDtypeStruct(tokens.shape, tokens.dtype),
        ]
        + weights,
        in_specs=[pl.BlockSpec(memory_space=pltpu.SMEM), held, anywhere, anywhere],
        out_specs=[held] * (3 + len(weights)),
        scratch_shapes=[pltpu.SemaphoreType.DMA((len(weights),))],
        cost_estimate=pl.CostEstimate(flops=0, bytes_accessed=0, transcendentals=0),
        compiler_params=pltpu.CompilerParams(vmem_limit_bytes=4 * MIB),
        name="prepare",
    )(lengths, tokens, gate_weight, up_weight)
    return out[0], out[1], out[2], [out[3 + 2 * i:5 + 2 * i] for i in range(len(chunks))]


def compact_kernel(pick_ref, *refs):
    rows = jnp.concatenate([r[...] for r in refs[:-1]], axis=0)
    refs[-1][...] = jnp.dot(pick_ref[...], rows, preferred_element_type=F32).astype(BF16)


def compact(pick, blocks):
    return pl.pallas_call(
        compact_kernel,
        out_shape=jax.ShapeDtypeStruct((pick.shape[0], blocks[0].shape[1]), BF16),
        compiler_params=pltpu.CompilerParams(vmem_limit_bytes=5 * MIB),
        cost_estimate=pl.CostEstimate(flops=0, bytes_accessed=0, transcendentals=0),
        name="compact",
    )(pick, *blocks)


def send_shapes(half, nx, width, split):
    if split:
        return [jax.ShapeDtypeStruct((half // nx, width), BF16)] * (2 * nx)
    return [jax.ShapeDtypeStruct((2, half, width), BF16)]


def put_part(i, part, columns, keep_ref, send_refs):
    half = keep_ref.shape[1]
    keep_ref[i, :, columns] = part[:half]
    if len(send_refs) == 1:
        send_refs[0][i, :, columns] = part[half:].astype(BF16)
        return
    nx = len(send_refs) // 2
    quarter = half // nx
    for k in range(nx):
        first = half + k * quarter
        send_refs[i * nx + k][:, columns] = part[first:first + quarter].astype(BF16)


def gate_up_held_kernel(n_after, tile, tok_ref, gate_ref, up_ref, *refs):
    keep_ref, *send_refs = refs[n_after:]
    rows = tok_ref[...]
    for j in range(0, keep_ref.shape[2], tile):
        columns = slice(j, j + tile)
        for i, w_ref in enumerate((gate_ref, up_ref)):
            part = jnp.dot(rows, w_ref[:, columns], preferred_element_type=F32)
            put_part(i, part, columns, keep_ref, send_refs)


def gate_up_held(tok, gate_held, up_held, after, nx, tile):
    half, width = tok.shape[0] // 2, gate_held.shape[1]
    held, anywhere = pl.BlockSpec(memory_space=pltpu.VMEM), pl.BlockSpec(memory_space=pl.ANY)
    keep, *send = pl.pallas_call(
        functools.partial(gate_up_held_kernel, len(after), tile),
        out_shape=[jax.ShapeDtypeStruct((2, half, width), F32)] + send_shapes(half, nx, width, False),
        in_specs=[held] * 3 + [anywhere] * len(after),
        out_specs=[held] * 2,
        compiler_params=pltpu.CompilerParams(vmem_limit_bytes=6 * MIB),
        cost_estimate=pl.CostEstimate(flops=0, bytes_accessed=0, transcendentals=0),
        name="gate_up_held",
    )(tok, gate_held, up_held, *after)
    return send, keep


def gate_up_kernel(n_after, tok_ref, gate_ref, up_ref, *refs):
    keep_ref, *send_refs = refs[n_after:]
    rows = tok_ref[...]
    for i, w_ref in enumerate((gate_ref, up_ref)):
        part = jnp.dot(rows, w_ref[...], preferred_element_type=F32)
        put_part(i, part, slice(None), keep_ref, send_refs)


def gate_up(tok, gate_weight, up_weight, after, start, width, nx, tile):
    live, depth = tok.shape
    half = live // 2
    weight = pl.BlockSpec((depth, tile), lambda j: (0, start // tile + j))
    keep, *send = pl.pallas_call(
        functools.partial(gate_up_kernel, len(after)),
        out_shape=[jax.ShapeDtypeStruct((2, half, width), F32)] + send_shapes(half, nx, width, True),
        grid=(width // tile,),
        in_specs=[pl.BlockSpec((live, depth), lambda j: (0, 0)), weight, weight]
        + [pl.BlockSpec(memory_space=pl.ANY)] * len(after),
        out_specs=[pl.BlockSpec((2, half, tile), lambda j: (0, 0, j))]
        + [pl.BlockSpec((half // nx, tile), lambda j: (0, j))] * (2 * nx),
        compiler_params=pltpu.CompilerParams(vmem_limit_bytes=40 * MIB),
        cost_estimate=pl.CostEstimate(flops=0, bytes_accessed=0, transcendentals=0),
        name="gate_up",
    )(tok, gate_weight, up_weight, *after)
    return send, keep


def join_kernel(n_got, n_unread, nx, keep_ref, *refs):
    got_refs, out_refs = refs[:n_got], refs[n_got + n_unread:][:nx]
    quarter = out_refs[0].shape[1]
    for i in range(2):
        for k, out_ref in enumerate(out_refs):
            rows = pl.ds(k * quarter, quarter)
            got = got_refs[0][i, rows] if n_got == 1 else got_refs[i * nx + k][...]
            out_ref[i] = (keep_ref[i, rows] + got.astype(F32)).astype(out_ref.dtype)


def join(keep, got, handed, after, nx):
    two, half, width = keep.shape
    shape = (two, half // nx, width)
    held, anywhere = pl.BlockSpec(memory_space=pltpu.VMEM), pl.BlockSpec(memory_space=pl.ANY)
    out = pl.pallas_call(
        functools.partial(join_kernel, len(got), len(handed) + len(after), nx),
        out_shape=[jax.ShapeDtypeStruct(shape, BF16 if k else F32) for k in range(nx)]
        + [jax.ShapeDtypeStruct(a.shape, a.dtype) for a in handed],
        in_specs=[held] * (1 + len(got)) + [anywhere] * (len(handed) + len(after)),
        out_specs=[held] * nx + [anywhere] * len(handed),
        input_output_aliases={1 + len(got) + i: nx + i for i in range(len(handed))},
        compiler_params=pltpu.CompilerParams(vmem_limit_bytes=8 * MIB),
        cost_estimate=pl.CostEstimate(flops=0, bytes_accessed=0, transcendentals=0),
        name="join",
    )(keep, *got, *handed, *after)
    return out[0], list(out[1:nx]), list(out[nx:])


def activate_kernel(n_got, n_chunks, n_unread, *refs):
    own_ref = refs[n_chunks * (1 + n_got) + n_unread]
    column = 0
    for c in range(n_chunks):
        mine_ref, *got_refs = refs[c * (1 + n_got):(c + 1) * (1 + n_got)]
        both = mine_ref[...]
        for got_ref in got_refs:
            both = both + got_ref[...].astype(F32)
        gate, up = both[0], both[1]
        own_ref[:, column:column + gate.shape[1]] = (gate / (1.0 + jnp.exp(-gate)) * up).astype(BF16)
        column += gate.shape[1]


def activate(sums, handed, after):
    held, anywhere = pl.BlockSpec(memory_space=pltpu.VMEM), pl.BlockSpec(memory_space=pl.ANY)
    flat = [a for chunk in sums for a in chunk]
    width = sum(chunk[0].shape[2] for chunk in sums)
    out = pl.pallas_call(
        functools.partial(activate_kernel, len(sums[0]) - 1, len(sums), len(handed) + len(after)),
        out_shape=[jax.ShapeDtypeStruct((flat[0].shape[1], width), BF16)]
        + [jax.ShapeDtypeStruct(a.shape, a.dtype) for a in handed],
        in_specs=[held] * len(flat) + [anywhere] * (len(handed) + len(after)),
        out_specs=[held] + [anywhere] * len(handed),
        input_output_aliases={len(flat) + i: 1 + i for i in range(len(handed))},
        compiler_params=pltpu.CompilerParams(vmem_limit_bytes=8 * MIB),
        cost_estimate=pl.CostEstimate(flops=0, bytes_accessed=0, transcendentals=0),
        name="activate",
    )(*flat, *handed, *after)
    return out[0], out[1:]


def relay_kernel(n_unread, own_ref, got_ref, *refs):
    out_ref = refs[n_unread]
    out_ref[...] = (own_ref[...].astype(F32) + got_ref[...].astype(F32)).astype(BF16)


def relay(own, got, handed, after):
    held, anywhere = pl.BlockSpec(memory_space=pltpu.VMEM), pl.BlockSpec(memory_space=pl.ANY)
    out = pl.pallas_call(
        functools.partial(relay_kernel, len(handed) + len(after)),
        out_shape=[jax.ShapeDtypeStruct(a.shape, a.dtype) for a in (own, *handed)],
        in_specs=[held, held] + [anywhere] * (len(handed) + len(after)),
        out_specs=[held] + [anywhere] * len(handed),
        input_output_aliases={2 + i: 1 + i for i in range(len(handed))},
        compiler_params=pltpu.CompilerParams(vmem_limit_bytes=8 * MIB),
        cost_estimate=pl.CostEstimate(flops=0, bytes_accessed=0, transcendentals=0),
        name="relay",
    )(own, got, *handed, *after)
    return out[0], out[1:]


def put_rows(h_refs, hidden):
    row = 0
    for r in h_refs:
        hidden[row:row + r.shape[0]] = r[...]
        row += r.shape[0]


def down_kernel(n_h, *refs):
    h_refs, w_ref, out_ref, hidden = refs[:n_h], refs[n_h], refs[-2], refs[-1]

    @pl.when(pl.program_id(0) == 0)
    def _():
        put_rows(h_refs, hidden)

    out_ref[...] = jnp.dot(hidden[...], w_ref[...], preferred_element_type=F32)


def down(hidden, down_weight, after, start):
    live = sum(h.shape[0] for h in hidden)
    width = hidden[0].shape[1]
    out_width = down_weight.shape[1]
    tile = min(out_width, 512)
    weight = pl.BlockSpec((pl.Element(width), pl.Element(tile)), lambda j: (start, j * tile))
    return pl.pallas_call(
        functools.partial(down_kernel, len(hidden)),
        out_shape=jax.ShapeDtypeStruct((live, out_width), F32),
        grid=(out_width // tile,),
        in_specs=[pl.BlockSpec(h.shape, lambda j: (0, 0)) for h in hidden]
        + [weight]
        + [pl.BlockSpec(memory_space=pl.ANY)] * len(after),
        out_specs=pl.BlockSpec((live, tile), lambda j: (0, j)),
        scratch_shapes=[pltpu.VMEM((live, width), BF16)],
        compiler_params=pltpu.CompilerParams(vmem_limit_bytes=28 * MIB),
        cost_estimate=pl.CostEstimate(flops=0, bytes_accessed=0, transcendentals=0),
        name="down",
    )(*hidden, down_weight, *after)


def fetch_kernel(starts, src_ref, *refs):
    outs, sems = refs[-1 - len(starts):-1], refs[-1]
    copies = [
        pltpu.make_async_copy(src_ref.at[pl.ds(start, out.shape[0])], out, sems.at[i])
        for i, (start, out) in enumerate(zip(starts, outs))
    ]
    for copy in copies:
        copy.start()
    for copy in copies:
        copy.wait()


def fetch(down_weight, chunks, after):
    held, anywhere = pl.BlockSpec(memory_space=pltpu.VMEM), pl.BlockSpec(memory_space=pl.ANY)
    return pl.pallas_call(
        functools.partial(fetch_kernel, [start for start, _ in chunks]),
        out_shape=[jax.ShapeDtypeStruct((width, down_weight.shape[1]), BF16) for _, width in chunks],
        in_specs=[anywhere] * (1 + len(after)),
        out_specs=[held] * len(chunks),
        scratch_shapes=[pltpu.SemaphoreType.DMA((len(chunks),))],
        compiler_params=pltpu.CompilerParams(vmem_limit_bytes=28 * MIB),
        cost_estimate=pl.CostEstimate(flops=0, bytes_accessed=0, transcendentals=0),
        name="fetch",
    )(down_weight, *after)


def down_held_kernel(n_h, last, out_rows, tile, *refs):
    h_refs, w_ref, total_ref, outs, hidden = refs[:n_h], refs[n_h], refs[n_h + 1], refs[n_h + 2:-1], refs[-1]
    put_rows(h_refs, hidden)
    for j in range(0, total_ref.shape[1], tile):
        total = jnp.dot(hidden[...], w_ref[:, j:j + tile], preferred_element_type=F32) + total_ref[:, j:j + tile]
        if not last:
            outs[0][:, j:j + tile] = total
            continue
        pick_ref = outs[0]
        spread = jnp.dot(pick_ref[...], total.astype(BF16), preferred_element_type=F32).astype(BF16)
        for row, out_ref in zip(out_rows, outs[1:]):
            out_ref[:, j:j + tile] = spread[row:row + out_ref.shape[0]]


def down_held(hidden, weight_held, total, pick, out_rows):
    live, out_width = total.shape
    held = pl.BlockSpec(memory_space=pltpu.VMEM)
    last = pick is not None
    if last:
        out_shape = [jax.ShapeDtypeStruct((n, out_width), BF16) for _, n in out_rows]
    else:
        out_shape = jax.ShapeDtypeStruct((live, out_width), F32)
    return pl.pallas_call(
        functools.partial(down_held_kernel, len(hidden), last, [row for row, _ in out_rows or []], min(out_width, 512)),
        out_shape=out_shape,
        in_specs=[held] * (len(hidden) + (3 if last else 2)),
        out_specs=[held] * len(out_rows) if last else held,
        scratch_shapes=[pltpu.VMEM((live, hidden[0].shape[1]), BF16)],
        compiler_params=pltpu.CompilerParams(vmem_limit_bytes=12 * MIB),
        cost_estimate=pl.CostEstimate(flops=0, bytes_accessed=0, transcendentals=0),
        name="down_held",
    )(*hidden, weight_held, total, *([pick] if last else []))


def column_chunks(cols, tile):
    tiles = cols // tile
    shares = (3, 3, 4, 3)
    edges = [round(tiles * sum(shares[:i]) / sum(shares)) for i in range(len(shares) + 1)]
    return [(a * tile, (b - a) * tile) for a, b in zip(edges, edges[1:]) if b > a]


def local(n_gx, n_gy, tokens, gate_weight, up_weight, down_weight, lengths):
    nx = n_gy // 2
    tok_dev = tokens.shape[0]
    live = 3 * tok_dev * n_gx // 4
    cols = gate_weight.shape[1]
    tile = 512 if cols % 512 == 0 else 128
    chunks = column_chunks(cols, tile)
    line = n_gx == 4
    part = tok_dev // 2

    def over_z(block, k, among=range(n_gx)):
        return lax.ppermute(block, "gx", [(z, z ^ k) for z in among])

    def over_core(block):
        return lax.ppermute(block, "gy", [(i, i ^ 1) for i in range(n_gy)])

    def over_x(block, k):
        return lax.ppermute(block, "gy", [(i, (i + 2 * k) % n_gy) for i in range(n_gy)])

    far = [over_z(tokens, gathered_block(k)) for k in range(1, n_gx)]
    pick_in, pick_out, held, weights = prepare(lengths, tokens, gate_weight, up_weight, chunks[:3], n_gx, nx, live)
    blocks = [held] + far
    tok = compact(pick_in, blocks)

    made = [gate_up_held(tok, *weights[i], [], nx, tile) for i in range(2)]
    sends, keeps = [list(a) for a in zip(*made)]
    sums = []

    def exchange(j, handed, after):
        mine, blocks, handed = join(keeps[j], [over_core(a) for a in sends[j]], handed, after, nx)
        sums.append([mine] + [over_x(b, k + 1) for k, b in enumerate(blocks)])
        return blocks, handed

    def finish(first, last, handed, after):
        own, handed = activate(sums[first:last], handed, after)
        return [own] + [over_x(own, -k) for k in range(1, nx)], handed

    def with_other_core(h):
        return h + [over_core(a) for a in h]

    ready, sends[1] = exchange(0, sends[1], [])
    ready = ready + exchange(1, [], [])[0]
    made = [gate_up_held(tok, *weights[2], ready, nx, tile)]
    made.append(gate_up(tok, gate_weight, up_weight, made[0][0][:1], *chunks[3], nx, tile))
    pieces = len(made[0][0])
    hidden, handed = finish(0, 2, made[0][0] + made[1][0], [])
    sends += [handed[:pieces], handed[pieces:]]
    keeps += [keep for _, keep in made]
    rows_held = fetch(down_weight, chunks[2:], hidden[:1])
    _, sends[3] = exchange(2, sends[3], [rows_held[0]])
    ready, _ = exchange(3, [], [])
    total = down(with_other_core(hidden), down_weight, ready, chunks[0][0])
    hidden, _ = finish(2, 3, [], [total])
    total = down_held(with_other_core(hidden), rows_held[0], total, None, None)
    hidden, _ = finish(3, 4, [], [])
    hidden = with_other_core(hidden)
    out_rows = [(k * tok_dev, tok_dev) for k in range(n_gx)]
    if line:
        halves = [(row, part) for row in range(tok_dev, n_gx * tok_dev, part)]
        out_rows = out_rows[:1] + out_rows[3:] + halves
    spread = down_held(hidden, rows_held[1], total, pick_out, out_rows)

    if line:
        own, three, *halves = spread
        ends = [over_z(piece, 1, (0, 3)) for piece in halves[4:]]
        middle = over_z(three, 3, (1, 2))
        low, _ = relay(halves[2], ends[0], [], [])
        high, near = relay(halves[3], ends[1], halves[:2], [middle])
        far = jnp.concatenate([over_z(low, 2), over_z(high, 2)], axis=0)
        near = jnp.concatenate([over_z(piece, 1) for piece in near], axis=0)
        parts = [own, near, far, middle]
    else:
        parts = [spread[0]] + [over_z(spread[k], k) for k in range(1, n_gx)]
    return sum(p.astype(F32) for p in parts).astype(BF16)


def solution(mesh):
    placed = (P(("group", "gx"), "gy"), P("gy", "gx"), P("gy", "gx"), P("gx", "gy"), P("group"))
    return jax.shard_map(
        functools.partial(local, mesh.shape["gx"], mesh.shape["gy"]),
        mesh=mesh, in_specs=placed, out_specs=P(("group", "gx"), "gy"), check_vma=False,
    )
```

```python
import functools

import jax
import jax.numpy as jnp
from jax import lax
from jax.experimental import pallas as pl
from jax.experimental.pallas import tpu as pltpu
from jax.sharding import PartitionSpec as P

MIB = 1 << 20
BF16, F32 = jnp.bfloat16, jnp.float32


def row_sources(lengths_ref, rows, n_gx, tok_dev):
    start = jnp.int32(0)
    slot = rows
    for g in range(n_gx):
        slot = jnp.where(rows >= start, rows - start + g * tok_dev, slot)
        start = start + lengths_ref[g]
    return slot


def local_rows(shape, dim, quarter, nx):
    gy = lax.axis_index("gy")
    x, core = gy // 2, gy % 2
    j = lax.broadcasted_iota(jnp.int32, shape, dim)
    rows = jnp.zeros(shape, jnp.int32)
    for kc in range(2):
        for kx in range(nx):
            first = (kc * nx + kx) * quarter
            owner = lax.rem(x + kx, nx) * 2 + (1 - core if kc else core)
            rows = jnp.where(j >= first, owner * quarter + j - first, rows)
    return rows


def start_copies(chunks, gate_ref, up_ref, outs, sems):
    copies = []
    for i, (start, width) in enumerate(chunks):
        for k, src in enumerate((gate_ref, up_ref)):
            copies.append(pltpu.make_async_copy(src.at[:, pl.ds(start, width)], outs[2 * i + k], sems.at[2 * i + k]))
    for copy in copies:
        copy.start()
    return copies


def fetch_columns_kernel(n_after, chunk, gate_ref, up_ref, *refs):
    for copy in start_copies([chunk], gate_ref, up_ref, refs[n_after:-1], refs[-1]):
        copy.wait()


def fetch_columns(gate_weight, up_weight, chunk, after):
    held, anywhere = pl.BlockSpec(memory_space=pltpu.VMEM), pl.BlockSpec(memory_space=pl.ANY)
    return pl.pallas_call(
        functools.partial(fetch_columns_kernel, len(after), chunk),
        out_shape=[jax.ShapeDtypeStruct((gate_weight.shape[0], chunk[1]), BF16)] * 2,
        in_specs=[anywhere] * (2 + len(after)),
        out_specs=[held] * 2,
        scratch_shapes=[pltpu.SemaphoreType.DMA((2,))],
        cost_estimate=pl.CostEstimate(flops=0, bytes_accessed=0, transcendentals=0),
        compiler_params=pltpu.CompilerParams(vmem_limit_bytes=6 * MIB),
        name="fetch_columns",
    )(gate_weight, up_weight, *after)


def follow(handed, after):
    anywhere = pl.BlockSpec(memory_space=pl.ANY)
    return pl.pallas_call(
        lambda *refs: None,
        out_shape=jax.ShapeDtypeStruct(handed.shape, handed.dtype),
        in_specs=[anywhere] * (1 + len(after)),
        out_specs=anywhere,
        input_output_aliases={0: 0},
        compiler_params=pltpu.CompilerParams(vmem_limit_bytes=4 * MIB),
        cost_estimate=pl.CostEstimate(flops=0, bytes_accessed=0, transcendentals=0),
        name="follow",
    )(handed, *after)


def prepare_kernel(n_gx, nx, chunks, lengths_ref, tok_ref, gate_ref, up_ref, in_ref, out_ref, held_ref, *refs):
    copies = start_copies(chunks, gate_ref, up_ref, refs[:-1], refs[-1])
    held_ref[...] = tok_ref[...]
    tok_dev = tok_ref.shape[0]
    z = lax.axis_index("gx")
    live, slots = in_ref.shape
    quarter = live // (2 * nx)

    def slot_of(column):
        return (z ^ (column // tok_dev)) * tok_dev + column % tok_dev

    shape = (live, slots)
    source = row_sources(lengths_ref, local_rows(shape, 0, quarter, nx), n_gx, tok_dev)
    in_ref[...] = (source == slot_of(lax.broadcasted_iota(jnp.int32, shape, 1))).astype(F32).astype(BF16)
    shape = (slots, live)
    source = row_sources(lengths_ref, local_rows(shape, 1, quarter, nx), n_gx, tok_dev)
    out_ref[...] = (source == slot_of(lax.broadcasted_iota(jnp.int32, shape, 0))).astype(F32).astype(BF16)
    for copy in copies:
        copy.wait()


def prepare(lengths, tokens, gate_weight, up_weight, chunks, n_gx, nx, live):
    slots = n_gx * tokens.shape[0]
    held, anywhere = pl.BlockSpec(memory_space=pltpu.VMEM), pl.BlockSpec(memory_space=pl.ANY)
    weights = [jax.ShapeDtypeStruct((gate_weight.shape[0], width), BF16) for _, width in chunks for _ in range(2)]
    out = pl.pallas_call(
        functools.partial(prepare_kernel, n_gx, nx, chunks),
        out_shape=[
            jax.ShapeDtypeStruct((live, slots), BF16),
            jax.ShapeDtypeStruct((slots, live), BF16),
            jax.ShapeDtypeStruct(tokens.shape, tokens.dtype),
        ]
        + weights,
        in_specs=[pl.BlockSpec(memory_space=pltpu.SMEM), held, anywhere, anywhere],
        out_specs=[held] * (3 + len(weights)),
        scratch_shapes=[pltpu.SemaphoreType.DMA((len(weights),))],
        cost_estimate=pl.CostEstimate(flops=0, bytes_accessed=0, transcendentals=0),
        compiler_params=pltpu.CompilerParams(vmem_limit_bytes=4 * MIB),
        name="prepare",
    )(lengths, tokens, gate_weight, up_weight)
    return out[0], out[1], out[2], [out[3 + 2 * i:5 + 2 * i] for i in range(len(chunks))]


def compact_kernel(sizes, pick_ref, *refs):
    refs = list(refs)
    blocks = []
    for n in sizes:
        block = refs.pop(0)[...]
        for _ in range(n - 1):
            block = block + refs.pop(0)[...]
        blocks.append(block)
    rows = jnp.concatenate(blocks, axis=0)
    refs[-1][...] = jnp.dot(pick_ref[...], rows, preferred_element_type=F32).astype(BF16)


def compact(pick, blocks, after):
    held, anywhere = pl.BlockSpec(memory_space=pltpu.VMEM), pl.BlockSpec(memory_space=pl.ANY)
    flat = [b for block in blocks for b in block]
    return pl.pallas_call(
        functools.partial(compact_kernel, [len(block) for block in blocks]),
        out_shape=jax.ShapeDtypeStruct((pick.shape[0], flat[0].shape[1]), BF16),
        in_specs=[held] * (1 + len(flat)) + [anywhere] * len(after),
        out_specs=held,
        compiler_params=pltpu.CompilerParams(vmem_limit_bytes=5 * MIB),
        cost_estimate=pl.CostEstimate(flops=0, bytes_accessed=0, transcendentals=0),
        name="compact",
    )(pick, *flat, *after)


def send_shapes(half, nx, width, split):
    if split:
        return [jax.ShapeDtypeStruct((half // nx, width), BF16)] * (2 * nx)
    return [jax.ShapeDtypeStruct((2, half, width), BF16)]


def put_part(i, part, columns, keep_ref, send_refs):
    half = keep_ref.shape[1]
    keep_ref[i, :, columns] = part[:half]
    if len(send_refs) == 1:
        send_refs[0][i, :, columns] = part[half:].astype(BF16)
        return
    nx = len(send_refs) // 2
    quarter = half // nx
    for k in range(nx):
        first = half + k * quarter
        send_refs[i * nx + k][:, columns] = part[first:first + quarter].astype(BF16)


def gate_up_held_kernel(n_after, tile, tok_ref, gate_ref, up_ref, *refs):
    keep_ref, *send_refs = refs[n_after:]
    rows = tok_ref[...]
    for j in range(0, keep_ref.shape[2], tile):
        columns = slice(j, j + tile)
        for i, w_ref in enumerate((gate_ref, up_ref)):
            part = jnp.dot(rows, w_ref[:, columns], preferred_element_type=F32)
            put_part(i, part, columns, keep_ref, send_refs)


def gate_up_held(tok, gate_held, up_held, after, nx, tile):
    half, width = tok.shape[0] // 2, gate_held.shape[1]
    held, anywhere = pl.BlockSpec(memory_space=pltpu.VMEM), pl.BlockSpec(memory_space=pl.ANY)
    keep, *send = pl.pallas_call(
        functools.partial(gate_up_held_kernel, len(after), tile),
        out_shape=[jax.ShapeDtypeStruct((2, half, width), F32)] + send_shapes(half, nx, width, False),
        in_specs=[held] * 3 + [anywhere] * len(after),
        out_specs=[held] * 2,
        compiler_params=pltpu.CompilerParams(vmem_limit_bytes=6 * MIB),
        cost_estimate=pl.CostEstimate(flops=0, bytes_accessed=0, transcendentals=0),
        name="gate_up_held",
    )(tok, gate_held, up_held, *after)
    return send, keep


def gate_up_kernel(n_after, tok_ref, gate_ref, up_ref, *refs):
    keep_ref, *send_refs = refs[n_after:]
    rows = tok_ref[...]
    for i, w_ref in enumerate((gate_ref, up_ref)):
        part = jnp.dot(rows, w_ref[...], preferred_element_type=F32)
        put_part(i, part, slice(None), keep_ref, send_refs)


def gate_up(tok, gate_weight, up_weight, after, start, width, nx, tile):
    live, depth = tok.shape
    half = live // 2
    weight = pl.BlockSpec((depth, tile), lambda j: (0, start // tile + j))
    keep, *send = pl.pallas_call(
        functools.partial(gate_up_kernel, len(after)),
        out_shape=[jax.ShapeDtypeStruct((2, half, width), F32)] + send_shapes(half, nx, width, True),
        grid=(width // tile,),
        in_specs=[pl.BlockSpec((live, depth), lambda j: (0, 0)), weight, weight]
        + [pl.BlockSpec(memory_space=pl.ANY)] * len(after),
        out_specs=[pl.BlockSpec((2, half, tile), lambda j: (0, 0, j))]
        + [pl.BlockSpec((half // nx, tile), lambda j: (0, j))] * (2 * nx),
        compiler_params=pltpu.CompilerParams(vmem_limit_bytes=40 * MIB),
        cost_estimate=pl.CostEstimate(flops=0, bytes_accessed=0, transcendentals=0),
        name="gate_up",
    )(tok, gate_weight, up_weight, *after)
    return send, keep


def join_kernel(n_got, n_unread, nx, keep_ref, *refs):
    got_refs, out_refs = refs[:n_got], refs[n_got + n_unread:][:nx]
    quarter = out_refs[0].shape[1]
    for i in range(2):
        for k, out_ref in enumerate(out_refs):
            rows = pl.ds(k * quarter, quarter)
            got = got_refs[0][i, rows] if n_got == 1 else got_refs[i * nx + k][...]
            out_ref[i] = (keep_ref[i, rows] + got.astype(F32)).astype(out_ref.dtype)


def join(keep, got, handed, after, nx):
    two, half, width = keep.shape
    shape = (two, half // nx, width)
    held, anywhere = pl.BlockSpec(memory_space=pltpu.VMEM), pl.BlockSpec(memory_space=pl.ANY)
    out = pl.pallas_call(
        functools.partial(join_kernel, len(got), len(handed) + len(after), nx),
        out_shape=[jax.ShapeDtypeStruct(shape, BF16 if k else F32) for k in range(nx)]
        + [jax.ShapeDtypeStruct(a.shape, a.dtype) for a in handed],
        in_specs=[held] * (1 + len(got)) + [anywhere] * (len(handed) + len(after)),
        out_specs=[held] * nx + [anywhere] * len(handed),
        input_output_aliases={1 + len(got) + i: nx + i for i in range(len(handed))},
        compiler_params=pltpu.CompilerParams(vmem_limit_bytes=8 * MIB),
        cost_estimate=pl.CostEstimate(flops=0, bytes_accessed=0, transcendentals=0),
        name="join",
    )(keep, *got, *handed, *after)
    return out[0], list(out[1:nx]), list(out[nx:])


def activate_kernel(n_got, n_chunks, n_unread, *refs):
    own_ref = refs[n_chunks * (1 + n_got) + n_unread]
    column = 0
    for c in range(n_chunks):
        mine_ref, *got_refs = refs[c * (1 + n_got):(c + 1) * (1 + n_got)]
        both = mine_ref[...]
        for got_ref in got_refs:
            both = both + got_ref[...].astype(F32)
        gate, up = both[0], both[1]
        own_ref[:, column:column + gate.shape[1]] = (gate / (1.0 + jnp.exp(-gate)) * up).astype(BF16)
        column += gate.shape[1]


def activate(sums, handed, after):
    held, anywhere = pl.BlockSpec(memory_space=pltpu.VMEM), pl.BlockSpec(memory_space=pl.ANY)
    flat = [a for chunk in sums for a in chunk]
    width = sum(chunk[0].shape[2] for chunk in sums)
    out = pl.pallas_call(
        functools.partial(activate_kernel, len(sums[0]) - 1, len(sums), len(handed) + len(after)),
        out_shape=[jax.ShapeDtypeStruct((flat[0].shape[1], width), BF16)]
        + [jax.ShapeDtypeStruct(a.shape, a.dtype) for a in handed],
        in_specs=[held] * len(flat) + [anywhere] * (len(handed) + len(after)),
        out_specs=[held] + [anywhere] * len(handed),
        input_output_aliases={len(flat) + i: 1 + i for i in range(len(handed))},
        compiler_params=pltpu.CompilerParams(vmem_limit_bytes=8 * MIB),
        cost_estimate=pl.CostEstimate(flops=0, bytes_accessed=0, transcendentals=0),
        name="activate",
    )(*flat, *handed, *after)
    return out[0], out[1:]


def relay_kernel(n_unread, own_ref, got_ref, *refs):
    out_ref = refs[n_unread]
    out_ref[...] = (own_ref[...].astype(F32) + got_ref[...].astype(F32)).astype(BF16)


def relay(own, got, handed, after):
    held, anywhere = pl.BlockSpec(memory_space=pltpu.VMEM), pl.BlockSpec(memory_space=pl.ANY)
    out = pl.pallas_call(
        functools.partial(relay_kernel, len(handed) + len(after)),
        out_shape=[jax.ShapeDtypeStruct(a.shape, a.dtype) for a in (own, *handed)],
        in_specs=[held, held] + [anywhere] * (len(handed) + len(after)),
        out_specs=[held] + [anywhere] * len(handed),
        input_output_aliases={2 + i: 1 + i for i in range(len(handed))},
        compiler_params=pltpu.CompilerParams(vmem_limit_bytes=8 * MIB),
        cost_estimate=pl.CostEstimate(flops=0, bytes_accessed=0, transcendentals=0),
        name="relay",
    )(own, got, *handed, *after)
    return out[0], out[1:]


def put_rows(h_refs, hidden):
    row = 0
    for r in h_refs:
        hidden[row:row + r.shape[0]] = r[...]
        row += r.shape[0]


def down_kernel(n_h, *refs):
    h_refs, w_ref, out_ref, hidden = refs[:n_h], refs[n_h], refs[-2], refs[-1]

    @pl.when(pl.program_id(0) == 0)
    def _():
        put_rows(h_refs, hidden)

    out_ref[...] = jnp.dot(hidden[...], w_ref[...], preferred_element_type=F32)


def down(hidden, down_weight, after, start):
    live = sum(h.shape[0] for h in hidden)
    width = hidden[0].shape[1]
    out_width = down_weight.shape[1]
    tile = min(out_width, 512)
    weight = pl.BlockSpec((pl.Element(width), pl.Element(tile)), lambda j: (start, j * tile))
    return pl.pallas_call(
        functools.partial(down_kernel, len(hidden)),
        out_shape=jax.ShapeDtypeStruct((live, out_width), F32),
        grid=(out_width // tile,),
        in_specs=[pl.BlockSpec(h.shape, lambda j: (0, 0)) for h in hidden]
        + [weight]
        + [pl.BlockSpec(memory_space=pl.ANY)] * len(after),
        out_specs=pl.BlockSpec((live, tile), lambda j: (0, j)),
        scratch_shapes=[pltpu.VMEM((live, width), BF16)],
        compiler_params=pltpu.CompilerParams(vmem_limit_bytes=28 * MIB),
        cost_estimate=pl.CostEstimate(flops=0, bytes_accessed=0, transcendentals=0),
        name="down",
    )(*hidden, down_weight, *after)


def fetch_kernel(starts, src_ref, *refs):
    outs, sems = refs[-1 - len(starts):-1], refs[-1]
    copies = [
        pltpu.make_async_copy(src_ref.at[pl.ds(start, out.shape[0])], out, sems.at[i])
        for i, (start, out) in enumerate(zip(starts, outs))
    ]
    for copy in copies:
        copy.start()
    for copy in copies:
        copy.wait()


def fetch(down_weight, chunks, after):
    held, anywhere = pl.BlockSpec(memory_space=pltpu.VMEM), pl.BlockSpec(memory_space=pl.ANY)
    return pl.pallas_call(
        functools.partial(fetch_kernel, [start for start, _ in chunks]),
        out_shape=[jax.ShapeDtypeStruct((width, down_weight.shape[1]), BF16) for _, width in chunks],
        in_specs=[anywhere] * (1 + len(after)),
        out_specs=[held] * len(chunks),
        scratch_shapes=[pltpu.SemaphoreType.DMA((len(chunks),))],
        compiler_params=pltpu.CompilerParams(vmem_limit_bytes=28 * MIB),
        cost_estimate=pl.CostEstimate(flops=0, bytes_accessed=0, transcendentals=0),
        name="fetch",
    )(down_weight, *after)


def down_held_kernel(n_h, last, out_rows, tile, *refs):
    h_refs, w_ref, total_ref, outs, hidden = refs[:n_h], refs[n_h], refs[n_h + 1], refs[n_h + 2:-1], refs[-1]
    put_rows(h_refs, hidden)
    for j in range(0, total_ref.shape[1], tile):
        total = jnp.dot(hidden[...], w_ref[:, j:j + tile], preferred_element_type=F32) + total_ref[:, j:j + tile]
        if not last:
            outs[0][:, j:j + tile] = total
            continue
        pick_ref = outs[0]
        spread = jnp.dot(pick_ref[...], total.astype(BF16), preferred_element_type=F32).astype(BF16)
        for row, out_ref in zip(out_rows, outs[1:]):
            out_ref[:, j:j + tile] = spread[row:row + out_ref.shape[0]]


def down_held(hidden, weight_held, total, pick, out_rows):
    live, out_width = total.shape
    held = pl.BlockSpec(memory_space=pltpu.VMEM)
    last = pick is not None
    if last:
        out_shape = [jax.ShapeDtypeStruct((n, out_width), BF16) for _, n in out_rows]
    else:
        out_shape = jax.ShapeDtypeStruct((live, out_width), F32)
    return pl.pallas_call(
        functools.partial(down_held_kernel, len(hidden), last, [row for row, _ in out_rows or []], min(out_width, 512)),
        out_shape=out_shape,
        in_specs=[held] * (len(hidden) + (3 if last else 2)),
        out_specs=[held] * len(out_rows) if last else held,
        scratch_shapes=[pltpu.VMEM((live, hidden[0].shape[1]), BF16)],
        compiler_params=pltpu.CompilerParams(vmem_limit_bytes=12 * MIB),
        cost_estimate=pl.CostEstimate(flops=0, bytes_accessed=0, transcendentals=0),
        name="down_held",
    )(*hidden, weight_held, total, *([pick] if last else []))


def column_chunks(cols, tile):
    tiles = cols // tile
    shares = (3, 3, 4, 3)
    edges = [round(tiles * sum(shares[:i]) / sum(shares)) for i in range(len(shares) + 1)]
    return [(a * tile, (b - a) * tile) for a, b in zip(edges, edges[1:]) if b > a]


def local(n_gx, n_gy, tokens, gate_weight, up_weight, down_weight, lengths):
    nx = n_gy // 2
    tok_dev = tokens.shape[0]
    live = 3 * tok_dev * n_gx // 4
    cols = gate_weight.shape[1]
    tile = 512 if cols % 512 == 0 else 128
    chunks = column_chunks(cols, tile)
    line = n_gx == 4
    part = tok_dev // 2

    def over_z(block, k, among=range(n_gx)):
        return lax.ppermute(block, "gx", [(z, z ^ k) for z in among])

    def over_core(block):
        return lax.ppermute(block, "gy", [(i, i ^ 1) for i in range(n_gy)])

    def over_x(block, k):
        return lax.ppermute(block, "gy", [(i, (i + 2 * k) % n_gy) for i in range(n_gy)])

    pick_in, pick_out, held, weights = prepare(lengths, tokens, gate_weight, up_weight, chunks[:2], n_gx, nx, live)
    if line:
        two = over_z(tokens, 2)
        one = over_z(tokens, 1)
        middle = over_z(tokens, 3, (1, 2))
        two = follow(two, [pick_in])
        blocks = [[held], [one], [two], [middle, over_z(two, 1, (1, 2))]]
        ready = [two]
    else:
        blocks = [[held]] + [[over_z(tokens, k)] for k in range(1, n_gx)]
        ready = [pick_in]
    weights.append(fetch_columns(gate_weight, up_weight, chunks[2], ready))
    tok = compact(pick_in, blocks, weights[2][:1])

    made = [gate_up_held(tok, *weights[i], [], nx, tile) for i in range(2)]
    sends, keeps = [list(a) for a in zip(*made)]
    sums = []

    def exchange(j, handed, after):
        mine, blocks, handed = join(keeps[j], [over_core(a) for a in sends[j]], handed, after, nx)
        sums.append([mine] + [over_x(b, k + 1) for k, b in enumerate(blocks)])
        return blocks, handed

    def finish(first, last, handed, after):
        own, handed = activate(sums[first:last], handed, after)
        return [own] + [over_x(own, -k) for k in range(1, nx)], handed

    def with_other_core(h):
        return h + [over_core(a) for a in h]

    ready, sends[1] = exchange(0, sends[1], [])
    ready = ready + exchange(1, [], [])[0]
    made = [gate_up_held(tok, *weights[2], ready, nx, tile)]
    made.append(gate_up(tok, gate_weight, up_weight, made[0][0][:1], *chunks[3], nx, tile))
    pieces = len(made[0][0])
    hidden, handed = finish(0, 2, made[0][0] + made[1][0], [])
    sends += [handed[:pieces], handed[pieces:]]
    keeps += [keep for _, keep in made]
    rows_held = fetch(down_weight, chunks[2:], hidden[:1])
    _, sends[3] = exchange(2, sends[3], [rows_held[0]])
    ready, _ = exchange(3, [], [])
    total = down(with_other_core(hidden), down_weight, ready, chunks[0][0])
    hidden, _ = finish(2, 3, [], [total])
    total = down_held(with_other_core(hidden), rows_held[0], total, None, None)
    hidden, _ = finish(3, 4, [], [])
    hidden = with_other_core(hidden)
    out_rows = [(k * tok_dev, tok_dev) for k in range(n_gx)]
    if line:
        halves = [(row, part) for row in range(tok_dev, n_gx * tok_dev, part)]
        out_rows = out_rows[:1] + out_rows[3:] + halves
    spread = down_held(hidden, rows_held[1], total, pick_out, out_rows)

    if line:
        own, three, *halves = spread
        ends = [over_z(piece, 1, (0, 3)) for piece in halves[4:]]
        middle = over_z(three, 3, (1, 2))
        low, _ = relay(halves[2], ends[0], [], [])
        high, near = relay(halves[3], ends[1], halves[:2], [middle])
        far = jnp.concatenate([over_z(low, 2), over_z(high, 2)], axis=0)
        near = jnp.concatenate([over_z(piece, 1) for piece in near], axis=0)
        parts = [own, near, far, middle]
    else:
        parts = [spread[0]] + [over_z(spread[k], k) for k in range(1, n_gx)]
    return sum(p.astype(F32) for p in parts).astype(BF16)


def solution(mesh):
    placed = (P(("group", "gx"), "gy"), P("gy", "gx"), P("gy", "gx"), P("gx", "gy"), P("group"))
    return jax.shard_map(
        functools.partial(local, mesh.shape["gx"], mesh.shape["gy"]),
        mesh=mesh, in_specs=placed, out_specs=P(("group", "gx"), "gy"), check_vma=False,
    )
```

```python
import functools

import jax
import jax.numpy as jnp
from jax import lax
from jax.experimental import pallas as pl
from jax.experimental.pallas import tpu as pltpu
from jax.sharding import PartitionSpec as P

MIB = 1 << 20
BF16, F32 = jnp.bfloat16, jnp.float32


def row_sources(lengths_ref, rows, n_gx, tok_dev):
    start = jnp.int32(0)
    slot = rows
    for g in range(n_gx):
        slot = jnp.where(rows >= start, rows - start + g * tok_dev, slot)
        start = start + lengths_ref[g]
    return slot


def local_rows(shape, dim, quarter, nx):
    gy = lax.axis_index("gy")
    x, core = gy // 2, gy % 2
    j = lax.broadcasted_iota(jnp.int32, shape, dim)
    rows = jnp.zeros(shape, jnp.int32)
    for kc in range(2):
        for kx in range(nx):
            first = (kc * nx + kx) * quarter
            owner = lax.rem(x + kx, nx) * 2 + (1 - core if kc else core)
            rows = jnp.where(j >= first, owner * quarter + j - first, rows)
    return rows


def start_copies(chunks, gate_ref, up_ref, outs, sems):
    copies = []
    for i, (start, width) in enumerate(chunks):
        for k, src in enumerate((gate_ref, up_ref)):
            copies.append(pltpu.make_async_copy(src.at[:, pl.ds(start, width)], outs[2 * i + k], sems.at[2 * i + k]))
    for copy in copies:
        copy.start()
    return copies


def fetch_columns_kernel(n_after, chunk, gate_ref, up_ref, *refs):
    for copy in start_copies([chunk], gate_ref, up_ref, refs[n_after:-1], refs[-1]):
        copy.wait()


def fetch_columns(gate_weight, up_weight, chunk, after):
    held, anywhere = pl.BlockSpec(memory_space=pltpu.VMEM), pl.BlockSpec(memory_space=pl.ANY)
    return pl.pallas_call(
        functools.partial(fetch_columns_kernel, len(after), chunk),
        out_shape=[jax.ShapeDtypeStruct((gate_weight.shape[0], chunk[1]), BF16)] * 2,
        in_specs=[anywhere] * (2 + len(after)),
        out_specs=[held] * 2,
        scratch_shapes=[pltpu.SemaphoreType.DMA((2,))],
        cost_estimate=pl.CostEstimate(flops=0, bytes_accessed=0, transcendentals=0),
        compiler_params=pltpu.CompilerParams(vmem_limit_bytes=12 * MIB),
        name="fetch_columns",
    )(gate_weight, up_weight, *after)


def follow(handed, after):
    anywhere = pl.BlockSpec(memory_space=pl.ANY)
    return pl.pallas_call(
        lambda *refs: None,
        out_shape=jax.ShapeDtypeStruct(handed.shape, handed.dtype),
        in_specs=[anywhere] * (1 + len(after)),
        out_specs=anywhere,
        input_output_aliases={0: 0},
        compiler_params=pltpu.CompilerParams(vmem_limit_bytes=4 * MIB),
        cost_estimate=pl.CostEstimate(flops=0, bytes_accessed=0, transcendentals=0),
        name="follow",
    )(handed, *after)


def prepare_kernel(n_gx, nx, chunks, lengths_ref, tok_ref, gate_ref, up_ref, in_ref, out_ref, held_ref, *refs):
    copies = start_copies(chunks, gate_ref, up_ref, refs[:-1], refs[-1])
    held_ref[...] = tok_ref[...]
    tok_dev = tok_ref.shape[0]
    z = lax.axis_index("gx")
    live, slots = in_ref.shape
    quarter = live // (2 * nx)

    def slot_of(column):
        return (z ^ (column // tok_dev)) * tok_dev + column % tok_dev

    shape = (live, slots)
    source = row_sources(lengths_ref, local_rows(shape, 0, quarter, nx), n_gx, tok_dev)
    in_ref[...] = (source == slot_of(lax.broadcasted_iota(jnp.int32, shape, 1))).astype(F32).astype(BF16)
    shape = (slots, live)
    source = row_sources(lengths_ref, local_rows(shape, 1, quarter, nx), n_gx, tok_dev)
    out_ref[...] = (source == slot_of(lax.broadcasted_iota(jnp.int32, shape, 0))).astype(F32).astype(BF16)
    for copy in copies:
        copy.wait()


def prepare(lengths, tokens, gate_weight, up_weight, chunks, n_gx, nx, live):
    slots = n_gx * tokens.shape[0]
    held, anywhere = pl.BlockSpec(memory_space=pltpu.VMEM), pl.BlockSpec(memory_space=pl.ANY)
    weights = [jax.ShapeDtypeStruct((gate_weight.shape[0], width), BF16) for _, width in chunks for _ in range(2)]
    out = pl.pallas_call(
        functools.partial(prepare_kernel, n_gx, nx, chunks),
        out_shape=[
            jax.ShapeDtypeStruct((live, slots), BF16),
            jax.ShapeDtypeStruct((slots, live), BF16),
            jax.ShapeDtypeStruct(tokens.shape, tokens.dtype),
        ]
        + weights,
        in_specs=[pl.BlockSpec(memory_space=pltpu.SMEM), held, anywhere, anywhere],
        out_specs=[held] * (3 + len(weights)),
        scratch_shapes=[pltpu.SemaphoreType.DMA((len(weights),))],
        cost_estimate=pl.CostEstimate(flops=0, bytes_accessed=0, transcendentals=0),
        compiler_params=pltpu.CompilerParams(vmem_limit_bytes=4 * MIB),
        name="prepare",
    )(lengths, tokens, gate_weight, up_weight)
    return out[0], out[1], out[2], [out[3 + 2 * i:5 + 2 * i] for i in range(len(chunks))]


def compact_kernel(sizes, pick_ref, *refs):
    refs = list(refs)
    blocks = []
    for n in sizes:
        block = refs.pop(0)[...]
        for _ in range(n - 1):
            block = block + refs.pop(0)[...]
        blocks.append(block)
    rows = jnp.concatenate(blocks, axis=0)
    refs[-1][...] = jnp.dot(pick_ref[...], rows, preferred_element_type=F32).astype(BF16)


def compact(pick, blocks, after):
    held, anywhere = pl.BlockSpec(memory_space=pltpu.VMEM), pl.BlockSpec(memory_space=pl.ANY)
    flat = [b for block in blocks for b in block]
    return pl.pallas_call(
        functools.partial(compact_kernel, [len(block) for block in blocks]),
        out_shape=jax.ShapeDtypeStruct((pick.shape[0], flat[0].shape[1]), BF16),
        in_specs=[held] * (1 + len(flat)) + [anywhere] * len(after),
        out_specs=held,
        compiler_params=pltpu.CompilerParams(vmem_limit_bytes=5 * MIB),
        cost_estimate=pl.CostEstimate(flops=0, bytes_accessed=0, transcendentals=0),
        name="compact",
    )(pick, *flat, *after)


def send_shapes(half, nx, width, split):
    if split:
        return [jax.ShapeDtypeStruct((half // nx, width), BF16)] * (2 * nx)
    return [jax.ShapeDtypeStruct((2, half, width), BF16)]


def put_part(i, part, columns, keep_ref, send_refs):
    half = keep_ref.shape[1]
    keep_ref[i, :, columns] = part[:half]
    if len(send_refs) == 1:
        send_refs[0][i, :, columns] = part[half:].astype(BF16)
        return
    nx = len(send_refs) // 2
    quarter = half // nx
    for k in range(nx):
        first = half + k * quarter
        send_refs[i * nx + k][:, columns] = part[first:first + quarter].astype(BF16)


def gate_up_held_kernel(n_after, tile, tok_ref, gate_ref, up_ref, *refs):
    keep_ref, *send_refs = refs[n_after:]
    rows = tok_ref[...]
    for j in range(0, keep_ref.shape[2], tile):
        columns = slice(j, j + tile)
        for i, w_ref in enumerate((gate_ref, up_ref)):
            part = jnp.dot(rows, w_ref[:, columns], preferred_element_type=F32)
            put_part(i, part, columns, keep_ref, send_refs)


def gate_up_held(tok, gate_held, up_held, after, nx, tile):
    half, width = tok.shape[0] // 2, gate_held.shape[1]
    held, anywhere = pl.BlockSpec(memory_space=pltpu.VMEM), pl.BlockSpec(memory_space=pl.ANY)
    keep, *send = pl.pallas_call(
        functools.partial(gate_up_held_kernel, len(after), tile),
        out_shape=[jax.ShapeDtypeStruct((2, half, width), F32)] + send_shapes(half, nx, width, False),
        in_specs=[held] * 3 + [anywhere] * len(after),
        out_specs=[held] * 2,
        compiler_params=pltpu.CompilerParams(vmem_limit_bytes=6 * MIB),
        cost_estimate=pl.CostEstimate(flops=0, bytes_accessed=0, transcendentals=0),
        name="gate_up_held",
    )(tok, gate_held, up_held, *after)
    return send, keep


def gate_up_kernel(n_after, tok_ref, gate_ref, up_ref, *refs):
    keep_ref, *send_refs = refs[n_after:]
    rows = tok_ref[...]
    for i, w_ref in enumerate((gate_ref, up_ref)):
        part = jnp.dot(rows, w_ref[...], preferred_element_type=F32)
        put_part(i, part, slice(None), keep_ref, send_refs)


def gate_up(tok, gate_weight, up_weight, after, start, width, nx, tile):
    live, depth = tok.shape
    half = live // 2
    weight = pl.BlockSpec((depth, tile), lambda j: (0, start // tile + j))
    keep, *send = pl.pallas_call(
        functools.partial(gate_up_kernel, len(after)),
        out_shape=[jax.ShapeDtypeStruct((2, half, width), F32)] + send_shapes(half, nx, width, True),
        grid=(width // tile,),
        in_specs=[pl.BlockSpec((live, depth), lambda j: (0, 0)), weight, weight]
        + [pl.BlockSpec(memory_space=pl.ANY)] * len(after),
        out_specs=[pl.BlockSpec((2, half, tile), lambda j: (0, 0, j))]
        + [pl.BlockSpec((half // nx, tile), lambda j: (0, j))] * (2 * nx),
        compiler_params=pltpu.CompilerParams(vmem_limit_bytes=40 * MIB),
        cost_estimate=pl.CostEstimate(flops=0, bytes_accessed=0, transcendentals=0),
        name="gate_up",
    )(tok, gate_weight, up_weight, *after)
    return send, keep


def join_kernel(n_got, n_unread, nx, keep_ref, *refs):
    got_refs, out_refs = refs[:n_got], refs[n_got + n_unread:][:nx]
    quarter = out_refs[0].shape[1]
    for i in range(2):
        for k, out_ref in enumerate(out_refs):
            rows = pl.ds(k * quarter, quarter)
            got = got_refs[0][i, rows] if n_got == 1 else got_refs[i * nx + k][...]
            out_ref[i] = (keep_ref[i, rows] + got.astype(F32)).astype(out_ref.dtype)


def join(keep, got, handed, after, nx):
    two, half, width = keep.shape
    shape = (two, half // nx, width)
    held, anywhere = pl.BlockSpec(memory_space=pltpu.VMEM), pl.BlockSpec(memory_space=pl.ANY)
    out = pl.pallas_call(
        functools.partial(join_kernel, len(got), len(handed) + len(after), nx),
        out_shape=[jax.ShapeDtypeStruct(shape, BF16 if k else F32) for k in range(nx)]
        + [jax.ShapeDtypeStruct(a.shape, a.dtype) for a in handed],
        in_specs=[held] * (1 + len(got)) + [anywhere] * (len(handed) + len(after)),
        out_specs=[held] * nx + [anywhere] * len(handed),
        input_output_aliases={1 + len(got) + i: nx + i for i in range(len(handed))},
        compiler_params=pltpu.CompilerParams(vmem_limit_bytes=8 * MIB),
        cost_estimate=pl.CostEstimate(flops=0, bytes_accessed=0, transcendentals=0),
        name="join",
    )(keep, *got, *handed, *after)
    return out[0], list(out[1:nx]), list(out[nx:])


def activate_kernel(n_got, n_chunks, n_unread, *refs):
    own_ref = refs[n_chunks * (1 + n_got) + n_unread]
    column = 0
    for c in range(n_chunks):
        mine_ref, *got_refs = refs[c * (1 + n_got):(c + 1) * (1 + n_got)]
        both = mine_ref[...]
        for got_ref in got_refs:
            both = both + got_ref[...].astype(F32)
        gate, up = both[0], both[1]
        own_ref[:, column:column + gate.shape[1]] = (gate / (1.0 + jnp.exp(-gate)) * up).astype(BF16)
        column += gate.shape[1]


def activate(sums, handed, after):
    held, anywhere = pl.BlockSpec(memory_space=pltpu.VMEM), pl.BlockSpec(memory_space=pl.ANY)
    flat = [a for chunk in sums for a in chunk]
    width = sum(chunk[0].shape[2] for chunk in sums)
    out = pl.pallas_call(
        functools.partial(activate_kernel, len(sums[0]) - 1, len(sums), len(handed) + len(after)),
        out_shape=[jax.ShapeDtypeStruct((flat[0].shape[1], width), BF16)]
        + [jax.ShapeDtypeStruct(a.shape, a.dtype) for a in handed],
        in_specs=[held] * len(flat) + [anywhere] * (len(handed) + len(after)),
        out_specs=[held] + [anywhere] * len(handed),
        input_output_aliases={len(flat) + i: 1 + i for i in range(len(handed))},
        compiler_params=pltpu.CompilerParams(vmem_limit_bytes=8 * MIB),
        cost_estimate=pl.CostEstimate(flops=0, bytes_accessed=0, transcendentals=0),
        name="activate",
    )(*flat, *handed, *after)
    return out[0], out[1:]


def relay_kernel(n_unread, own_ref, got_ref, *refs):
    out_ref = refs[n_unread]
    out_ref[...] = (own_ref[...].astype(F32) + got_ref[...].astype(F32)).astype(BF16)


def relay(own, got, handed, after):
    held, anywhere = pl.BlockSpec(memory_space=pltpu.VMEM), pl.BlockSpec(memory_space=pl.ANY)
    out = pl.pallas_call(
        functools.partial(relay_kernel, len(handed) + len(after)),
        out_shape=[jax.ShapeDtypeStruct(a.shape, a.dtype) for a in (own, *handed)],
        in_specs=[held, held] + [anywhere] * (len(handed) + len(after)),
        out_specs=[held] + [anywhere] * len(handed),
        input_output_aliases={2 + i: 1 + i for i in range(len(handed))},
        compiler_params=pltpu.CompilerParams(vmem_limit_bytes=8 * MIB),
        cost_estimate=pl.CostEstimate(flops=0, bytes_accessed=0, transcendentals=0),
        name="relay",
    )(own, got, *handed, *after)
    return out[0], out[1:]


def put_rows(h_refs, hidden):
    row = 0
    for r in h_refs:
        hidden[row:row + r.shape[0]] = r[...]
        row += r.shape[0]


def down_kernel(n_h, *refs):
    h_refs, w_ref, out_ref, hidden = refs[:n_h], refs[n_h], refs[-2], refs[-1]

    @pl.when(pl.program_id(0) == 0)
    def _():
        put_rows(h_refs, hidden)

    out_ref[...] = jnp.dot(hidden[...], w_ref[...], preferred_element_type=F32)


def down(hidden, down_weight, after, start):
    live = sum(h.shape[0] for h in hidden)
    width = hidden[0].shape[1]
    out_width = down_weight.shape[1]
    tile = min(out_width, 512)
    weight = pl.BlockSpec((pl.Element(width), pl.Element(tile)), lambda j: (start, j * tile))
    return pl.pallas_call(
        functools.partial(down_kernel, len(hidden)),
        out_shape=jax.ShapeDtypeStruct((live, out_width), F32),
        grid=(out_width // tile,),
        in_specs=[pl.BlockSpec(h.shape, lambda j: (0, 0)) for h in hidden]
        + [weight]
        + [pl.BlockSpec(memory_space=pl.ANY)] * len(after),
        out_specs=pl.BlockSpec((live, tile), lambda j: (0, j)),
        scratch_shapes=[pltpu.VMEM((live, width), BF16)],
        compiler_params=pltpu.CompilerParams(vmem_limit_bytes=28 * MIB),
        cost_estimate=pl.CostEstimate(flops=0, bytes_accessed=0, transcendentals=0),
        name="down",
    )(*hidden, down_weight, *after)


def fetch_kernel(starts, src_ref, *refs):
    outs, sems = refs[-1 - len(starts):-1], refs[-1]
    copies = [
        pltpu.make_async_copy(src_ref.at[pl.ds(start, out.shape[0])], out, sems.at[i])
        for i, (start, out) in enumerate(zip(starts, outs))
    ]
    for copy in copies:
        copy.start()
    for copy in copies:
        copy.wait()


def fetch(down_weight, chunks, after):
    held, anywhere = pl.BlockSpec(memory_space=pltpu.VMEM), pl.BlockSpec(memory_space=pl.ANY)
    return pl.pallas_call(
        functools.partial(fetch_kernel, [start for start, _ in chunks]),
        out_shape=[jax.ShapeDtypeStruct((width, down_weight.shape[1]), BF16) for _, width in chunks],
        in_specs=[anywhere] * (1 + len(after)),
        out_specs=[held] * len(chunks),
        scratch_shapes=[pltpu.SemaphoreType.DMA((len(chunks),))],
        compiler_params=pltpu.CompilerParams(vmem_limit_bytes=28 * MIB),
        cost_estimate=pl.CostEstimate(flops=0, bytes_accessed=0, transcendentals=0),
        name="fetch",
    )(down_weight, *after)


def down_held_kernel(n_h, last, out_rows, tile, *refs):
    h_refs, w_ref, total_ref, outs, hidden = refs[:n_h], refs[n_h], refs[n_h + 1], refs[n_h + 2:-1], refs[-1]
    put_rows(h_refs, hidden)
    for j in range(0, total_ref.shape[1], tile):
        total = jnp.dot(hidden[...], w_ref[:, j:j + tile], preferred_element_type=F32) + total_ref[:, j:j + tile]
        if not last:
            outs[0][:, j:j + tile] = total
            continue
        pick_ref = outs[0]
        spread = jnp.dot(pick_ref[...], total.astype(BF16), preferred_element_type=F32).astype(BF16)
        for row, out_ref in zip(out_rows, outs[1:]):
            out_ref[:, j:j + tile] = spread[row:row + out_ref.shape[0]]


def down_held(hidden, weight_held, total, pick, out_rows):
    live, out_width = total.shape
    held = pl.BlockSpec(memory_space=pltpu.VMEM)
    last = pick is not None
    if last:
        out_shape = [jax.ShapeDtypeStruct((n, out_width), BF16) for _, n in out_rows]
    else:
        out_shape = jax.ShapeDtypeStruct((live, out_width), F32)
    return pl.pallas_call(
        functools.partial(down_held_kernel, len(hidden), last, [row for row, _ in out_rows or []], min(out_width, 512)),
        out_shape=out_shape,
        in_specs=[held] * (len(hidden) + (3 if last else 2)),
        out_specs=[held] * len(out_rows) if last else held,
        scratch_shapes=[pltpu.VMEM((live, hidden[0].shape[1]), BF16)],
        compiler_params=pltpu.CompilerParams(vmem_limit_bytes=12 * MIB),
        cost_estimate=pl.CostEstimate(flops=0, bytes_accessed=0, transcendentals=0),
        name="down_held",
    )(*hidden, weight_held, total, *([pick] if last else []))


def column_chunks(cols, tile):
    tiles = cols // tile
    shares = (3, 3, 4, 3)
    edges = [round(tiles * sum(shares[:i]) / sum(shares)) for i in range(len(shares) + 1)]
    return [(a * tile, (b - a) * tile) for a, b in zip(edges, edges[1:]) if b > a]


def local(n_gx, n_gy, tokens, gate_weight, up_weight, down_weight, lengths):
    nx = n_gy // 2
    tok_dev = tokens.shape[0]
    live = 3 * tok_dev * n_gx // 4
    cols = gate_weight.shape[1]
    tile = 512 if cols % 512 == 0 else 128
    chunks = column_chunks(cols, tile)
    line = n_gx == 4
    part = tok_dev // 2

    def over_z(block, k, among=range(n_gx)):
        return lax.ppermute(block, "gx", [(z, z ^ k) for z in among])

    def over_core(block):
        return lax.ppermute(block, "gy", [(i, i ^ 1) for i in range(n_gy)])

    def over_x(block, k):
        return lax.ppermute(block, "gy", [(i, (i + 2 * k) % n_gy) for i in range(n_gy)])

    pick_in, pick_out, held, weights = prepare(lengths, tokens, gate_weight, up_weight, chunks[:2], n_gx, nx, live)
    if line:
        two = over_z(tokens, 2)
        one = over_z(tokens, 1)
        middle = over_z(tokens, 3, (1, 2))
        two = follow(two, [pick_in])
        blocks = [[held], [one], [two], [middle, over_z(two, 1, (1, 2))]]
        ready = [two]
    else:
        blocks = [[held]] + [[over_z(tokens, k)] for k in range(1, n_gx)]
        ready = [pick_in]
    weights.append(fetch_columns(gate_weight, up_weight, chunks[2], ready))
    tok = compact(pick_in, blocks, weights[2][:1])

    made = [gate_up_held(tok, *weights[i], [], nx, tile) for i in range(2)]
    sends, keeps = [list(a) for a in zip(*made)]
    sums = []

    def exchange(j, handed, after):
        mine, blocks, handed = join(keeps[j], [over_core(a) for a in sends[j]], handed, after, nx)
        sums.append([mine] + [over_x(b, k + 1) for k, b in enumerate(blocks)])
        return blocks, handed

    def finish(first, last, handed, after):
        own, handed = activate(sums[first:last], handed, after)
        return [own] + [over_x(own, -k) for k in range(1, nx)], handed

    def with_other_core(h):
        return h + [over_core(a) for a in h]

    ready, sends[1] = exchange(0, sends[1], [])
    ready = ready + exchange(1, [], [])[0]
    made = [gate_up_held(tok, *weights[2], ready, nx, tile)]
    made.append(gate_up(tok, gate_weight, up_weight, made[0][0][:1], *chunks[3], nx, tile))
    pieces = len(made[0][0])
    hidden, handed = finish(0, 2, made[0][0] + made[1][0], [])
    sends += [handed[:pieces], handed[pieces:]]
    keeps += [keep for _, keep in made]
    rows_held = fetch(down_weight, chunks[2:], hidden[:1])
    _, sends[3] = exchange(2, sends[3], [rows_held[0]])
    ready, _ = exchange(3, [], [])
    total = down(with_other_core(hidden), down_weight, ready, chunks[0][0])
    hidden, _ = finish(2, 3, [], [total])
    total = down_held(with_other_core(hidden), rows_held[0], total, None, None)
    hidden, _ = finish(3, 4, [], [])
    hidden = with_other_core(hidden)
    out_rows = [(k * tok_dev, tok_dev) for k in range(n_gx)]
    if line:
        halves = [(row, part) for row in range(tok_dev, n_gx * tok_dev, part)]
        out_rows = out_rows[:1] + out_rows[3:] + halves
    spread = down_held(hidden, rows_held[1], total, pick_out, out_rows)

    if line:
        own, three, *halves = spread
        ends = [over_z(piece, 1, (0, 3)) for piece in halves[4:]]
        middle = over_z(three, 3, (1, 2))
        low, _ = relay(halves[2], ends[0], [], [])
        high, near = relay(halves[3], ends[1], halves[:2], [middle])
        far = jnp.concatenate([over_z(low, 2), over_z(high, 2)], axis=0)
        near = jnp.concatenate([over_z(piece, 1) for piece in near], axis=0)
        parts = [own, near, far, middle]
    else:
        parts = [spread[0]] + [over_z(spread[k], k) for k in range(1, n_gx)]
    return sum(p.astype(F32) for p in parts).astype(BF16)


def solution(mesh):
    placed = (P(("group", "gx"), "gy"), P("gy", "gx"), P("gy", "gx"), P("gx", "gy"), P("group"))
    return jax.shard_map(
        functools.partial(local, mesh.shape["gx"], mesh.shape["gy"]),
        mesh=mesh, in_specs=placed, out_specs=P(("group", "gx"), "gy"), check_vma=False,
    )
```

```python
import functools

import jax
import jax.numpy as jnp
from jax import lax
from jax.experimental import pallas as pl
from jax.experimental.pallas import tpu as pltpu
from jax.sharding import PartitionSpec as P

MIB = 1 << 20
BF16, F32 = jnp.bfloat16, jnp.float32


def row_sources(lengths_ref, rows, n_gx, tok_dev):
    start = jnp.int32(0)
    slot = rows
    for g in range(n_gx):
        slot = jnp.where(rows >= start, rows - start + g * tok_dev, slot)
        start = start + lengths_ref[g]
    return slot


def local_rows(shape, dim, quarter, nx):
    gy = lax.axis_index("gy")
    x, core = gy // 2, gy % 2
    j = lax.broadcasted_iota(jnp.int32, shape, dim)
    rows = jnp.zeros(shape, jnp.int32)
    for kc in range(2):
        for kx in range(nx):
            first = (kc * nx + kx) * quarter
            owner = lax.rem(x + kx, nx) * 2 + (1 - core if kc else core)
            rows = jnp.where(j >= first, owner * quarter + j - first, rows)
    return rows


def start_copies(chunks, gate_ref, up_ref, outs, sems):
    copies = []
    for i, (start, width) in enumerate(chunks):
        for k, src in enumerate((gate_ref, up_ref)):
            copies.append(pltpu.make_async_copy(src.at[:, pl.ds(start, width)], outs[2 * i + k], sems.at[2 * i + k]))
    for copy in copies:
        copy.start()
    return copies


def fetch_columns_kernel(n_after, chunk, gate_ref, up_ref, *refs):
    for copy in start_copies([chunk], gate_ref, up_ref, refs[n_after:-1], refs[-1]):
        copy.wait()


def fetch_columns(gate_weight, up_weight, chunk, after):
    held, anywhere = pl.BlockSpec(memory_space=pltpu.VMEM), pl.BlockSpec(memory_space=pl.ANY)
    return pl.pallas_call(
        functools.partial(fetch_columns_kernel, len(after), chunk),
        out_shape=[jax.ShapeDtypeStruct((gate_weight.shape[0], chunk[1]), BF16)] * 2,
        in_specs=[anywhere] * (2 + len(after)),
        out_specs=[held] * 2,
        scratch_shapes=[pltpu.SemaphoreType.DMA((2,))],
        cost_estimate=pl.CostEstimate(flops=0, bytes_accessed=0, transcendentals=0),
        compiler_params=pltpu.CompilerParams(vmem_limit_bytes=12 * MIB),
        name="fetch_columns",
    )(gate_weight, up_weight, *after)


def follow(handed, after):
    anywhere = pl.BlockSpec(memory_space=pl.ANY)
    return pl.pallas_call(
        lambda *refs: None,
        out_shape=jax.ShapeDtypeStruct(handed.shape, handed.dtype),
        in_specs=[anywhere] * (1 + len(after)),
        out_specs=anywhere,
        input_output_aliases={0: 0},
        compiler_params=pltpu.CompilerParams(vmem_limit_bytes=4 * MIB),
        cost_estimate=pl.CostEstimate(flops=0, bytes_accessed=0, transcendentals=0),
        name="follow",
    )(handed, *after)


def prepare_kernel(n_gx, nx, chunks, lengths_ref, tok_ref, gate_ref, up_ref, in_ref, out_ref, held_ref, *refs):
    copies = start_copies(chunks, gate_ref, up_ref, refs[:-1], refs[-1])
    held_ref[...] = tok_ref[...]
    tok_dev = tok_ref.shape[0]
    z = lax.axis_index("gx")
    live, slots = in_ref.shape
    quarter = live // (2 * nx)

    def slot_of(column):
        return (z ^ (column // tok_dev)) * tok_dev + column % tok_dev

    shape = (live, slots)
    source = row_sources(lengths_ref, local_rows(shape, 0, quarter, nx), n_gx, tok_dev)
    in_ref[...] = (source == slot_of(lax.broadcasted_iota(jnp.int32, shape, 1))).astype(F32).astype(BF16)
    shape = (slots, live)
    source = row_sources(lengths_ref, local_rows(shape, 1, quarter, nx), n_gx, tok_dev)
    out_ref[...] = (source == slot_of(lax.broadcasted_iota(jnp.int32, shape, 0))).astype(F32).astype(BF16)
    for copy in copies:
        copy.wait()


def prepare(lengths, tokens, gate_weight, up_weight, chunks, n_gx, nx, live):
    slots = n_gx * tokens.shape[0]
    held, anywhere = pl.BlockSpec(memory_space=pltpu.VMEM), pl.BlockSpec(memory_space=pl.ANY)
    weights = [jax.ShapeDtypeStruct((gate_weight.shape[0], width), BF16) for _, width in chunks for _ in range(2)]
    out = pl.pallas_call(
        functools.partial(prepare_kernel, n_gx, nx, chunks),
        out_shape=[
            jax.ShapeDtypeStruct((live, slots), BF16),
            jax.ShapeDtypeStruct((slots, live), BF16),
            jax.ShapeDtypeStruct(tokens.shape, tokens.dtype),
        ]
        + weights,
        in_specs=[pl.BlockSpec(memory_space=pltpu.SMEM), held, anywhere, anywhere],
        out_specs=[held] * (3 + len(weights)),
        scratch_shapes=[pltpu.SemaphoreType.DMA((len(weights),))],
        cost_estimate=pl.CostEstimate(flops=0, bytes_accessed=0, transcendentals=0),
        compiler_params=pltpu.CompilerParams(vmem_limit_bytes=4 * MIB),
        name="prepare",
    )(lengths, tokens, gate_weight, up_weight)
    return out[0], out[1], out[2], [out[3 + 2 * i:5 + 2 * i] for i in range(len(chunks))]


def compact_kernel(sizes, pick_ref, *refs):
    refs = list(refs)
    blocks = []
    for n in sizes:
        block = refs.pop(0)[...]
        for _ in range(n - 1):
            block = block + refs.pop(0)[...]
        blocks.append(block)
    rows = jnp.concatenate(blocks, axis=0)
    refs[-1][...] = jnp.dot(pick_ref[...], rows, preferred_element_type=F32).astype(BF16)


def compact(pick, blocks, after):
    held, anywhere = pl.BlockSpec(memory_space=pltpu.VMEM), pl.BlockSpec(memory_space=pl.ANY)
    flat = [b for block in blocks for b in block]
    return pl.pallas_call(
        functools.partial(compact_kernel, [len(block) for block in blocks]),
        out_shape=jax.ShapeDtypeStruct((pick.shape[0], flat[0].shape[1]), BF16),
        in_specs=[held] * (1 + len(flat)) + [anywhere] * len(after),
        out_specs=held,
        compiler_params=pltpu.CompilerParams(vmem_limit_bytes=5 * MIB),
        cost_estimate=pl.CostEstimate(flops=0, bytes_accessed=0, transcendentals=0),
        name="compact",
    )(pick, *flat, *after)


def send_shapes(half, nx, width, split):
    if split:
        return [jax.ShapeDtypeStruct((half // nx, width), BF16)] * (2 * nx)
    return [jax.ShapeDtypeStruct((2, half, width), BF16)]


def put_part(i, part, columns, keep_ref, send_refs):
    half = keep_ref.shape[1]
    keep_ref[i, :, columns] = part[:half]
    if len(send_refs) == 1:
        send_refs[0][i, :, columns] = part[half:].astype(BF16)
        return
    nx = len(send_refs) // 2
    quarter = half // nx
    for k in range(nx):
        first = half + k * quarter
        send_refs[i * nx + k][:, columns] = part[first:first + quarter].astype(BF16)


def gate_up_held_kernel(n_after, tile, tok_ref, gate_ref, up_ref, *refs):
    keep_ref, *send_refs = refs[n_after:]
    rows = tok_ref[...]
    for j in range(0, keep_ref.shape[2], tile):
        columns = slice(j, j + tile)
        for i, w_ref in enumerate((gate_ref, up_ref)):
            part = jnp.dot(rows, w_ref[:, columns], preferred_element_type=F32)
            put_part(i, part, columns, keep_ref, send_refs)


def gate_up_held(tok, gate_held, up_held, after, nx, tile):
    half, width = tok.shape[0] // 2, gate_held.shape[1]
    held, anywhere = pl.BlockSpec(memory_space=pltpu.VMEM), pl.BlockSpec(memory_space=pl.ANY)
    keep, *send = pl.pallas_call(
        functools.partial(gate_up_held_kernel, len(after), tile),
        out_shape=[jax.ShapeDtypeStruct((2, half, width), F32)] + send_shapes(half, nx, width, False),
        in_specs=[held] * 3 + [anywhere] * len(after),
        out_specs=[held] * 2,
        compiler_params=pltpu.CompilerParams(vmem_limit_bytes=6 * MIB),
        cost_estimate=pl.CostEstimate(flops=0, bytes_accessed=0, transcendentals=0),
        name="gate_up_held",
    )(tok, gate_held, up_held, *after)
    return send, keep


def gate_up_kernel(n_after, tok_ref, gate_ref, up_ref, *refs):
    keep_ref, *send_refs = refs[n_after:]
    rows = tok_ref[...]
    for i, w_ref in enumerate((gate_ref, up_ref)):
        part = jnp.dot(rows, w_ref[...], preferred_element_type=F32)
        put_part(i, part, slice(None), keep_ref, send_refs)


def gate_up(tok, gate_weight, up_weight, after, start, width, nx, tile):
    live, depth = tok.shape
    half = live // 2
    weight = pl.BlockSpec((depth, tile), lambda j: (0, start // tile + j))
    keep, *send = pl.pallas_call(
        functools.partial(gate_up_kernel, len(after)),
        out_shape=[jax.ShapeDtypeStruct((2, half, width), F32)] + send_shapes(half, nx, width, True),
        grid=(width // tile,),
        in_specs=[pl.BlockSpec((live, depth), lambda j: (0, 0)), weight, weight]
        + [pl.BlockSpec(memory_space=pl.ANY)] * len(after),
        out_specs=[pl.BlockSpec((2, half, tile), lambda j: (0, 0, j))]
        + [pl.BlockSpec((half // nx, tile), lambda j: (0, j))] * (2 * nx),
        compiler_params=pltpu.CompilerParams(vmem_limit_bytes=40 * MIB),
        cost_estimate=pl.CostEstimate(flops=0, bytes_accessed=0, transcendentals=0),
        name="gate_up",
    )(tok, gate_weight, up_weight, *after)
    return send, keep


def join_kernel(n_got, n_unread, nx, keep_ref, *refs):
    got_refs, out_refs = refs[:n_got], refs[n_got + n_unread:][:nx]
    quarter = out_refs[0].shape[1]
    for i in range(2):
        for k, out_ref in enumerate(out_refs):
            rows = pl.ds(k * quarter, quarter)
            got = got_refs[0][i, rows] if n_got == 1 else got_refs[i * nx + k][...]
            out_ref[i] = (keep_ref[i, rows] + got.astype(F32)).astype(out_ref.dtype)


def join(keep, got, handed, after, nx):
    two, half, width = keep.shape
    shape = (two, half // nx, width)
    held, anywhere = pl.BlockSpec(memory_space=pltpu.VMEM), pl.BlockSpec(memory_space=pl.ANY)
    out = pl.pallas_call(
        functools.partial(join_kernel, len(got), len(handed) + len(after), nx),
        out_shape=[jax.ShapeDtypeStruct(shape, BF16 if k else F32) for k in range(nx)]
        + [jax.ShapeDtypeStruct(a.shape, a.dtype) for a in handed],
        in_specs=[held] * (1 + len(got)) + [anywhere] * (len(handed) + len(after)),
        out_specs=[held] * nx + [anywhere] * len(handed),
        input_output_aliases={1 + len(got) + i: nx + i for i in range(len(handed))},
        compiler_params=pltpu.CompilerParams(vmem_limit_bytes=8 * MIB),
        cost_estimate=pl.CostEstimate(flops=0, bytes_accessed=0, transcendentals=0),
        name="join",
    )(keep, *got, *handed, *after)
    return out[0], list(out[1:nx]), list(out[nx:])


def activate_kernel(n_got, n_chunks, n_unread, *refs):
    own_ref = refs[n_chunks * (1 + n_got) + n_unread]
    column = 0
    for c in range(n_chunks):
        mine_ref, *got_refs = refs[c * (1 + n_got):(c + 1) * (1 + n_got)]
        both = mine_ref[...]
        for got_ref in got_refs:
            both = both + got_ref[...].astype(F32)
        gate, up = both[0], both[1]
        own_ref[:, column:column + gate.shape[1]] = (gate / (1.0 + jnp.exp(-gate)) * up).astype(BF16)
        column += gate.shape[1]


def activate(sums, handed, after):
    held, anywhere = pl.BlockSpec(memory_space=pltpu.VMEM), pl.BlockSpec(memory_space=pl.ANY)
    flat = [a for chunk in sums for a in chunk]
    width = sum(chunk[0].shape[2] for chunk in sums)
    out = pl.pallas_call(
        functools.partial(activate_kernel, len(sums[0]) - 1, len(sums), len(handed) + len(after)),
        out_shape=[jax.ShapeDtypeStruct((flat[0].shape[1], width), BF16)]
        + [jax.ShapeDtypeStruct(a.shape, a.dtype) for a in handed],
        in_specs=[held] * len(flat) + [anywhere] * (len(handed) + len(after)),
        out_specs=[held] + [anywhere] * len(handed),
        input_output_aliases={len(flat) + i: 1 + i for i in range(len(handed))},
        compiler_params=pltpu.CompilerParams(vmem_limit_bytes=8 * MIB),
        cost_estimate=pl.CostEstimate(flops=0, bytes_accessed=0, transcendentals=0),
        name="activate",
    )(*flat, *handed, *after)
    return out[0], out[1:]


def relay_kernel(n_unread, own_ref, got_ref, *refs):
    out_ref = refs[n_unread]
    out_ref[...] = (own_ref[...].astype(F32) + got_ref[...].astype(F32)).astype(BF16)


def relay(own, got, handed, after):
    held, anywhere = pl.BlockSpec(memory_space=pltpu.VMEM), pl.BlockSpec(memory_space=pl.ANY)
    out = pl.pallas_call(
        functools.partial(relay_kernel, len(handed) + len(after)),
        out_shape=[jax.ShapeDtypeStruct(a.shape, a.dtype) for a in (own, *handed)],
        in_specs=[held, held] + [anywhere] * (len(handed) + len(after)),
        out_specs=[held] + [anywhere] * len(handed),
        input_output_aliases={2 + i: 1 + i for i in range(len(handed))},
        compiler_params=pltpu.CompilerParams(vmem_limit_bytes=8 * MIB),
        cost_estimate=pl.CostEstimate(flops=0, bytes_accessed=0, transcendentals=0),
        name="relay",
    )(own, got, *handed, *after)
    return out[0], out[1:]


def put_rows(h_refs, hidden):
    row = 0
    for r in h_refs:
        hidden[row:row + r.shape[0]] = r[...]
        row += r.shape[0]


def down_kernel(n_h, *refs):
    h_refs, w_ref, out_ref, hidden = refs[:n_h], refs[n_h], refs[-2], refs[-1]

    @pl.when(pl.program_id(0) == 0)
    def _():
        put_rows(h_refs, hidden)

    out_ref[...] = jnp.dot(hidden[...], w_ref[...], preferred_element_type=F32)


def down(hidden, down_weight, after, start):
    live = sum(h.shape[0] for h in hidden)
    width = hidden[0].shape[1]
    out_width = down_weight.shape[1]
    tile = min(out_width, 512)
    weight = pl.BlockSpec((pl.Element(width), pl.Element(tile)), lambda j: (start, j * tile))
    return pl.pallas_call(
        functools.partial(down_kernel, len(hidden)),
        out_shape=jax.ShapeDtypeStruct((live, out_width), F32),
        grid=(out_width // tile,),
        in_specs=[pl.BlockSpec(h.shape, lambda j: (0, 0)) for h in hidden]
        + [weight]
        + [pl.BlockSpec(memory_space=pl.ANY)] * len(after),
        out_specs=pl.BlockSpec((live, tile), lambda j: (0, j)),
        scratch_shapes=[pltpu.VMEM((live, width), BF16)],
        compiler_params=pltpu.CompilerParams(vmem_limit_bytes=28 * MIB),
        cost_estimate=pl.CostEstimate(flops=0, bytes_accessed=0, transcendentals=0),
        name="down",
    )(*hidden, down_weight, *after)


def fetch_kernel(starts, src_ref, *refs):
    outs, sems = refs[-1 - len(starts):-1], refs[-1]
    copies = [
        pltpu.make_async_copy(src_ref.at[pl.ds(start, out.shape[0])], out, sems.at[i])
        for i, (start, out) in enumerate(zip(starts, outs))
    ]
    for copy in copies:
        copy.start()
    for copy in copies:
        copy.wait()


def fetch(down_weight, chunks, after):
    held, anywhere = pl.BlockSpec(memory_space=pltpu.VMEM), pl.BlockSpec(memory_space=pl.ANY)
    return pl.pallas_call(
        functools.partial(fetch_kernel, [start for start, _ in chunks]),
        out_shape=[jax.ShapeDtypeStruct((width, down_weight.shape[1]), BF16) for _, width in chunks],
        in_specs=[anywhere] * (1 + len(after)),
        out_specs=[held] * len(chunks),
        scratch_shapes=[pltpu.SemaphoreType.DMA((len(chunks),))],
        compiler_params=pltpu.CompilerParams(vmem_limit_bytes=28 * MIB),
        cost_estimate=pl.CostEstimate(flops=0, bytes_accessed=0, transcendentals=0),
        name="fetch",
    )(down_weight, *after)


def down_held_kernel(n_h, last, out_rows, tile, *refs):
    h_refs, w_ref, total_ref, outs, hidden = refs[:n_h], refs[n_h], refs[n_h + 1], refs[n_h + 2:-1], refs[-1]
    put_rows(h_refs, hidden)
    for j in range(0, total_ref.shape[1], tile):
        total = jnp.dot(hidden[...], w_ref[:, j:j + tile], preferred_element_type=F32) + total_ref[:, j:j + tile]
        if not last:
            outs[0][:, j:j + tile] = total
            continue
        pick_ref = outs[0]
        spread = jnp.dot(pick_ref[...], total.astype(BF16), preferred_element_type=F32).astype(BF16)
        for row, out_ref in zip(out_rows, outs[1:]):
            out_ref[:, j:j + tile] = spread[row:row + out_ref.shape[0]]


def down_held(hidden, weight_held, total, pick, out_rows):
    live, out_width = total.shape
    held = pl.BlockSpec(memory_space=pltpu.VMEM)
    last = pick is not None
    if last:
        out_shape = [jax.ShapeDtypeStruct((n, out_width), BF16) for _, n in out_rows]
    else:
        out_shape = jax.ShapeDtypeStruct((live, out_width), F32)
    return pl.pallas_call(
        functools.partial(down_held_kernel, len(hidden), last, [row for row, _ in out_rows or []], min(out_width, 512)),
        out_shape=out_shape,
        in_specs=[held] * (len(hidden) + (3 if last else 2)),
        out_specs=[held] * len(out_rows) if last else held,
        scratch_shapes=[pltpu.VMEM((live, hidden[0].shape[1]), BF16)],
        compiler_params=pltpu.CompilerParams(vmem_limit_bytes=12 * MIB),
        cost_estimate=pl.CostEstimate(flops=0, bytes_accessed=0, transcendentals=0),
        name="down_held",
    )(*hidden, weight_held, total, *([pick] if last else []))


def column_chunks(cols, tile):
    tiles = cols // tile
    shares = (3, 3, 4, 3)
    edges = [round(tiles * sum(shares[:i]) / sum(shares)) for i in range(len(shares) + 1)]
    return [(a * tile, (b - a) * tile) for a, b in zip(edges, edges[1:]) if b > a]


def local(n_gx, n_gy, tokens, gate_weight, up_weight, down_weight, lengths):
    nx = n_gy // 2
    tok_dev = tokens.shape[0]
    live = 3 * tok_dev * n_gx // 4
    cols = gate_weight.shape[1]
    tile = 512 if cols % 512 == 0 else 128
    chunks = column_chunks(cols, tile)
    line = n_gx == 4
    part = tok_dev // 2

    def over_z(block, k, among=range(n_gx)):
        return lax.ppermute(block, "gx", [(z, z ^ k) for z in among])

    def over_core(block):
        return lax.ppermute(block, "gy", [(i, i ^ 1) for i in range(n_gy)])

    def over_x(block, k):
        return lax.ppermute(block, "gy", [(i, (i + 2 * k) % n_gy) for i in range(n_gy)])

    pick_in, pick_out, held, weights = prepare(lengths, tokens, gate_weight, up_weight, chunks[:2], n_gx, nx, live)
    if line:
        two = over_z(tokens, 2)
        one = over_z(tokens, 1)
        middle = over_z(tokens, 3, (1, 2))
        two = follow(two, [pick_in])
        blocks = [[held], [one], [two], [middle, over_z(two, 1, (1, 2))]]
        ready = [two]
    else:
        blocks = [[held]] + [[over_z(tokens, k)] for k in range(1, n_gx)]
        ready = [pick_in]
    weights.append(fetch_columns(gate_weight, up_weight, chunks[2], ready))
    tok = compact(pick_in, blocks, weights[2][:1])

    made = [gate_up_held(tok, *weights[i], [], nx, tile) for i in range(2)]
    sends, keeps = [list(a) for a in zip(*made)]
    sums = []

    def exchange(j, handed, after):
        mine, blocks, handed = join(keeps[j], [over_core(a) for a in sends[j]], handed, after, nx)
        sums.append([mine] + [over_x(b, k + 1) for k, b in enumerate(blocks)])
        return blocks, handed

    def finish(first, last, handed, after):
        own, handed = activate(sums[first:last], handed, after)
        return [own] + [over_x(own, -k) for k in range(1, nx)], handed

    def with_other_core(h):
        return h + [over_core(a) for a in h]

    ready, sends[1] = exchange(0, sends[1], [])
    ready = ready + exchange(1, [], [])[0]
    made = [gate_up_held(tok, *weights[2], ready, nx, tile)]
    made.append(gate_up(tok, gate_weight, up_weight, made[0][0][:1], *chunks[3], nx, tile))
    pieces = len(made[0][0])
    hidden, handed = finish(0, 2, made[0][0] + made[1][0], [])
    sends += [handed[:pieces], handed[pieces:]]
    keeps += [keep for _, keep in made]
    rows_held = fetch(down_weight, chunks[2:], hidden[:1])
    _, sends[3] = exchange(2, sends[3], [rows_held[0]])
    ready, _ = exchange(3, [], [])
    total = down(with_other_core(hidden), down_weight, ready, chunks[0][0])
    hidden, _ = finish(2, 3, [], [total])
    total = down_held(with_other_core(hidden), rows_held[0], total, None, None)
    hidden, _ = finish(3, 4, [], [])
    hidden = with_other_core(hidden)
    out_rows = [(k * tok_dev, tok_dev) for k in range(n_gx)]
    if line:
        halves = [(row, part) for row in range(tok_dev, n_gx * tok_dev, part)]
        out_rows = out_rows[:1] + halves
    spread = down_held(hidden, rows_held[1], total, pick_out, out_rows)

    if line:
        own, *halves = spread
        ends = [over_z(piece, 1, (0, 3)) for piece in halves[4:]]
        middle = [over_z(piece, 3, (1, 2)) for piece in halves[4:]]
        low, _ = relay(halves[2], ends[0], [], [])
        high, near = relay(halves[3], ends[1], halves[:2], middle)
        far = jnp.concatenate([over_z(low, 2), over_z(high, 2)], axis=0)
        near = jnp.concatenate([over_z(piece, 1) for piece in near], axis=0)
        parts = [own, near, far, jnp.concatenate(middle, axis=0)]
    else:
        parts = [spread[0]] + [over_z(spread[k], k) for k in range(1, n_gx)]
    return sum(p.astype(F32) for p in parts).astype(BF16)


def solution(mesh):
    placed = (P(("group", "gx"), "gy"), P("gy", "gx"), P("gy", "gx"), P("gx", "gy"), P("group"))
    return jax.shard_map(
        functools.partial(local, mesh.shape["gx"], mesh.shape["gy"]),
        mesh=mesh, in_specs=placed, out_specs=P(("group", "gx"), "gy"), check_vma=False,
    )
```

```python
import functools

import jax
import jax.numpy as jnp
from jax import lax
from jax.experimental import pallas as pl
from jax.experimental.pallas import tpu as pltpu
from jax.sharding import PartitionSpec as P

MIB = 1 << 20
BF16, F32 = jnp.bfloat16, jnp.float32


def row_sources(lengths_ref, rows, n_gx, tok_dev):
    start = jnp.int32(0)
    slot = rows
    for g in range(n_gx):
        slot = jnp.where(rows >= start, rows - start + g * tok_dev, slot)
        start = start + lengths_ref[g]
    return slot


def local_rows(shape, dim, quarter, nx):
    gy = lax.axis_index("gy")
    x, core = gy // 2, gy % 2
    j = lax.broadcasted_iota(jnp.int32, shape, dim)
    rows = jnp.zeros(shape, jnp.int32)
    for kc in range(2):
        for kx in range(nx):
            first = (kc * nx + kx) * quarter
            owner = lax.rem(x + kx, nx) * 2 + (1 - core if kc else core)
            rows = jnp.where(j >= first, owner * quarter + j - first, rows)
    return rows


def start_copies(chunks, gate_ref, up_ref, outs, sems):
    copies = []
    for i, (start, width) in enumerate(chunks):
        for k, src in enumerate((gate_ref, up_ref)):
            copies.append(pltpu.make_async_copy(src.at[:, pl.ds(start, width)], outs[2 * i + k], sems.at[2 * i + k]))
    for copy in copies:
        copy.start()
    return copies


def fetch_columns_kernel(n_after, chunk, gate_ref, up_ref, *refs):
    for copy in start_copies([chunk], gate_ref, up_ref, refs[n_after:-1], refs[-1]):
        copy.wait()


def fetch_columns(gate_weight, up_weight, chunk, after):
    held, anywhere = pl.BlockSpec(memory_space=pltpu.VMEM), pl.BlockSpec(memory_space=pl.ANY)
    return pl.pallas_call(
        functools.partial(fetch_columns_kernel, len(after), chunk),
        out_shape=[jax.ShapeDtypeStruct((gate_weight.shape[0], chunk[1]), BF16)] * 2,
        in_specs=[anywhere] * (2 + len(after)),
        out_specs=[held] * 2,
        scratch_shapes=[pltpu.SemaphoreType.DMA((2,))],
        cost_estimate=pl.CostEstimate(flops=0, bytes_accessed=0, transcendentals=0),
        compiler_params=pltpu.CompilerParams(vmem_limit_bytes=12 * MIB),
        name="fetch_columns",
    )(gate_weight, up_weight, *after)


def follow(handed, after):
    anywhere = pl.BlockSpec(memory_space=pl.ANY)
    return pl.pallas_call(
        lambda *refs: None,
        out_shape=jax.ShapeDtypeStruct(handed.shape, handed.dtype),
        in_specs=[anywhere] * (1 + len(after)),
        out_specs=anywhere,
        input_output_aliases={0: 0},
        compiler_params=pltpu.CompilerParams(vmem_limit_bytes=4 * MIB),
        cost_estimate=pl.CostEstimate(flops=0, bytes_accessed=0, transcendentals=0),
        name="follow",
    )(handed, *after)


def prepare_kernel(n_gx, nx, chunks, lengths_ref, tok_ref, gate_ref, up_ref, in_ref, out_ref, held_ref, *refs):
    copies = start_copies(chunks, gate_ref, up_ref, refs[:-1], refs[-1])
    held_ref[...] = tok_ref[...]
    tok_dev = tok_ref.shape[0]
    z = lax.axis_index("gx")
    live, slots = in_ref.shape
    quarter = live // (2 * nx)

    def slot_of(column):
        return (z ^ (column // tok_dev)) * tok_dev + column % tok_dev

    shape = (live, slots)
    source = row_sources(lengths_ref, local_rows(shape, 0, quarter, nx), n_gx, tok_dev)
    in_ref[...] = (source == slot_of(lax.broadcasted_iota(jnp.int32, shape, 1))).astype(F32).astype(BF16)
    shape = (slots, live)
    source = row_sources(lengths_ref, local_rows(shape, 1, quarter, nx), n_gx, tok_dev)
    out_ref[...] = (source == slot_of(lax.broadcasted_iota(jnp.int32, shape, 0))).astype(F32).astype(BF16)
    for copy in copies:
        copy.wait()


def prepare(lengths, tokens, gate_weight, up_weight, chunks, n_gx, nx, live):
    slots = n_gx * tokens.shape[0]
    held, anywhere = pl.BlockSpec(memory_space=pltpu.VMEM), pl.BlockSpec(memory_space=pl.ANY)
    weights = [jax.ShapeDtypeStruct((gate_weight.shape[0], width), BF16) for _, width in chunks for _ in range(2)]
    out = pl.pallas_call(
        functools.partial(prepare_kernel, n_gx, nx, chunks),
        out_shape=[
            jax.ShapeDtypeStruct((live, slots), BF16),
            jax.ShapeDtypeStruct((slots, live), BF16),
            jax.ShapeDtypeStruct(tokens.shape, tokens.dtype),
        ]
        + weights,
        in_specs=[pl.BlockSpec(memory_space=pltpu.SMEM), held, anywhere, anywhere],
        out_specs=[held] * (3 + len(weights)),
        scratch_shapes=[pltpu.SemaphoreType.DMA((len(weights),))],
        cost_estimate=pl.CostEstimate(flops=0, bytes_accessed=0, transcendentals=0),
        compiler_params=pltpu.CompilerParams(vmem_limit_bytes=4 * MIB),
        name="prepare",
    )(lengths, tokens, gate_weight, up_weight)
    return out[0], out[1], out[2], [out[3 + 2 * i:5 + 2 * i] for i in range(len(chunks))]


def compact_kernel(sizes, pick_ref, *refs):
    refs = list(refs)
    blocks = []
    for n in sizes:
        block = refs.pop(0)[...]
        for _ in range(n - 1):
            block = block + refs.pop(0)[...]
        blocks.append(block)
    rows = jnp.concatenate(blocks, axis=0)
    refs[-1][...] = jnp.dot(pick_ref[...], rows, preferred_element_type=F32).astype(BF16)


def compact(pick, blocks, after):
    held, anywhere = pl.BlockSpec(memory_space=pltpu.VMEM), pl.BlockSpec(memory_space=pl.ANY)
    flat = [b for block in blocks for b in block]
    return pl.pallas_call(
        functools.partial(compact_kernel, [len(block) for block in blocks]),
        out_shape=jax.ShapeDtypeStruct((pick.shape[0], flat[0].shape[1]), BF16),
        in_specs=[held] * (1 + len(flat)) + [anywhere] * len(after),
        out_specs=held,
        compiler_params=pltpu.CompilerParams(vmem_limit_bytes=5 * MIB),
        cost_estimate=pl.CostEstimate(flops=0, bytes_accessed=0, transcendentals=0),
        name="compact",
    )(pick, *flat, *after)


def send_shapes(half, nx, width, split):
    if split:
        return [jax.ShapeDtypeStruct((half // nx, width), BF16)] * (2 * nx)
    return [jax.ShapeDtypeStruct((2, half, width), BF16)]


def put_part(i, part, columns, keep_ref, send_refs):
    half = keep_ref.shape[1]
    keep_ref[i, :, columns] = part[:half]
    if len(send_refs) == 1:
        send_refs[0][i, :, columns] = part[half:].astype(BF16)
        return
    nx = len(send_refs) // 2
    quarter = half // nx
    for k in range(nx):
        first = half + k * quarter
        send_refs[i * nx + k][:, columns] = part[first:first + quarter].astype(BF16)


def gate_up_held_kernel(n_after, tile, tok_ref, gate_ref, up_ref, *refs):
    keep_ref, *send_refs = refs[n_after:]
    rows = tok_ref[...]
    for j in range(0, keep_ref.shape[2], tile):
        columns = slice(j, j + tile)
        for i, w_ref in enumerate((gate_ref, up_ref)):
            part = jnp.dot(rows, w_ref[:, columns], preferred_element_type=F32)
            put_part(i, part, columns, keep_ref, send_refs)


def gate_up_held(tok, gate_held, up_held, after, nx, tile):
    half, width = tok.shape[0] // 2, gate_held.shape[1]
    held, anywhere = pl.BlockSpec(memory_space=pltpu.VMEM), pl.BlockSpec(memory_space=pl.ANY)
    keep, *send = pl.pallas_call(
        functools.partial(gate_up_held_kernel, len(after), tile),
        out_shape=[jax.ShapeDtypeStruct((2, half, width), F32)] + send_shapes(half, nx, width, False),
        in_specs=[held] * 3 + [anywhere] * len(after),
        out_specs=[held] * 2,
        compiler_params=pltpu.CompilerParams(vmem_limit_bytes=6 * MIB),
        cost_estimate=pl.CostEstimate(flops=0, bytes_accessed=0, transcendentals=0),
        name="gate_up_held",
    )(tok, gate_held, up_held, *after)
    return send, keep


def gate_up_kernel(n_after, tok_ref, gate_ref, up_ref, *refs):
    keep_ref, *send_refs = refs[n_after:]
    rows = tok_ref[...]
    for i, w_ref in enumerate((gate_ref, up_ref)):
        part = jnp.dot(rows, w_ref[...], preferred_element_type=F32)
        put_part(i, part, slice(None), keep_ref, send_refs)


def gate_up(tok, gate_weight, up_weight, after, start, width, nx, tile):
    live, depth = tok.shape
    half = live // 2
    weight = pl.BlockSpec((depth, tile), lambda j: (0, start // tile + j))
    keep, *send = pl.pallas_call(
        functools.partial(gate_up_kernel, len(after)),
        out_shape=[jax.ShapeDtypeStruct((2, half, width), F32)] + send_shapes(half, nx, width, True),
        grid=(width // tile,),
        in_specs=[pl.BlockSpec((live, depth), lambda j: (0, 0)), weight, weight]
        + [pl.BlockSpec(memory_space=pl.ANY)] * len(after),
        out_specs=[pl.BlockSpec((2, half, tile), lambda j: (0, 0, j))]
        + [pl.BlockSpec((half // nx, tile), lambda j: (0, j))] * (2 * nx),
        compiler_params=pltpu.CompilerParams(vmem_limit_bytes=40 * MIB),
        cost_estimate=pl.CostEstimate(flops=0, bytes_accessed=0, transcendentals=0),
        name="gate_up",
    )(tok, gate_weight, up_weight, *after)
    return send, keep


def join_kernel(n_got, n_unread, nx, keep_ref, *refs):
    got_refs, out_refs = refs[:n_got], refs[n_got + n_unread:][:nx]
    quarter = out_refs[0].shape[1]
    for i in range(2):
        for k, out_ref in enumerate(out_refs):
            rows = pl.ds(k * quarter, quarter)
            got = got_refs[0][i, rows] if n_got == 1 else got_refs[i * nx + k][...]
            out_ref[i] = (keep_ref[i, rows] + got.astype(F32)).astype(out_ref.dtype)


def join(keep, got, handed, after, nx):
    two, half, width = keep.shape
    shape = (two, half // nx, width)
    held, anywhere = pl.BlockSpec(memory_space=pltpu.VMEM), pl.BlockSpec(memory_space=pl.ANY)
    out = pl.pallas_call(
        functools.partial(join_kernel, len(got), len(handed) + len(after), nx),
        out_shape=[jax.ShapeDtypeStruct(shape, BF16 if k else F32) for k in range(nx)]
        + [jax.ShapeDtypeStruct(a.shape, a.dtype) for a in handed],
        in_specs=[held] * (1 + len(got)) + [anywhere] * (len(handed) + len(after)),
        out_specs=[held] * nx + [anywhere] * len(handed),
        input_output_aliases={1 + len(got) + i: nx + i for i in range(len(handed))},
        compiler_params=pltpu.CompilerParams(vmem_limit_bytes=8 * MIB),
        cost_estimate=pl.CostEstimate(flops=0, bytes_accessed=0, transcendentals=0),
        name="join",
    )(keep, *got, *handed, *after)
    return out[0], list(out[1:nx]), list(out[nx:])


def activate_kernel(n_got, n_chunks, n_unread, *refs):
    own_ref = refs[n_chunks * (1 + n_got) + n_unread]
    column = 0
    for c in range(n_chunks):
        mine_ref, *got_refs = refs[c * (1 + n_got):(c + 1) * (1 + n_got)]
        both = mine_ref[...]
        for got_ref in got_refs:
            both = both + got_ref[...].astype(F32)
        gate, up = both[0], both[1]
        own_ref[:, column:column + gate.shape[1]] = (gate / (1.0 + jnp.exp(-gate)) * up).astype(BF16)
        column += gate.shape[1]


def activate(sums, handed, after):
    held, anywhere = pl.BlockSpec(memory_space=pltpu.VMEM), pl.BlockSpec(memory_space=pl.ANY)
    flat = [a for chunk in sums for a in chunk]
    width = sum(chunk[0].shape[2] for chunk in sums)
    out = pl.pallas_call(
        functools.partial(activate_kernel, len(sums[0]) - 1, len(sums), len(handed) + len(after)),
        out_shape=[jax.ShapeDtypeStruct((flat[0].shape[1], width), BF16)]
        + [jax.ShapeDtypeStruct(a.shape, a.dtype) for a in handed],
        in_specs=[held] * len(flat) + [anywhere] * (len(handed) + len(after)),
        out_specs=[held] + [anywhere] * len(handed),
        input_output_aliases={len(flat) + i: 1 + i for i in range(len(handed))},
        compiler_params=pltpu.CompilerParams(vmem_limit_bytes=8 * MIB),
        cost_estimate=pl.CostEstimate(flops=0, bytes_accessed=0, transcendentals=0),
        name="activate",
    )(*flat, *handed, *after)
    return out[0], out[1:]


def relay_kernel(n_unread, own_ref, got_ref, *refs):
    out_ref = refs[n_unread]
    out_ref[...] = (own_ref[...].astype(F32) + got_ref[...].astype(F32)).astype(BF16)


def relay(own, got, handed, after):
    held, anywhere = pl.BlockSpec(memory_space=pltpu.VMEM), pl.BlockSpec(memory_space=pl.ANY)
    out = pl.pallas_call(
        functools.partial(relay_kernel, len(handed) + len(after)),
        out_shape=[jax.ShapeDtypeStruct(a.shape, a.dtype) for a in (own, *handed)],
        in_specs=[held, held] + [anywhere] * (len(handed) + len(after)),
        out_specs=[held] + [anywhere] * len(handed),
        input_output_aliases={2 + i: 1 + i for i in range(len(handed))},
        compiler_params=pltpu.CompilerParams(vmem_limit_bytes=8 * MIB),
        cost_estimate=pl.CostEstimate(flops=0, bytes_accessed=0, transcendentals=0),
        name="relay",
    )(own, got, *handed, *after)
    return out[0], out[1:]


def put_rows(h_refs, hidden):
    row = 0
    for r in h_refs:
        hidden[row:row + r.shape[0]] = r[...]
        row += r.shape[0]


def down_kernel(n_h, *refs):
    h_refs, w_ref, out_ref, hidden = refs[:n_h], refs[n_h], refs[-2], refs[-1]

    @pl.when(pl.program_id(0) == 0)
    def _():
        put_rows(h_refs, hidden)

    out_ref[...] = jnp.dot(hidden[...], w_ref[...], preferred_element_type=F32)


def down(hidden, down_weight, after, start):
    live = sum(h.shape[0] for h in hidden)
    width = hidden[0].shape[1]
    out_width = down_weight.shape[1]
    tile = min(out_width, 512)
    weight = pl.BlockSpec((pl.Element(width), pl.Element(tile)), lambda j: (start, j * tile))
    return pl.pallas_call(
        functools.partial(down_kernel, len(hidden)),
        out_shape=jax.ShapeDtypeStruct((live, out_width), F32),
        grid=(out_width // tile,),
        in_specs=[pl.BlockSpec(h.shape, lambda j: (0, 0)) for h in hidden]
        + [weight]
        + [pl.BlockSpec(memory_space=pl.ANY)] * len(after),
        out_specs=pl.BlockSpec((live, tile), lambda j: (0, j)),
        scratch_shapes=[pltpu.VMEM((live, width), BF16)],
        compiler_params=pltpu.CompilerParams(vmem_limit_bytes=28 * MIB),
        cost_estimate=pl.CostEstimate(flops=0, bytes_accessed=0, transcendentals=0),
        name="down",
    )(*hidden, down_weight, *after)


def fetch_kernel(starts, src_ref, *refs):
    outs, sems = refs[-1 - len(starts):-1], refs[-1]
    copies = [
        pltpu.make_async_copy(src_ref.at[pl.ds(start, out.shape[0])], out, sems.at[i])
        for i, (start, out) in enumerate(zip(starts, outs))
    ]
    for copy in copies:
        copy.start()
    for copy in copies:
        copy.wait()


def fetch(down_weight, chunks, after):
    held, anywhere = pl.BlockSpec(memory_space=pltpu.VMEM), pl.BlockSpec(memory_space=pl.ANY)
    return pl.pallas_call(
        functools.partial(fetch_kernel, [start for start, _ in chunks]),
        out_shape=[jax.ShapeDtypeStruct((width, down_weight.shape[1]), BF16) for _, width in chunks],
        in_specs=[anywhere] * (1 + len(after)),
        out_specs=[held] * len(chunks),
        scratch_shapes=[pltpu.SemaphoreType.DMA((len(chunks),))],
        compiler_params=pltpu.CompilerParams(vmem_limit_bytes=28 * MIB),
        cost_estimate=pl.CostEstimate(flops=0, bytes_accessed=0, transcendentals=0),
        name="fetch",
    )(down_weight, *after)


def down_held_kernel(n_h, last, out_rows, tile, *refs):
    h_refs, w_ref, total_ref, outs, hidden = refs[:n_h], refs[n_h], refs[n_h + 1], refs[n_h + 2:-1], refs[-1]
    put_rows(h_refs, hidden)
    for j in range(0, total_ref.shape[1], tile):
        total = jnp.dot(hidden[...], w_ref[:, j:j + tile], preferred_element_type=F32) + total_ref[:, j:j + tile]
        if not last:
            outs[0][:, j:j + tile] = total
            continue
        pick_ref = outs[0]
        spread = jnp.dot(pick_ref[...], total.astype(BF16), preferred_element_type=F32).astype(BF16)
        for row, out_ref in zip(out_rows, outs[1:]):
            out_ref[:, j:j + tile] = spread[row:row + out_ref.shape[0]]


def down_held(hidden, weight_held, total, pick, out_rows):
    live, out_width = total.shape
    held = pl.BlockSpec(memory_space=pltpu.VMEM)
    last = pick is not None
    if last:
        out_shape = [jax.ShapeDtypeStruct((n, out_width), BF16) for _, n in out_rows]
    else:
        out_shape = jax.ShapeDtypeStruct((live, out_width), F32)
    return pl.pallas_call(
        functools.partial(down_held_kernel, len(hidden), last, [row for row, _ in out_rows or []], min(out_width, 512)),
        out_shape=out_shape,
        in_specs=[held] * (len(hidden) + (3 if last else 2)),
        out_specs=[held] * len(out_rows) if last else held,
        scratch_shapes=[pltpu.VMEM((live, hidden[0].shape[1]), BF16)],
        compiler_params=pltpu.CompilerParams(vmem_limit_bytes=12 * MIB),
        cost_estimate=pl.CostEstimate(flops=0, bytes_accessed=0, transcendentals=0),
        name="down_held",
    )(*hidden, weight_held, total, *([pick] if last else []))


def column_chunks(cols, tile):
    tiles = cols // tile
    shares = (3, 3, 4, 3)
    edges = [round(tiles * sum(shares[:i]) / sum(shares)) for i in range(len(shares) + 1)]
    return [(a * tile, (b - a) * tile) for a, b in zip(edges, edges[1:]) if b > a]


def local(n_gx, n_gy, tokens, gate_weight, up_weight, down_weight, lengths):
    nx = n_gy // 2
    tok_dev = tokens.shape[0]
    live = 3 * tok_dev * n_gx // 4
    cols = gate_weight.shape[1]
    tile = 512 if cols % 512 == 0 else 128
    chunks = column_chunks(cols, tile)
    line = n_gx == 4
    part = tok_dev // 2

    def over_z(block, k, among=range(n_gx)):
        return lax.ppermute(block, "gx", [(z, z ^ k) for z in among])

    def over_core(block):
        return lax.ppermute(block, "gy", [(i, i ^ 1) for i in range(n_gy)])

    def over_x(block, k):
        return lax.ppermute(block, "gy", [(i, (i + 2 * k) % n_gy) for i in range(n_gy)])

    pick_in, pick_out, held, weights = prepare(lengths, tokens, gate_weight, up_weight, chunks[:2], n_gx, nx, live)
    if line:
        two = over_z(tokens, 2)
        one = over_z(tokens, 1)
        middle = over_z(tokens, 3, (1, 2))
        two = follow(two, [pick_in])
        blocks = [[held], [one], [two], [middle, over_z(two, 1, (1, 2))]]
        ready = [two]
    else:
        blocks = [[held]] + [[over_z(tokens, k)] for k in range(1, n_gx)]
        ready = [pick_in]
    weights.append(fetch_columns(gate_weight, up_weight, chunks[2], ready))
    tok = compact(pick_in, blocks, weights[2][:1])

    made = [gate_up_held(tok, *weights[i], [], nx, tile) for i in range(2)]
    sends, keeps = [list(a) for a in zip(*made)]
    sums = []

    def exchange(j, handed, after):
        mine, blocks, handed = join(keeps[j], [over_core(a) for a in sends[j]], handed, after, nx)
        sums.append([mine] + [over_x(b, k + 1) for k, b in enumerate(blocks)])
        return blocks, handed

    def finish(first, last, handed, after):
        own, handed = activate(sums[first:last], handed, after)
        return [own] + [over_x(own, -k) for k in range(1, nx)], handed

    def with_other_core(h):
        return h + [over_core(a) for a in h]

    ready, sends[1] = exchange(0, sends[1], [])
    ready = ready + exchange(1, [], [])[0]
    made = [gate_up_held(tok, *weights[2], ready, nx, tile)]
    made.append(gate_up(tok, gate_weight, up_weight, made[0][0][:1], *chunks[3], nx, tile))
    pieces = len(made[0][0])
    hidden, handed = finish(0, 2, made[0][0] + made[1][0], [])
    sends += [handed[:pieces], handed[pieces:]]
    keeps += [keep for _, keep in made]
    rows_held = fetch(down_weight, chunks[2:], hidden[:1])
    _, sends[3] = exchange(2, sends[3], [rows_held[0]])
    ready, _ = exchange(3, [], [])
    total = down(with_other_core(hidden), down_weight, ready, chunks[0][0])
    hidden, _ = finish(2, 3, [], [total])
    total = down_held(with_other_core(hidden), rows_held[0], total, None, None)
    hidden, _ = finish(3, 4, [], [])
    hidden = with_other_core(hidden)
    out_rows = [(k * tok_dev, tok_dev) for k in range(n_gx)]
    if line:
        halves = [(row, part) for row in range(tok_dev, n_gx * tok_dev, part)]
        out_rows = out_rows[:1] + halves
    spread = down_held(hidden, rows_held[1], total, pick_out, out_rows)

    if line:
        own, *halves = spread
        ends = [over_z(piece, 1, (0, 3)) for piece in halves[4:]]
        middle = [over_z(piece, 3, (1, 2)) for piece in halves[4:]]
        low, _ = relay(halves[2], ends[0], [], [])
        high, near = relay(halves[3], ends[1], halves[:2], [low])
        far = jnp.concatenate([over_z(low, 2), over_z(high, 2)], axis=0)
        near = jnp.concatenate([over_z(piece, 1) for piece in near], axis=0)
        parts = [own, far, near, jnp.concatenate(middle, axis=0)]
    else:
        parts = [spread[0]] + [over_z(spread[k], k) for k in range(1, n_gx)]
    return sum(p.astype(F32) for p in parts).astype(BF16)


def solution(mesh):
    placed = (P(("group", "gx"), "gy"), P("gy", "gx"), P("gy", "gx"), P("gx", "gy"), P("group"))
    return jax.shard_map(
        functools.partial(local, mesh.shape["gx"], mesh.shape["gy"]),
        mesh=mesh, in_specs=placed, out_specs=P(("group", "gx"), "gy"), check_vma=False,
    )
```

```python
import functools

import jax
import jax.numpy as jnp
from jax import lax
from jax.experimental import pallas as pl
from jax.experimental.pallas import tpu as pltpu
from jax.sharding import PartitionSpec as P

MIB = 1 << 20
BF16, F32 = jnp.bfloat16, jnp.float32


def row_sources(lengths_ref, rows, n_gx, tok_dev):
    start = jnp.int32(0)
    slot = rows
    for g in range(n_gx):
        slot = jnp.where(rows >= start, rows - start + g * tok_dev, slot)
        start = start + lengths_ref[g]
    return slot


def local_rows(shape, dim, quarter, nx):
    gy = lax.axis_index("gy")
    x, core = gy // 2, gy % 2
    j = lax.broadcasted_iota(jnp.int32, shape, dim)
    rows = jnp.zeros(shape, jnp.int32)
    for kc in range(2):
        for kx in range(nx):
            first = (kc * nx + kx) * quarter
            owner = lax.rem(x + kx, nx) * 2 + (1 - core if kc else core)
            rows = jnp.where(j >= first, owner * quarter + j - first, rows)
    return rows


def start_copies(chunks, gate_ref, up_ref, outs, sems):
    copies = []
    for i, (start, width) in enumerate(chunks):
        for k, src in enumerate((gate_ref, up_ref)):
            copies.append(pltpu.make_async_copy(src.at[:, pl.ds(start, width)], outs[2 * i + k], sems.at[2 * i + k]))
    for copy in copies:
        copy.start()
    return copies


def fetch_columns_kernel(n_after, chunk, gate_ref, up_ref, *refs):
    for copy in start_copies([chunk], gate_ref, up_ref, refs[n_after:-1], refs[-1]):
        copy.wait()


def fetch_columns(gate_weight, up_weight, chunk, after):
    held, anywhere = pl.BlockSpec(memory_space=pltpu.VMEM), pl.BlockSpec(memory_space=pl.ANY)
    return pl.pallas_call(
        functools.partial(fetch_columns_kernel, len(after), chunk),
        out_shape=[jax.ShapeDtypeStruct((gate_weight.shape[0], chunk[1]), BF16)] * 2,
        in_specs=[anywhere] * (2 + len(after)),
        out_specs=[held] * 2,
        scratch_shapes=[pltpu.SemaphoreType.DMA((2,))],
        cost_estimate=pl.CostEstimate(flops=0, bytes_accessed=0, transcendentals=0),
        compiler_params=pltpu.CompilerParams(vmem_limit_bytes=12 * MIB),
        name="fetch_columns",
    )(gate_weight, up_weight, *after)


def follow(handed, after):
    anywhere = pl.BlockSpec(memory_space=pl.ANY)
    return pl.pallas_call(
        lambda *refs: None,
        out_shape=jax.ShapeDtypeStruct(handed.shape, handed.dtype),
        in_specs=[anywhere] * (1 + len(after)),
        out_specs=anywhere,
        input_output_aliases={0: 0},
        compiler_params=pltpu.CompilerParams(vmem_limit_bytes=4 * MIB),
        cost_estimate=pl.CostEstimate(flops=0, bytes_accessed=0, transcendentals=0),
        name="follow",
    )(handed, *after)


def prepare_kernel(n_gx, nx, chunks, lengths_ref, tok_ref, gate_ref, up_ref, in_ref, out_ref, held_ref, *refs):
    copies = start_copies(chunks, gate_ref, up_ref, refs[:-1], refs[-1])
    held_ref[...] = tok_ref[...]
    tok_dev = tok_ref.shape[0]
    z = lax.axis_index("gx")
    live, slots = in_ref.shape
    quarter = live // (2 * nx)

    def slot_of(column):
        return (z ^ (column // tok_dev)) * tok_dev + column % tok_dev

    shape = (live, slots)
    source = row_sources(lengths_ref, local_rows(shape, 0, quarter, nx), n_gx, tok_dev)
    in_ref[...] = (source == slot_of(lax.broadcasted_iota(jnp.int32, shape, 1))).astype(F32).astype(BF16)
    shape = (slots, live)
    source = row_sources(lengths_ref, local_rows(shape, 1, quarter, nx), n_gx, tok_dev)
    out_ref[...] = (source == slot_of(lax.broadcasted_iota(jnp.int32, shape, 0))).astype(F32).astype(BF16)
    for copy in copies:
        copy.wait()


def prepare(lengths, tokens, gate_weight, up_weight, chunks, n_gx, nx, live):
    slots = n_gx * tokens.shape[0]
    held, anywhere = pl.BlockSpec(memory_space=pltpu.VMEM), pl.BlockSpec(memory_space=pl.ANY)
    weights = [jax.ShapeDtypeStruct((gate_weight.shape[0], width), BF16) for _, width in chunks for _ in range(2)]
    out = pl.pallas_call(
        functools.partial(prepare_kernel, n_gx, nx, chunks),
        out_shape=[
            jax.ShapeDtypeStruct((live, slots), BF16),
            jax.ShapeDtypeStruct((slots, live), BF16),
            jax.ShapeDtypeStruct(tokens.shape, tokens.dtype),
        ]
        + weights,
        in_specs=[pl.BlockSpec(memory_space=pltpu.SMEM), held, anywhere, anywhere],
        out_specs=[held] * (3 + len(weights)),
        scratch_shapes=[pltpu.SemaphoreType.DMA((len(weights),))],
        cost_estimate=pl.CostEstimate(flops=0, bytes_accessed=0, transcendentals=0),
        compiler_params=pltpu.CompilerParams(vmem_limit_bytes=4 * MIB),
        name="prepare",
    )(lengths, tokens, gate_weight, up_weight)
    return out[0], out[1], out[2], [out[3 + 2 * i:5 + 2 * i] for i in range(len(chunks))]


def compact_kernel(sizes, pick_ref, *refs):
    refs = list(refs)
    blocks = []
    for n in sizes:
        block = refs.pop(0)[...]
        for _ in range(n - 1):
            block = block + refs.pop(0)[...]
        blocks.append(block)
    rows = jnp.concatenate(blocks, axis=0)
    refs[-1][...] = jnp.dot(pick_ref[...], rows, preferred_element_type=F32).astype(BF16)


def compact(pick, blocks, after):
    held, anywhere = pl.BlockSpec(memory_space=pltpu.VMEM), pl.BlockSpec(memory_space=pl.ANY)
    flat = [b for block in blocks for b in block]
    return pl.pallas_call(
        functools.partial(compact_kernel, [len(block) for block in blocks]),
        out_shape=jax.ShapeDtypeStruct((pick.shape[0], flat[0].shape[1]), BF16),
        in_specs=[held] * (1 + len(flat)) + [anywhere] * len(after),
        out_specs=held,
        compiler_params=pltpu.CompilerParams(vmem_limit_bytes=5 * MIB),
        cost_estimate=pl.CostEstimate(flops=0, bytes_accessed=0, transcendentals=0),
        name="compact",
    )(pick, *flat, *after)


def send_shapes(half, nx, width, split):
    if split:
        return [jax.ShapeDtypeStruct((half // nx, width), BF16)] * (2 * nx)
    return [jax.ShapeDtypeStruct((2, half, width), BF16)]


def put_part(i, part, columns, keep_ref, send_refs):
    half = keep_ref.shape[1]
    keep_ref[i, :, columns] = part[:half]
    if len(send_refs) == 1:
        send_refs[0][i, :, columns] = part[half:].astype(BF16)
        return
    nx = len(send_refs) // 2
    quarter = half // nx
    for k in range(nx):
        first = half + k * quarter
        send_refs[i * nx + k][:, columns] = part[first:first + quarter].astype(BF16)


def gate_up_held_kernel(n_after, tile, tok_ref, gate_ref, up_ref, *refs):
    keep_ref, *send_refs = refs[n_after:]
    rows = tok_ref[...]
    for j in range(0, keep_ref.shape[2], tile):
        columns = slice(j, j + tile)
        for i, w_ref in enumerate((gate_ref, up_ref)):
            part = jnp.dot(rows, w_ref[:, columns], preferred_element_type=F32)
            put_part(i, part, columns, keep_ref, send_refs)


def gate_up_held(tok, gate_held, up_held, after, nx, tile):
    half, width = tok.shape[0] // 2, gate_held.shape[1]
    held, anywhere = pl.BlockSpec(memory_space=pltpu.VMEM), pl.BlockSpec(memory_space=pl.ANY)
    keep, *send = pl.pallas_call(
        functools.partial(gate_up_held_kernel, len(after), tile),
        out_shape=[jax.ShapeDtypeStruct((2, half, width), F32)] + send_shapes(half, nx, width, False),
        in_specs=[held] * 3 + [anywhere] * len(after),
        out_specs=[held] * 2,
        compiler_params=pltpu.CompilerParams(vmem_limit_bytes=6 * MIB),
        cost_estimate=pl.CostEstimate(flops=0, bytes_accessed=0, transcendentals=0),
        name="gate_up_held",
    )(tok, gate_held, up_held, *after)
    return send, keep


def gate_up_kernel(n_after, tok_ref, gate_ref, up_ref, *refs):
    keep_ref, *send_refs = refs[n_after:]
    rows = tok_ref[...]
    for i, w_ref in enumerate((gate_ref, up_ref)):
        part = jnp.dot(rows, w_ref[...], preferred_element_type=F32)
        put_part(i, part, slice(None), keep_ref, send_refs)


def gate_up(tok, gate_weight, up_weight, after, start, width, nx, tile):
    live, depth = tok.shape
    half = live // 2
    weight = pl.BlockSpec((depth, tile), lambda j: (0, start // tile + j))
    keep, *send = pl.pallas_call(
        functools.partial(gate_up_kernel, len(after)),
        out_shape=[jax.ShapeDtypeStruct((2, half, width), F32)] + send_shapes(half, nx, width, True),
        grid=(width // tile,),
        in_specs=[pl.BlockSpec((live, depth), lambda j: (0, 0)), weight, weight]
        + [pl.BlockSpec(memory_space=pl.ANY)] * len(after),
        out_specs=[pl.BlockSpec((2, half, tile), lambda j: (0, 0, j))]
        + [pl.BlockSpec((half // nx, tile), lambda j: (0, j))] * (2 * nx),
        compiler_params=pltpu.CompilerParams(vmem_limit_bytes=40 * MIB),
        cost_estimate=pl.CostEstimate(flops=0, bytes_accessed=0, transcendentals=0),
        name="gate_up",
    )(tok, gate_weight, up_weight, *after)
    return send, keep


def join_kernel(n_got, n_unread, nx, keep_ref, *refs):
    got_refs, out_refs = refs[:n_got], refs[n_got + n_unread:][:nx]
    quarter = out_refs[0].shape[1]
    for i in range(2):
        for k, out_ref in enumerate(out_refs):
            rows = pl.ds(k * quarter, quarter)
            got = got_refs[0][i, rows] if n_got == 1 else got_refs[i * nx + k][...]
            out_ref[i] = (keep_ref[i, rows] + got.astype(F32)).astype(out_ref.dtype)


def join(keep, got, handed, after, nx):
    two, half, width = keep.shape
    shape = (two, half // nx, width)
    held, anywhere = pl.BlockSpec(memory_space=pltpu.VMEM), pl.BlockSpec(memory_space=pl.ANY)
    out = pl.pallas_call(
        functools.partial(join_kernel, len(got), len(handed) + len(after), nx),
        out_shape=[jax.ShapeDtypeStruct(shape, BF16 if k else F32) for k in range(nx)]
        + [jax.ShapeDtypeStruct(a.shape, a.dtype) for a in handed],
        in_specs=[held] * (1 + len(got)) + [anywhere] * (len(handed) + len(after)),
        out_specs=[held] * nx + [anywhere] * len(handed),
        input_output_aliases={1 + len(got) + i: nx + i for i in range(len(handed))},
        compiler_params=pltpu.CompilerParams(vmem_limit_bytes=8 * MIB),
        cost_estimate=pl.CostEstimate(flops=0, bytes_accessed=0, transcendentals=0),
        name="join",
    )(keep, *got, *handed, *after)
    return out[0], list(out[1:nx]), list(out[nx:])


def activate_kernel(n_got, n_chunks, n_unread, *refs):
    own_ref = refs[n_chunks * (1 + n_got) + n_unread]
    column = 0
    for c in range(n_chunks):
        mine_ref, *got_refs = refs[c * (1 + n_got):(c + 1) * (1 + n_got)]
        both = mine_ref[...]
        for got_ref in got_refs:
            both = both + got_ref[...].astype(F32)
        gate, up = both[0], both[1]
        own_ref[:, column:column + gate.shape[1]] = (gate / (1.0 + jnp.exp(-gate)) * up).astype(BF16)
        column += gate.shape[1]


def activate(sums, handed, after):
    held, anywhere = pl.BlockSpec(memory_space=pltpu.VMEM), pl.BlockSpec(memory_space=pl.ANY)
    flat = [a for chunk in sums for a in chunk]
    width = sum(chunk[0].shape[2] for chunk in sums)
    out = pl.pallas_call(
        functools.partial(activate_kernel, len(sums[0]) - 1, len(sums), len(handed) + len(after)),
        out_shape=[jax.ShapeDtypeStruct((flat[0].shape[1], width), BF16)]
        + [jax.ShapeDtypeStruct(a.shape, a.dtype) for a in handed],
        in_specs=[held] * len(flat) + [anywhere] * (len(handed) + len(after)),
        out_specs=[held] + [anywhere] * len(handed),
        input_output_aliases={len(flat) + i: 1 + i for i in range(len(handed))},
        compiler_params=pltpu.CompilerParams(vmem_limit_bytes=8 * MIB),
        cost_estimate=pl.CostEstimate(flops=0, bytes_accessed=0, transcendentals=0),
        name="activate",
    )(*flat, *handed, *after)
    return out[0], out[1:]


def relay_kernel(n_unread, own_ref, got_ref, *refs):
    out_ref = refs[n_unread]
    out_ref[...] = (own_ref[...].astype(F32) + got_ref[...].astype(F32)).astype(BF16)


def relay(own, got, handed, after):
    held, anywhere = pl.BlockSpec(memory_space=pltpu.VMEM), pl.BlockSpec(memory_space=pl.ANY)
    out = pl.pallas_call(
        functools.partial(relay_kernel, len(handed) + len(after)),
        out_shape=[jax.ShapeDtypeStruct(a.shape, a.dtype) for a in (own, *handed)],
        in_specs=[held, held] + [anywhere] * (len(handed) + len(after)),
        out_specs=[held] + [anywhere] * len(handed),
        input_output_aliases={2 + i: 1 + i for i in range(len(handed))},
        compiler_params=pltpu.CompilerParams(vmem_limit_bytes=8 * MIB),
        cost_estimate=pl.CostEstimate(flops=0, bytes_accessed=0, transcendentals=0),
        name="relay",
    )(own, got, *handed, *after)
    return out[0], out[1:]


def put_rows(h_refs, hidden):
    row = 0
    for r in h_refs:
        hidden[row:row + r.shape[0]] = r[...]
        row += r.shape[0]


def down_kernel(n_h, *refs):
    h_refs, w_ref, out_ref, hidden = refs[:n_h], refs[n_h], refs[-2], refs[-1]

    @pl.when(pl.program_id(0) == 0)
    def _():
        put_rows(h_refs, hidden)

    out_ref[...] = jnp.dot(hidden[...], w_ref[...], preferred_element_type=F32)


def down(hidden, down_weight, after, start):
    live = sum(h.shape[0] for h in hidden)
    width = hidden[0].shape[1]
    out_width = down_weight.shape[1]
    tile = min(out_width, 512)
    weight = pl.BlockSpec((pl.Element(width), pl.Element(tile)), lambda j: (start, j * tile))
    return pl.pallas_call(
        functools.partial(down_kernel, len(hidden)),
        out_shape=jax.ShapeDtypeStruct((live, out_width), F32),
        grid=(out_width // tile,),
        in_specs=[pl.BlockSpec(h.shape, lambda j: (0, 0)) for h in hidden]
        + [weight]
        + [pl.BlockSpec(memory_space=pl.ANY)] * len(after),
        out_specs=pl.BlockSpec((live, tile), lambda j: (0, j)),
        scratch_shapes=[pltpu.VMEM((live, width), BF16)],
        compiler_params=pltpu.CompilerParams(vmem_limit_bytes=28 * MIB),
        cost_estimate=pl.CostEstimate(flops=0, bytes_accessed=0, transcendentals=0),
        name="down",
    )(*hidden, down_weight, *after)


def fetch_kernel(starts, src_ref, *refs):
    outs, sems = refs[-1 - len(starts):-1], refs[-1]
    copies = [
        pltpu.make_async_copy(src_ref.at[pl.ds(start, out.shape[0])], out, sems.at[i])
        for i, (start, out) in enumerate(zip(starts, outs))
    ]
    for copy in copies:
        copy.start()
    for copy in copies:
        copy.wait()


def fetch(down_weight, chunks, after):
    held, anywhere = pl.BlockSpec(memory_space=pltpu.VMEM), pl.BlockSpec(memory_space=pl.ANY)
    return pl.pallas_call(
        functools.partial(fetch_kernel, [start for start, _ in chunks]),
        out_shape=[jax.ShapeDtypeStruct((width, down_weight.shape[1]), BF16) for _, width in chunks],
        in_specs=[anywhere] * (1 + len(after)),
        out_specs=[held] * len(chunks),
        scratch_shapes=[pltpu.SemaphoreType.DMA((len(chunks),))],
        compiler_params=pltpu.CompilerParams(vmem_limit_bytes=28 * MIB),
        cost_estimate=pl.CostEstimate(flops=0, bytes_accessed=0, transcendentals=0),
        name="fetch",
    )(down_weight, *after)


def down_held_kernel(n_h, last, out_rows, tile, *refs):
    h_refs, w_ref, total_ref, outs, hidden = refs[:n_h], refs[n_h], refs[n_h + 1], refs[n_h + 2:-1], refs[-1]
    put_rows(h_refs, hidden)
    for j in range(0, total_ref.shape[1], tile):
        total = jnp.dot(hidden[...], w_ref[:, j:j + tile], preferred_element_type=F32) + total_ref[:, j:j + tile]
        if not last:
            outs[0][:, j:j + tile] = total
            continue
        pick_ref = outs[0]
        spread = jnp.dot(pick_ref[...], total.astype(BF16), preferred_element_type=F32).astype(BF16)
        for row, out_ref in zip(out_rows, outs[1:]):
            out_ref[:, j:j + tile] = spread[row:row + out_ref.shape[0]]


def down_held(hidden, weight_held, total, pick, out_rows):
    live, out_width = total.shape
    held = pl.BlockSpec(memory_space=pltpu.VMEM)
    last = pick is not None
    if last:
        out_shape = [jax.ShapeDtypeStruct((n, out_width), BF16) for _, n in out_rows]
    else:
        out_shape = jax.ShapeDtypeStruct((live, out_width), F32)
    return pl.pallas_call(
        functools.partial(down_held_kernel, len(hidden), last, [row for row, _ in out_rows or []], min(out_width, 512)),
        out_shape=out_shape,
        in_specs=[held] * (len(hidden) + (3 if last else 2)),
        out_specs=[held] * len(out_rows) if last else held,
        scratch_shapes=[pltpu.VMEM((live, hidden[0].shape[1]), BF16)],
        compiler_params=pltpu.CompilerParams(vmem_limit_bytes=12 * MIB),
        cost_estimate=pl.CostEstimate(flops=0, bytes_accessed=0, transcendentals=0),
        name="down_held",
    )(*hidden, weight_held, total, *([pick] if last else []))


def column_chunks(cols, tile):
    tiles = cols // tile
    shares = (3, 3, 4, 3)
    edges = [round(tiles * sum(shares[:i]) / sum(shares)) for i in range(len(shares) + 1)]
    return [(a * tile, (b - a) * tile) for a, b in zip(edges, edges[1:]) if b > a]


def local(n_gx, n_gy, tokens, gate_weight, up_weight, down_weight, lengths):
    nx = n_gy // 2
    tok_dev = tokens.shape[0]
    live = 3 * tok_dev * n_gx // 4
    cols = gate_weight.shape[1]
    tile = 512 if cols % 512 == 0 else 128
    chunks = column_chunks(cols, tile)
    line = n_gx == 4
    part = tok_dev // 2

    def over_z(block, k, among=range(n_gx)):
        return lax.ppermute(block, "gx", [(z, z ^ k) for z in among])

    def over_core(block):
        return lax.ppermute(block, "gy", [(i, i ^ 1) for i in range(n_gy)])

    def over_x(block, k):
        return lax.ppermute(block, "gy", [(i, (i + 2 * k) % n_gy) for i in range(n_gy)])

    pick_in, pick_out, held, weights = prepare(lengths, tokens, gate_weight, up_weight, chunks[:2], n_gx, nx, live)
    if line:
        two = over_z(tokens, 2)
        one = over_z(tokens, 1)
        middle = over_z(tokens, 3, (1, 2))
        two = follow(two, [pick_in])
        blocks = [[held], [one], [two], [middle, over_z(two, 1, (1, 2))]]
        ready = [two]
    else:
        blocks = [[held]] + [[over_z(tokens, k)] for k in range(1, n_gx)]
        ready = [pick_in]
    weights.append(fetch_columns(gate_weight, up_weight, chunks[2], ready))
    tok = compact(pick_in, blocks, weights[2][:1])

    made = [gate_up_held(tok, *weights[i], [], nx, tile) for i in range(2)]
    sends, keeps = [list(a) for a in zip(*made)]
    sums = []

    def exchange(j, handed, after):
        mine, blocks, handed = join(keeps[j], [over_core(a) for a in sends[j]], handed, after, nx)
        sums.append([mine] + [over_x(b, k + 1) for k, b in enumerate(blocks)])
        return blocks, handed

    def finish(first, last, handed, after):
        own, handed = activate(sums[first:last], handed, after)
        return [own] + [over_x(own, -k) for k in range(1, nx)], handed

    def with_other_core(h):
        return h + [over_core(a) for a in h]

    ready, sends[1] = exchange(0, sends[1], [])
    ready = ready + exchange(1, [], [])[0]
    made = [gate_up_held(tok, *weights[2], ready, nx, tile)]
    made.append(gate_up(tok, gate_weight, up_weight, made[0][0][:1], *chunks[3], nx, tile))
    pieces = len(made[0][0])
    hidden, handed = finish(0, 2, made[0][0] + made[1][0], [])
    sends += [handed[:pieces], handed[pieces:]]
    keeps += [keep for _, keep in made]
    rows_held = fetch(down_weight, chunks[2:], hidden[:1])
    _, sends[3] = exchange(2, sends[3], [rows_held[0]])
    ready, _ = exchange(3, [], [])
    total = down(with_other_core(hidden), down_weight, ready, chunks[0][0])
    hidden, _ = finish(2, 3, [], [total])
    total = down_held(with_other_core(hidden), rows_held[0], total, None, None)
    hidden, _ = finish(3, 4, [], [])
    hidden = with_other_core(hidden)
    out_rows = [(k * tok_dev, tok_dev) for k in range(n_gx)]
    if line:
        halves = [(row, part) for row in range(tok_dev, n_gx * tok_dev, part)]
        out_rows = out_rows[:1] + out_rows[3:] + halves
    spread = down_held(hidden, rows_held[1], total, pick_out, out_rows)

    if line:
        own, three, *halves = spread
        ends = [over_z(piece, 1, (0, 3)) for piece in halves[4:]]
        middle = over_z(three, 3, (1, 2))
        low, near = relay(halves[2], ends[0], halves[:2], [])
        high, _ = relay(halves[3], ends[1], [], [middle])
        far = jnp.concatenate([over_z(low, 2), over_z(high, 2)], axis=0)
        near = jnp.concatenate([over_z(piece, 1) for piece in near], axis=0)
        parts = [own, far, near, middle]
    else:
        parts = [spread[0]] + [over_z(spread[k], k) for k in range(1, n_gx)]
    return sum(p.astype(F32) for p in parts).astype(BF16)


def solution(mesh):
    placed = (P(("group", "gx"), "gy"), P("gy", "gx"), P("gy", "gx"), P("gx", "gy"), P("group"))
    return jax.shard_map(
        functools.partial(local, mesh.shape["gx"], mesh.shape["gy"]),
        mesh=mesh, in_specs=placed, out_specs=P(("group", "gx"), "gy"), check_vma=False,
    )
```
